128 devices in a mesh: gx: 16 (over x, y), gy: 8 (over z, core).
Axes of the slice: x: 4, y: 4, z: 4, core: 2. Of those that a mesh axis runs over, the one named last changes fastest.
Arguments:
- pressure_old: float32 [64, 256, 2048], P(None, 'gx', 'gy'), may hold values from -2.5 to 0.5
- conductivity: float32 [64, 256, 2048], P(None, 'gx', 'gy'), may hold values from 0.2 to 12
- forcing: float32 [8, 256, 2048], P(None, 'gx', 'gy'), may hold values from -5 to 5
- vegetated: int32 [256, 2048], P('gx', 'gy'), may hold values from 0 to 1, as said below
- cover_type: int32 [256, 2048], P('gx', 'gy'), may hold values from 0 to 15
- canopy_table: float32 [16, 8], replicated, may hold values from -2 to 2
- root_table: float32 [16, 8], replicated, may hold values from 0.2 to 2
- pair_counts: int32 [16, 16, 8], P('gx', None, 'gy'), may hold values from 0 to 256, as said below
- send_cols: int32 [16, 16, 8, 256], P('gx', None, 'gy'), may hold values from 0 to 4095, as said below
- canopy_state: float32 [16, 16, 8, 16, 256], P('gx', None, 'gy'), may hold values from -6 to 6
Outputs:
- pressure: float32 [64, 256, 2048], P(None, 'gx', 'gy')
- new_state: float32 [16, 16, 8, 16, 256], P('gx', None, 'gy')
The draws below stay inside these ranges and needn't reach their ends.
Inputs may be any that keep to these rules, and one draw needn't show every extreme that they name: `pair_counts`: in each column j of tiles one owner o receives exactly 256 columns from every tile (i, j). `send_cols`: for tile (i, j) and owner o the first pair_counts[i, o, j] entries are distinct local column numbers; over all o they are exactly the tile's vegetated columns, each once. The remaining entries are arbitrary local column numbers. `vegetated`: 1 exactly at the columns named by live entries of send_cols.
All inputs are finite; a program needn't handle non-finite values.
Results may differ from the reference program's by a relative error of at most 0.00022.
Values sent between devices are 32-bit elements; how exact they have to be, the bound alone decides.
No kernel may reach another device: no remote copies, remote signals or barrier semaphores. Data moves between devices by JAX's collectives and lax.ppermute only.
A program may use at most 128 MiB of HBM per device.

```python
import math
import jax
import jax.numpy as jnp

CX = 16
CY = 256
NZ = 64
FORC = 8
NPFT = 16
ROOT = 8
STATE = 16
CAP = 256
NEWTON = 2
ITERS = 3
NX = 256
NY = 2048
N_GX = 16
N_GY = 8


def column_lists(key):
    tiles_x = NX // CX
    tiles_y = NY // CY
    columns = CX * CY
    key_counts, key_full, key_perm = jax.random.split(key, 3)
    counts = jax.random.randint(key_counts, (tiles_x, tiles_x, tiles_y), 0, CAP + 1)
    full_owner = jax.random.randint(key_full, (tiles_y,), 0, tiles_x)
    counts = jnp.where(jnp.arange(tiles_x)[None, :, None] == full_owner[None, None, :], CAP, counts)
    perm_keys = jax.random.split(key_perm, tiles_x * tiles_y)
    orders = jax.vmap(lambda single: jax.random.permutation(single, columns))(perm_keys)
    return (counts.astype(jnp.int32), orders.reshape(tiles_x, tiles_y, columns).astype(jnp.int32))


def draw_pair_counts(key, part):
    counts, orders = column_lists(key)
    return counts


def draw_send_cols(key, part):
    counts, orders = column_lists(key)
    key = jax.random.fold_in(key, 12)
    tiles_x = NX // CX
    tiles_y = NY // CY
    columns = CX * CY
    offsets = jnp.cumsum(counts, axis=1) - counts
    position = offsets[..., None] + jnp.arange(CAP)[None, None, None, :]
    valid = jnp.arange(CAP)[None, None, None, :] < counts[..., None]
    first_index = jnp.arange(tiles_x)[:, None, None, None]
    third_index = jnp.arange(tiles_y)[None, None, :, None]
    chosen = orders[first_index, third_index, jnp.clip(position, 0, columns - 1)]
    filler = jax.random.randint(key, chosen.shape, 0, columns)
    return jnp.where(valid, chosen, filler).astype(jnp.int32)


def draw_vegetated(key, part):
    counts, orders = column_lists(key)
    tiles_x = NX // CX
    tiles_y = NY // CY
    totals = jnp.sum(counts, axis=1)
    ranks = jnp.argsort(orders, axis=-1, stable=True)
    marked = (ranks < totals[..., None]).astype(jnp.int32)
    return marked.reshape(tiles_x, tiles_y, CX, CY).transpose(0, 2, 1, 3).reshape(NX, NY)


def draw_conductivity(key, part):
    key = jax.random.fold_in(key, 14)
    across = jnp.arange(NX).astype(jnp.float32) / NX
    trend = jnp.exp(math.log(3.0) * across)[None, :, None]
    rough = jnp.exp(jax.random.uniform(key, (NZ, NX, NY), jnp.float32, math.log(0.3), math.log(3.0)))
    return rough * trend


def place_ends(entries, key, low, top_value):
    shape = entries.shape
    spot = [jax.random.randint(jax.random.fold_in(key, axis), (), 0, shape[axis]) for axis in range(len(shape))]
    entries = entries.at[tuple(spot)].set(low)
    longest = shape.index(max(shape))
    spot[longest] = (spot[longest] + 1) % shape[longest]
    return entries.at[tuple(spot)].set(top_value)


def levels(own_key, extent, pieces, low, top_value):
    def one(dim, shards_of):
        steps = jax.random.uniform(jax.random.fold_in(jax.random.fold_in(own_key, 6), dim), (shards_of,), jnp.float32, low / len(pieces), top_value / len(pieces))
        return jnp.repeat(jnp.exp(steps), extent[dim] // shards_of).reshape((-1,) + (1,) * (len(extent) - dim - 1))

    factor_of = one(*pieces[0])
    for cut in pieces[1:]:
        factor_of = factor_of * one(*cut)
    return factor_of


def centred(stream_key, extent, width, limit, cuts=(), kind=jnp.bfloat16):
    values = width * jax.random.normal(stream_key, extent, jnp.float32)
    if cuts:
        values = values * levels(stream_key, extent, cuts, -0.22, 0.18)
    return jnp.clip(values, -limit, limit).astype(kind)


def setup_inputs(seed: int = 0) -> dict:
    splits = jax.random.split(jax.random.key(seed), 11)
    return {
        "pressure_old": jnp.clip(-2.5 + 3.0 * jax.random.uniform(splits[0], (NZ, NX, NY), jnp.float32) ** levels(splits[0], (NZ, NX, NY), ((1, 16), (2, 8)), -0.2, 0.2), -2.5, 0.5),
        "conductivity": draw_conductivity(jax.random.fold_in(splits[10], 71), 0),
        "forcing": centred(splits[2], (FORC, NX, NY), 1.0, 5.0, ((1, 16), (2, 8)), jnp.float32),
        "vegetated": draw_vegetated(jax.random.fold_in(splits[10], 71), 0),
        "cover_type": place_ends(jax.random.randint(splits[4], (NX, NY), 0, NPFT), jax.random.fold_in(splits[4], 1), 0, NPFT - 1).astype(jnp.int32),
        "canopy_table": centred(splits[5], (NPFT, FORC), FORC ** -0.5, 2.0, (), jnp.float32),
        "root_table": jnp.clip(jnp.exp(jax.random.uniform(splits[6], (NPFT, ROOT), jnp.float32, math.log(0.2), math.log(2.0))), 0.2, 2.0),
        "pair_counts": draw_pair_counts(jax.random.fold_in(splits[10], 71), 0),
        "send_cols": draw_send_cols(jax.random.fold_in(splits[10], 71), 0),
        "canopy_state": centred(splits[9], (N_GX, N_GX, N_GY, STATE, CAP), 1.0, 6.0, ((0, 16), (2, 8)), jnp.float32),
    }


specific_storage = 0.05
gravity_step = 0.5


def canopy_physics(payload, state_in):
    forcing_part = payload[0:FORC]
    weights_part = payload[FORC:2 * FORC]
    root_part = payload[2 * FORC:2 * FORC + ROOT]
    soil_head = payload[2 * FORC + ROOT:2 * FORC + 2 * ROOT]
    conductance = 2.0 * jax.nn.sigmoid(jnp.sum(weights_part * forcing_part, axis=0))
    start_temp = state_in[1]
    leaf_temp = start_temp
    for repeat in range(3):
        leaf_temp = 0.5 * (start_temp + forcing_part[0]) + 0.5 * jnp.tanh(forcing_part[1] - conductance * (leaf_temp - forcing_part[2]))
    demand = conductance * jax.nn.softplus(leaf_temp - forcing_part[3]) / (1.0 + state_in[0] * state_in[0])
    uptake = demand[None] * root_part * jax.nn.sigmoid(2.0 * (soil_head + 1.5))
    canopy_water = 0.8 * state_in[0] + 0.2 * jnp.tanh(forcing_part[4])
    soil_temp = state_in[2:]
    temp_above = jnp.concatenate([leaf_temp[None], soil_temp[:-1]], axis=0)
    temp_below = jnp.concatenate([soil_temp[1:], soil_temp[-1:]], axis=0)
    soil_next = 0.6 * soil_temp + 0.2 * temp_above + 0.2 * temp_below
    return uptake, jnp.concatenate([canopy_water[None], leaf_temp[None], soil_next], axis=0)


def neighbours(field):
    padded = jnp.pad(field, 1)
    return [padded[:-2, 1:-1, 1:-1], padded[2:, 1:-1, 1:-1],
            padded[1:-1, :-2, 1:-1], padded[1:-1, 2:, 1:-1],
            padded[1:-1, 1:-1, :-2], padded[1:-1, 1:-1, 2:]]


def reference(pressure_old, conductivity, forcing, vegetated, cover_type, canopy_table, root_table, pair_counts, send_cols, canopy_state):
    tiles_x = N_GX
    tiles_y = N_GY
    columns = CX * CY

    def blocks(field):
        depth_count = field.shape[0]
        shaped = field.reshape(depth_count, tiles_x, CX, tiles_y, CY).transpose(1, 3, 0, 2, 4)
        return shaped.reshape(tiles_x, tiles_y, depth_count, columns)

    param_table = jnp.concatenate([canopy_table, root_table], axis=1)
    params = jnp.moveaxis(param_table[cover_type], -1, 0)
    local_data = jnp.concatenate([forcing, params, pressure_old[:ROOT]], axis=0)
    local_blocks = blocks(local_data)
    index_list = send_cols.transpose(0, 2, 1, 3).reshape(tiles_x, tiles_y, tiles_x * CAP)
    picked = jnp.take_along_axis(local_blocks, index_list[:, :, None, :], axis=3)
    picked = picked.reshape(tiles_x, tiles_y, local_data.shape[0], tiles_x, CAP)
    slot_live = (jnp.arange(CAP)[None, None, None, :] < pair_counts[..., None]).transpose(0, 2, 1, 3)
    state_src = canopy_state.transpose(3, 1, 2, 0, 4)
    uptake, updated = canopy_physics(jnp.moveaxis(picked, 2, 0), state_src)
    kept_state = jnp.where(slot_live[None], updated, state_src)
    new_state = kept_state.transpose(3, 1, 2, 0, 4)
    values = jnp.where(slot_live[None], uptake, jnp.float32(0.0))
    values = values.transpose(1, 2, 0, 3, 4).reshape(tiles_x, tiles_y, ROOT, tiles_x * CAP)

    def place(index_row, value_rows):
        return jnp.zeros((ROOT, columns), jnp.float32).at[:, index_row].add(value_rows)

    root_sink = jax.vmap(jax.vmap(place))(index_list, values)
    root_sink = root_sink.reshape(tiles_x, tiles_y, ROOT, CX, CY).transpose(2, 0, 3, 1, 4).reshape(ROOT, NX, NY)

    veg_float = vegetated.astype(jnp.float32)
    evaporation = (1.0 - veg_float) * 0.5 * jax.nn.softplus(forcing[3] - forcing[2]) * jax.nn.sigmoid(2.0 * (pressure_old[0] + 1.5))
    rainfall = 0.3 * jax.nn.softplus(forcing[4])
    source_field = jnp.concatenate([-root_sink, jnp.zeros((NZ - ROOT, NX, NY), jnp.float32)], axis=0)
    source_field = source_field.at[0].add(rainfall - evaporation)

    layer_depth = jnp.arange(NZ).astype(jnp.float32)[:, None, None]
    stored_old = 0.3 + 0.7 * jax.nn.sigmoid(2.0 * pressure_old) + specific_storage * pressure_old
    head = pressure_old
    for newton_index in range(NEWTON):
        squash = jax.nn.sigmoid(2.0 * head)
        mobility = conductivity * (0.1 + 0.9 * squash)
        potential = head - gravity_step * layer_depth
        mob_near = neighbours(mobility)
        pot_near = neighbours(potential)
        coupling = [2.0 * mobility * other / (mobility + other) for other in mob_near]
        outflow = jnp.zeros_like(head)
        for weight, other in zip(coupling, pot_near):
            outflow = outflow + weight * (potential - other)
        stored = 0.3 + 0.7 * squash + specific_storage * head
        imbalance = (stored - stored_old) + outflow - source_field
        capacity = 1.4 * squash * (1.0 - squash) + specific_storage

        def apply_jacobian(field):
            result = capacity * field
            for weight, other in zip(coupling, neighbours(field)):
                result = result + weight * (field - other)
            return result

        right_side = -imbalance
        update = jnp.zeros_like(head)
        residual = right_side
        direction = right_side
        norm_now = jnp.sum(residual * residual)
        for sweep_index in range(ITERS):
            image = apply_jacobian(direction)
            step_size = norm_now / jnp.sum(direction * image)
            update = update + step_size * direction
            residual = residual - step_size * image
            norm_after = jnp.sum(residual * residual)
            direction = residual + (norm_after / norm_now) * direction
            norm_now = norm_after
        head = head + update
    return head, new_state
```

```python
import jax
import jax.numpy as jnp
from jax import lax
from jax.experimental import pallas as pl
from jax.experimental.pallas import tpu as pltpu
from jax.sharding import PartitionSpec as P

FORC = 8
ROOT = 8
LEV = 64
ROWS = 16
COLS = 256
XR = 24
XC = 384
STORE = 0.05
GRAV = 0.5
F32 = jnp.float32
BF16 = jnp.bfloat16
VMEM_LIMIT = 56 * 1024 * 1024


def vmem(n=1):
    return [pl.BlockSpec(memory_space=pltpu.VMEM)] * n


def params():
    return pltpu.CompilerParams(vmem_limit_bytes=VMEM_LIMIT)


def shaped(*shape):
    return jax.ShapeDtypeStruct(shape, F32)


def iota(shape, dim):
    return lax.broadcasted_iota(jnp.int32, shape, dim)


def right(v):
    return pltpu.roll(v, v.shape[1] - 1, 1)


def left(v):
    return pltpu.roll(v, 1, 1)


def below(v):
    return pltpu.roll(v, v.shape[0] - 1, 0)


def above(v):
    return pltpu.roll(v, 1, 0)


def lanes(v, shift):
    return v if shift % 128 == 0 else pltpu.roll(v, shift % 128, v.ndim - 1)


def pieces(v):
    high = v.astype(BF16)
    rest = v - high.astype(F32)
    mid = rest.astype(BF16)
    low = (rest - mid.astype(F32)).astype(BF16)
    return high, mid, low


def canopy_send_kernel(
    forcing, cover, canopy_table, counts, cols, state, payload, split, gathered
):
    weights = [jnp.zeros((ROWS, COLS), F32) for _ in range(FORC)]
    kinds = cover[...]
    for kind in range(canopy_table.shape[0]):
        hit = kinds == kind
        for m in range(FORC):
            weights[m] = jnp.where(hit, canopy_table[kind, m], weights[m])
    total = weights[0] * forcing[0]
    for m in range(1, FORC):
        total = total + weights[m] * forcing[m]
    conductance = 2.0 * jax.nn.sigmoid(total)
    channels = [forcing[0], forcing[1], forcing[2], jnp.tanh(forcing[4]), conductance]
    used = len(channels)
    for c, channel in enumerate(channels):
        for p, piece in enumerate(pieces(channel)):
            split[pl.ds((p * used + c) * ROWS, ROWS), :] = piece

    def owner(o, carry):
        index = cols[pl.ds(o, 1), :]
        row_hit = iota((ROWS, COLS), 0) == (index // COLS)
        col_hit = iota((COLS, COLS), 0) == (index % COLS)
        onehot = jnp.where(col_hit, 1.0, 0.0).astype(BF16)
        picked = jnp.dot(split[...], onehot, preferred_element_type=F32)
        span = used * ROWS
        picked = picked[:span] + picked[span : 2 * span] + picked[2 * span :]
        sub = iota((8, COLS), 0)
        out = pltpu.roll(state[o, 0:8, :], 6, 0)
        for c in range(used):
            chosen = jnp.where(row_hit, picked[c * ROWS : (c + 1) * ROWS], 0.0)
            chosen = jnp.sum(chosen, axis=0, keepdims=True)
            out = jnp.where(sub == c, chosen, out)
        live = jnp.where(iota((8, COLS), 1) < counts[o], 1.0, 0.0)
        payload[o] = jnp.where(sub == used, live, out)
        return carry

    lax.fori_loop(0, cols.shape[0], owner, 0)


def canopy_send(forcing, cover, canopy_table, counts, cols, state):
    owners = cols.shape[0]
    return pl.pallas_call(
        canopy_send_kernel,
        out_shape=shaped(owners, 8, COLS),
        in_specs=vmem(2)
        + [pl.BlockSpec(memory_space=pltpu.SMEM)] * 2
        + vmem(2),
        out_specs=vmem()[0],
        scratch_shapes=[
            pltpu.VMEM((15 * ROWS, COLS), BF16),
            pltpu.VMEM((8, COLS), F32),
        ],
        compiler_params=params(),
        name="canopy_send",
    )(forcing, cover, canopy_table, counts, cols, state)


def softplus(v):
    return jnp.maximum(v, 0.0) + jnp.log1p(jnp.exp(-jnp.abs(v)))


def leaf(start, f0, f1, f2, g):
    temp = start
    for _ in range(3):
        temp = 0.5 * (start + f0) + 0.5 * jnp.tanh(f1 - g * (temp - f2))
    return temp


def source_kernel(
    arrived, cols, counts, forcing, cover, vegetated, canopy_table, root_table, pressure, source, edge, total
):
    total[...] = jnp.zeros_like(total)

    def owner(o, carry):
        index = cols[pl.ds(o, 1), :]
        row_hit = iota((ROWS, COLS), 0) == (index // COLS)
        col_hit = iota((COLS, COLS), 0) == (index % COLS)
        onehot = jnp.where(col_hit, 1.0, 0.0).astype(BF16)
        wanted = jnp.logical_and(row_hit, iota((ROWS, COLS), 1) < counts[o])
        block = arrived[o]
        parts = []
        for c in (6, 7):
            value = jnp.where(wanted, block[c : c + 1, :], 0.0)
            parts.extend(pieces(value))
        stacked = jnp.concatenate(parts, axis=0)
        placed = lax.dot_general(
            stacked, onehot, (((1,), (1,)), ((), ())), preferred_element_type=F32
        )
        total[...] += placed
        return carry

    lax.fori_loop(0, cols.shape[0], owner, 0)

    def piece(k):
        return total[k * ROWS : (k + 1) * ROWS, :]

    water = piece(0) + piece(1) + piece(2)
    start = piece(3) + piece(4) + piece(5)
    kinds = cover[...]
    weights = [jnp.zeros((ROWS, COLS), F32) for _ in range(FORC)]
    roots = [jnp.zeros((ROWS, COLS), F32) for _ in range(ROOT)]
    for kind in range(canopy_table.shape[0]):
        hit = kinds == kind
        for m in range(FORC):
            weights[m] = jnp.where(hit, canopy_table[kind, m], weights[m])
        for m in range(ROOT):
            roots[m] = jnp.where(hit, root_table[kind, m], roots[m])
    mixed = weights[0] * forcing[0]
    for m in range(1, FORC):
        mixed = mixed + weights[m] * forcing[m]
    conductance = 2.0 * jax.nn.sigmoid(mixed)
    temp = leaf(start, forcing[0], forcing[1], forcing[2], conductance)
    demand = conductance * softplus(temp - forcing[3]) / (1.0 + water * water)
    planted = vegetated[...] == 1
    demand = jnp.where(planted, demand, 0.0)
    dry = jnp.where(planted, 0.0, 0.5)
    lane = iota((ROWS, 128), 1)
    packed = jnp.zeros((ROWS, 128), F32)
    for m in range(ROOT):
        moist = jax.nn.sigmoid(2.0 * (pressure[m] + 1.5))
        value = -(demand * roots[m] * moist)
        if m == 0:
            evaporation = dry * softplus(forcing[3] - forcing[2]) * moist
            value = value + (0.3 * softplus(forcing[4]) - evaporation)
        source[m] = value
        first = jnp.logical_and(lane >= 8 * m, lane < 8 * m + 8)
        last = jnp.logical_and(lane >= 64 + 8 * m, lane < 72 + 8 * m)
        packed = jnp.where(first, lanes(value[:, :128], 8 * m), packed)
        packed = jnp.where(last, lanes(value[:, 128:], 64 + 8 * m - 120), packed)
    edge[...] = packed


def canopy_source(arrived, cols, counts, forcing, cover, vegetated, canopy_table, root_table, pressure):
    smem = pl.BlockSpec(memory_space=pltpu.SMEM)
    v = vmem()[0]
    return pl.pallas_call(
        source_kernel,
        out_shape=(shaped(ROOT, ROWS, COLS), shaped(ROWS, 128)),
        in_specs=[v, v, smem, v, v, v, smem, smem, v],
        out_specs=(v, v),
        scratch_shapes=[pltpu.VMEM((6 * ROWS, COLS), F32)],
        compiler_params=params(),
        name="canopy_source",
    )(arrived, cols, counts, forcing, cover, vegetated, canopy_table, root_table, pressure)


def owner_kernel(arrived, state, updated):
    def slot(i, carry):
        block = arrived[i]
        old = state[i]
        temp = leaf(old[1:2], block[0:1], block[1:2], block[2:3], block[4:5])
        sub = iota(old.shape, 0)
        base = jnp.where(sub == 1, temp, old)
        upper = pltpu.roll(base, 1, 0)
        lower = pltpu.roll(base, base.shape[0] - 1, 0)
        lower = jnp.where(sub == base.shape[0] - 1, base, lower)
        fresh = 0.6 * base + 0.2 * upper + 0.2 * lower
        fresh = jnp.where(sub == 1, temp, fresh)
        fresh = jnp.where(sub == 0, 0.8 * old + 0.2 * block[3:4], fresh)
        updated[i] = jnp.where(block[5:6] > 0.5, fresh, old)
        return carry

    lax.fori_loop(0, arrived.shape[0], slot, 0)


def owner_update(arrived, state):
    return pl.pallas_call(
        owner_kernel,
        out_shape=shaped(*state.shape),
        in_specs=vmem(2),
        out_specs=vmem()[0],
        compiler_params=params(),
        name="owner_update",
    )(arrived, state)


def edge_pack_kernel(pressure, conductivity, to_right, to_left):
    lane = iota((ROWS, 128), 1)
    for f, field in enumerate((pressure, conductivity)):

        def group(g, carry):
            low = jnp.zeros((ROWS, 128), F32)
            high = jnp.zeros((ROWS, 128), F32)
            for k in range(16):
                here = jnp.logical_and(lane >= 8 * k, lane < 8 * k + 8)
                low = jnp.where(here, lanes(field[g * 16 + k, :, :128], 8 * k), low)
                high = jnp.where(here, lanes(field[g * 16 + k, :, 128:], 8 * k - 120), high)
            to_left[f, g] = low
            to_right[f, g] = high
            return carry

        lax.fori_loop(0, LEV // 16, group, 0)


def edge_pack(pressure, conductivity):
    return pl.pallas_call(
        edge_pack_kernel,
        out_shape=(shaped(2, 4, ROWS, 128), shaped(2, 4, ROWS, 128)),
        in_specs=vmem(2),
        out_specs=tuple(vmem(2)),
        compiler_params=params(),
        name="edge_pack",
    )(pressure, conductivity)


RIM = LEV * 2 + 8


def rim_pack_kernel(pressure, conductivity, from_left, from_right, to_next, to_prev):
    low = iota((8, COLS), 0) < 4
    low_one = iota((8, 128), 0) < 4

    def level(z, carry):
        q = pressure[z]
        k = conductivity[z]
        ahead = jnp.where(low, pltpu.roll(q[8:], 4, 0), k[8:])
        behind = jnp.where(low, q[:8], pltpu.roll(k[:8], 4, 0))
        to_next[2 * z] = ahead[:, :128]
        to_next[2 * z + 1] = ahead[:, 128:]
        to_prev[2 * z] = behind[:, :128]
        to_prev[2 * z + 1] = behind[:, 128:]
        return carry

    lax.fori_loop(0, LEV, level, 0, unroll=4)
    for s, side in enumerate((from_left, from_right)):
        for g in range(4):
            q = side[0, g]
            k = side[1, g]
            to_next[2 * LEV + 4 * s + g] = jnp.where(low_one, pltpu.roll(q[8:], 4, 0), k[8:])
            to_prev[2 * LEV + 4 * s + g] = jnp.where(low_one, q[:8], pltpu.roll(k[:8], 4, 0))


def rim_pack(pressure, conductivity, from_left, from_right):
    return pl.pallas_call(
        rim_pack_kernel,
        out_shape=(shaped(RIM, 8, 128), shaped(RIM, 8, 128)),
        in_specs=vmem(4),
        out_specs=tuple(vmem(2)),
        compiler_params=params(),
        name="rim_pack",
    )(pressure, conductivity, from_left, from_right)


def source_rim_kernel(source, edge, from_left, from_right, wide, to_both):
    lane = iota((ROWS, 128), 1)
    low = iota((8, XC), 0) < 4
    wide[...] = jnp.zeros_like(wide)
    for m in range(ROOT):
        halo = jnp.where(lane < 8, lanes(from_right[...], -8 * m), 0.0)
        halo = jnp.where(lane >= 120, lanes(from_left[...], 120 - 64 - 8 * m), halo)
        row = jnp.concatenate([source[m], halo], axis=1)
        wide[m, 0:ROWS, :] = row
        to_both[m] = jnp.where(low, row[:8], row[8:])


def source_rim(source, edge, from_left, from_right):
    return pl.pallas_call(
        source_rim_kernel,
        out_shape=(shaped(ROOT, XR, XC), shaped(ROOT, 8, XC)),
        in_specs=vmem(4),
        out_specs=tuple(vmem(2)),
        compiler_params=params(),
        name="source_rim",
    )(source, edge, from_left, from_right)


def harmonic(m, n):
    return 2.0 * m * n / jnp.maximum(m + n, 1e-30)


def own(v):
    return v[:ROWS, :COLS]


def couplings(q_ref, k_ref, right_hand, cx, cy, cz, cap, v0):
    def parts(z):
        q = q_ref[z]
        s = 0.5 + 0.5 * jnp.tanh(q)
        return q, s, k_ref[z] * (0.1 + 0.9 * s)

    def level(z, carry):
        q, s, m, flux_z = carry
        after = jnp.minimum(z + 1, LEV - 1)
        q_n, s_n, m_n = parts(after)
        y = harmonic(m, right(m))
        x = harmonic(m, below(m))
        deep = jnp.where(z < LEV - 1, harmonic(m, m_n), 0.0)
        cy[z] = y
        cx[z] = x
        cz[z] = deep
        cap[z] = 1.4 * s * (1.0 - s) + STORE
        flow_y = y * (q - right(q))
        flow_x = x * (q - below(q))
        flow_z = deep * (q - q_n + GRAV)
        out = (flow_y - left(flow_y)) + (flow_x - above(flow_x)) + (flow_z - flux_z)
        v0[z] = right_hand(z, q, s) - out
        return q_n, s_n, m_n, flow_z

    lax.fori_loop(0, LEV, level, (*parts(0), jnp.zeros((XR, XC), F32)))


def apply(v_in, cx, cy, cz, cap, visit, sums):
    def level(z, carry):
        v, flux_z, held = carry
        v_n = v_in[jnp.minimum(z + 1, LEV - 1)]
        flow_y = cy[z] * (v - right(v))
        flow_x = cx[z] * (v - below(v))
        flow_z = cz[z] * (v - v_n)
        image = (
            cap[z] * v
            + (flow_y - left(flow_y))
            + (flow_x - above(flow_x))
            + (flow_z - flux_z)
        )
        held = visit(z, v, image, held)
        return v_n, flow_z, held

    start = (v_in[0], jnp.zeros((XR, XC), F32), sums)
    return lax.fori_loop(0, LEV, level, start)[2]


def chain(cx, cy, cz, cap, v0, v1, v2, moments):
    zero = jnp.zeros((ROWS, COLS), F32)

    def store(target):
        def visit(z, v, image, held):
            target[z] = image
            a, b = own(v), own(image)
            return held[0] + a * a, held[1] + a * b

        return visit

    def last(z, v, image, held):
        a, b = own(v), own(image)
        return held[0] + a * a, held[1] + a * b

    sums = []
    sums += apply(v0, cx, cy, cz, cap, store(v1), (zero, zero))
    sums += apply(v1, cx, cy, cz, cap, store(v2), (zero, zero))
    sums += apply(v2, cx, cy, cz, cap, last, (zero, zero))
    row = jnp.zeros((1, 128), F32)
    lane = iota((1, 128), 1)
    for k, held in enumerate(sums):
        value = jnp.sum(jnp.sum(held, axis=0, keepdims=True), axis=1, keepdims=True)
        row = jnp.where(lane == k, value, row)
    moments[...] = jnp.broadcast_to(row, moments.shape)


def coefficients(gathered):
    row = jnp.sum(gathered[...], axis=0, keepdims=True)
    lane = iota((1, 128), 1)
    m = [
        jnp.sum(jnp.where(lane == k, row, 0.0), axis=1, keepdims=True) for k in range(6)
    ]

    def dot(a, b, shift):
        total = jnp.zeros((1, 1), F32)
        for i, p in enumerate(a):
            for j, q in enumerate(b):
                total = total + p * q * m[i + j + shift]
        return total

    one = jnp.ones((1, 1), F32)
    a0 = m[0] / m[1]
    r1 = [one, -a0]
    n1 = dot(r1, r1, 0)
    b0 = n1 / m[0]
    p1 = [one + b0, -a0]
    a1 = n1 / dot(p1, p1, 1)
    r2 = [one, -a0 - a1 * p1[0], -a1 * p1[1]]
    n2 = dot(r2, r2, 0)
    b1 = n2 / n1
    p2 = [r2[0] + b1 * p1[0], r2[1] + b1 * p1[1], r2[2]]
    a2 = n2 / dot(p2, p2, 1)
    return (
        a0 + a1 * p1[0] + a2 * p2[0],
        a1 * p1[1] + a2 * p2[1],
        a2 * p2[2],
    )


def spread(part, lane, k, width, half):
    moved = lanes(part, -half - width * k) if half < width else lanes(part, -width * k)
    return moved


def first_kernel(
    pressure, conductivity, from_left, from_right, from_prev, from_next, source, source_prev, source_next,
    q, k, b, v0, v1, v2, to_next, to_prev, moments,
    cx, cy, cz, cap,
):
    lane = iota((ROWS, 128), 1)
    lane8 = iota((8, 128), 1)
    low = iota((8, COLS), 0) < 4
    low_one = iota((8, 128), 0) < 4

    def fill(g, carry):
        for j in range(16):
            z = g * 16 + j
            q[z, 0:ROWS, 0:COLS] = pressure[z]
            k[z, 0:ROWS, 0:COLS] = conductivity[z]
            for f, target in enumerate((q, k)):
                halo = jnp.where(lane < 8, lanes(from_right[f, g], -8 * j), 0.0)
                halo = jnp.where(lane >= 120, lanes(from_left[f, g], 120 - 8 * j), halo)
                target[z, 0:ROWS, COLS:] = halo
            ahead = jnp.concatenate([from_next[2 * z], from_next[2 * z + 1]], axis=1)
            behind = jnp.concatenate([from_prev[2 * z], from_prev[2 * z + 1]], axis=1)
            q[z, ROWS:, 0:COLS] = jnp.where(low, ahead, pltpu.roll(behind, 4, 0))
            k[z, ROWS:, 0:COLS] = jnp.where(low, pltpu.roll(ahead, 4, 0), behind)
            corner = []
            for side in (from_next, from_prev):
                halo = jnp.where(lane8 < 8, lanes(side[2 * LEV + 4 + g], -8 * j), 0.0)
                halo = jnp.where(lane8 >= 120, lanes(side[2 * LEV + g], 120 - 8 * j), halo)
                corner.append(halo)
            q[z, ROWS:, COLS:] = jnp.where(low_one, corner[0], pltpu.roll(corner[1], 4, 0))
            k[z, ROWS:, COLS:] = jnp.where(low_one, pltpu.roll(corner[0], 4, 0), corner[1])
        return carry

    lax.fori_loop(0, LEV // 16, fill, 0)

    low_wide = iota((8, XC), 0) < 4
    for m in range(ROOT):
        b[m, 0:ROWS, :] = source[m, 0:ROWS, :]
        b[m, ROWS:, :] = jnp.where(low_wide, source_next[m], source_prev[m])

    def right_hand(z, q_z, s_z):
        level = b[jnp.minimum(z, ROOT - 1)]
        return jnp.where(z < ROOT, level, 0.0)

    couplings(q, k, right_hand, cx, cy, cz, cap, v0)
    chain(cx, cy, cz, cap, v0, v1, v2, moments)

    sub = iota((8, XC), 0)

    def rims(g, carry):
        corner_next = jnp.zeros((8, 128), F32)
        corner_prev = jnp.zeros((8, 128), F32)
        for j in range(16):
            z = g * 16 + j
            t0, t1, t2 = v0[z, 0:8, :], v1[z, 0:8, :], v2[z, 0:8, :]
            prev = jnp.where(sub >= 6, pltpu.roll(t1, 4, 0), t2)
            prev = jnp.where(sub == 4, pltpu.roll(t0, 1, 0), prev)
            t0, t1, t2 = v0[z, 8:16, :], v1[z, 8:16, :], v2[z, 8:16, :]
            nxt = jnp.where(sub < 2, pltpu.roll(t1, 4, 0), t2)
            nxt = jnp.where(sub == 3, pltpu.roll(t0, 7, 0), nxt)
            to_next[2 * z] = nxt[:, 0:128]
            to_next[2 * z + 1] = nxt[:, 128:256]
            to_prev[2 * z] = prev[:, 0:128]
            to_prev[2 * z + 1] = prev[:, 128:256]
            here = jnp.logical_and(lane8 >= 8 * j, lane8 < 8 * j + 8)
            corner_next = jnp.where(here, lanes(nxt[:, 256:], 4 + 8 * j), corner_next)
            corner_prev = jnp.where(here, lanes(prev[:, 256:], 4 + 8 * j), corner_prev)
        to_next[2 * LEV + g] = corner_next
        to_prev[2 * LEV + g] = corner_prev
        return carry

    lax.fori_loop(0, LEV // 16, rims, 0)


RIM2 = 2 * LEV + 4


def wide_shape():
    return shaped(LEV, XR, XC)


def scratch(n):
    return [pltpu.VMEM((LEV, XR, XC), F32)] * n


def first_newton(*arrays):
    w = wide_shape()
    outs = (w, w, shaped(ROOT, XR, XC), w, w, w, shaped(RIM2, 8, 128), shaped(RIM2, 8, 128), shaped(128, 128))
    return pl.pallas_call(
        first_kernel,
        out_shape=outs,
        in_specs=vmem(len(arrays)),
        out_specs=tuple(vmem(len(outs))),
        scratch_shapes=scratch(4),
        compiler_params=params(),
        name="first_newton",
    )(*arrays)


def second_kernel(
    q, k, b, u0, u1, u2, from_prev, from_next, gathered,
    q_own, w0, w1, w2, moments,
    q1, cx, cy, cz, cap, v0, v1, v2,
):
    c0, c1, c2 = coefficients(gathered)
    sub = iota((8, XC), 0)
    lane8 = iota((8, 128), 1)
    row_in = jnp.logical_or(lane8 < 4, lane8 >= 124)

    def update(g, carry):
        for j in range(16):
            z = g * 16 + j
            q1[z, 0:ROWS, :] = (
                q[z, 0:ROWS, :] + c0 * u0[z, 0:ROWS, :] + c1 * u1[z, 0:ROWS, :] + c2 * u2[z, 0:ROWS, :]
            )
            sides = []
            for side in (from_next, from_prev):
                halo = jnp.where(row_in, lanes(side[2 * LEV + g], -4 - 8 * j), 0.0)
                sides.append(jnp.concatenate([side[2 * z], side[2 * z + 1], halo], axis=1))
            ahead, behind = sides
            t0, t1, t2 = u0[z, ROWS:, :], u1[z, ROWS:, :], u2[z, ROWS:, :]
            t0 = jnp.where(sub == 3, pltpu.roll(ahead, 7, 0), t0)
            t0 = jnp.where(sub == 4, pltpu.roll(behind, 1, 0), t0)
            t1 = jnp.where(jnp.logical_or(sub == 2, sub == 3), pltpu.roll(ahead, 4, 0), t1)
            t1 = jnp.where(jnp.logical_or(sub == 4, sub == 5), pltpu.roll(behind, 4, 0), t1)
            t2 = jnp.where(jnp.logical_and(sub >= 1, sub <= 3), ahead, t2)
            t2 = jnp.where(jnp.logical_and(sub >= 4, sub <= 6), behind, t2)
            q1[z, ROWS:, :] = q[z, ROWS:, :] + c0 * t0 + c1 * t1 + c2 * t2
        return carry

    lax.fori_loop(0, LEV // 16, update, 0)

    def right_hand(z, q_z, s_z):
        before = q[z]
        s_b = 0.5 + 0.5 * jnp.tanh(before)
        stored = 0.7 * (s_z - s_b) + STORE * (q_z - before)
        level = b[jnp.minimum(z, ROOT - 1)]
        return jnp.where(z < ROOT, level, 0.0) - stored

    couplings(q1, k, right_hand, cx, cy, cz, cap, v0)
    chain(cx, cy, cz, cap, v0, v1, v2, moments)
    for source, target in ((q1, q_own), (v0, w0), (v1, w1), (v2, w2)):
        target[...] = source[:, 0:ROWS, 0:COLS]


def second_newton(*arrays):
    o = shaped(LEV, ROWS, COLS)
    outs = (o, o, o, o, shaped(128, 128))
    return pl.pallas_call(
        second_kernel,
        out_shape=outs,
        in_specs=vmem(len(arrays)),
        out_specs=tuple(vmem(len(outs))),
        scratch_shapes=scratch(8),
        compiler_params=params(),
        name="second_newton",
    )(*arrays)


def final_kernel(q, v0, v1, v2, gathered, out):
    c0, c1, c2 = coefficients(gathered)

    def level(z, carry):
        out[z] = q[z] + c0 * v0[z] + c1 * v1[z] + c2 * v2[z]
        return carry

    lax.fori_loop(0, LEV, level, 0, unroll=4)


def final_update(*arrays):
    return pl.pallas_call(
        final_kernel,
        out_shape=shaped(LEV, ROWS, COLS),
        in_specs=vmem(len(arrays)),
        out_specs=vmem()[0],
        compiler_params=params(),
        name="final_update",
    )(*arrays)


def exchange(to_high, to_low, axis):
    count = lax.axis_size(axis)
    up = [(i, i + 1) for i in range(count - 1)]
    down = [(i + 1, i) for i in range(count - 1)]
    return lax.ppermute(to_high, axis, up), lax.ppermute(to_low, axis, down)


def share(moments):
    return lax.all_to_all(moments, ("gx", "gy"), split_axis=0, concat_axis=0, tiled=True)


def body(
    pressure_old,
    conductivity,
    forcing,
    vegetated,
    cover_type,
    canopy_table,
    root_table,
    pair_counts,
    send_cols,
    canopy_state,
):
    owners = send_cols.shape[1]
    cols = send_cols.reshape(owners, COLS)
    counts = pair_counts.reshape(owners)
    state = canopy_state.reshape(owners, 16, COLS)

    to_right, to_left = edge_pack(pressure_old, conductivity)
    from_left, from_right = exchange(to_right, to_left, "gy")
    payload = canopy_send(forcing, cover_type, canopy_table, counts, cols, state)
    to_next, to_prev = rim_pack(pressure_old, conductivity, from_left, from_right)
    from_prev, from_next = exchange(to_next, to_prev, "gx")
    arrived = lax.all_to_all(payload, "gx", split_axis=0, concat_axis=0, tiled=True)

    source, edge = canopy_source(
        arrived, cols, counts, forcing, cover_type, vegetated, canopy_table, root_table, pressure_old[:ROOT]
    )
    source_left, source_right = exchange(edge, edge, "gy")
    source_wide, both = source_rim(source, edge, source_left, source_right)
    source_prev, source_next = exchange(both, both, "gx")
    new_state = owner_update(arrived, state).reshape(canopy_state.shape)

    q, k, b, v0, v1, v2, to_next, to_prev, moments = first_newton(
        pressure_old, conductivity, from_left, from_right, from_prev, from_next,
        source_wide, source_prev, source_next,
    )
    from_prev, from_next = exchange(to_next, to_prev, "gx")
    gathered = share(moments)
    q1, w0, w1, w2, moments = second_newton(q, k, b, v0, v1, v2, from_prev, from_next, gathered)
    pressure = final_update(q1, w0, w1, w2, share(moments))
    return pressure, new_state


def solution(mesh):
    placed = (
        P(None, "gx", "gy"),
        P(None, "gx", "gy"),
        P(None, "gx", "gy"),
        P("gx", "gy"),
        P("gx", "gy"),
        P(),
        P(),
        P("gx", None, "gy"),
        P("gx", None, "gy", None),
        P("gx", None, "gy", None, None),
    )
    return jax.shard_map(
        body,
        mesh=mesh,
        in_specs=placed,
        out_specs=(P(None, "gx", "gy"), P("gx", None, "gy", None, None)),
        check_vma=False,
    )
```

```python
import jax
import jax.numpy as jnp
from jax import lax
from jax.experimental import pallas as pl
from jax.experimental.pallas import tpu as pltpu
from jax.sharding import PartitionSpec as P

FORC = 8
ROOT = 8
LEV = 64
ROWS = 16
COLS = 256
L = 8
HALO = 7
XR = ROWS + 2 * HALO
XC = 384
OUTSIDE = 1e37
STORE = 0.05
GRAV = 0.5
F32 = jnp.float32
BF16 = jnp.bfloat16


def vmem(n=1):
    return [pl.BlockSpec(memory_space=pltpu.VMEM)] * n


def params(mib):
    return pltpu.CompilerParams(vmem_limit_bytes=mib * 1024 * 1024)


def shaped(*shape):
    return jax.ShapeDtypeStruct(shape, F32)


def iota(shape, dim):
    return lax.broadcasted_iota(jnp.int32, shape, dim)


def right(v):
    return pltpu.roll(v, v.shape[1] - 1, 1)


def left(v):
    return pltpu.roll(v, 1, 1)


def deeper(v):
    return pltpu.roll(v, v.shape[0] - 1, 0)


def higher(v):
    return pltpu.roll(v, 1, 0)


def lanes(v, shift):
    return v if shift % 128 == 0 else pltpu.roll(v, shift % 128, v.ndim - 1)


def pieces(v):
    high = v.astype(BF16)
    rest = v - high.astype(F32)
    mid = rest.astype(BF16)
    low = (rest - mid.astype(F32)).astype(BF16)
    return high, mid, low


def canopy_send_kernel(
    forcing, cover, canopy_table, counts, cols, state, payload, split, gathered
):
    weights = [jnp.zeros((ROWS, COLS), F32) for _ in range(FORC)]
    kinds = cover[...]
    for kind in range(canopy_table.shape[0]):
        hit = kinds == kind
        for m in range(FORC):
            weights[m] = jnp.where(hit, canopy_table[kind, m], weights[m])
    total = weights[0] * forcing[0]
    for m in range(1, FORC):
        total = total + weights[m] * forcing[m]
    conductance = 2.0 * jax.nn.sigmoid(total)
    channels = [forcing[0], forcing[1], forcing[2], jnp.tanh(forcing[4]), conductance]
    used = len(channels)
    for c, channel in enumerate(channels):
        for p, piece in enumerate(pieces(channel)):
            split[pl.ds((p * used + c) * ROWS, ROWS), :] = piece

    def owner(o, carry):
        index = cols[pl.ds(o, 1), :]
        row_hit = iota((ROWS, COLS), 0) == (index // COLS)
        col_hit = iota((COLS, COLS), 0) == (index % COLS)
        onehot = jnp.where(col_hit, 1.0, 0.0).astype(BF16)
        picked = jnp.dot(split[...], onehot, preferred_element_type=F32)
        span = used * ROWS
        picked = picked[:span] + picked[span : 2 * span] + picked[2 * span :]
        sub = iota((8, COLS), 0)
        out = pltpu.roll(state[o, 0:8, :], 6, 0)
        for c in range(used):
            chosen = jnp.where(row_hit, picked[c * ROWS : (c + 1) * ROWS], 0.0)
            chosen = jnp.sum(chosen, axis=0, keepdims=True)
            out = jnp.where(sub == c, chosen, out)
        live = jnp.where(iota((8, COLS), 1) < counts[o], 1.0, 0.0)
        payload[o] = jnp.where(sub == used, live, out)
        return carry

    lax.fori_loop(0, cols.shape[0], owner, 0)


def canopy_send(forcing, cover, canopy_table, counts, cols, state):
    owners = cols.shape[0]
    return pl.pallas_call(
        canopy_send_kernel,
        out_shape=shaped(owners, 8, COLS),
        in_specs=vmem(2)
        + [pl.BlockSpec(memory_space=pltpu.SMEM)] * 2
        + vmem(2),
        out_specs=vmem()[0],
        scratch_shapes=[
            pltpu.VMEM((15 * ROWS, COLS), BF16),
            pltpu.VMEM((8, COLS), F32),
        ],
        compiler_params=params(8),
        name="canopy_send",
    )(forcing, cover, canopy_table, counts, cols, state)


def softplus(v):
    return jnp.maximum(v, 0.0) + jnp.log1p(jnp.exp(-jnp.abs(v)))


def leaf(start, f0, f1, f2, g):
    temp = start
    for _ in range(3):
        temp = 0.5 * (start + f0) + 0.5 * jnp.tanh(f1 - g * (temp - f2))
    return temp


def source_kernel(
    arrived, cols, counts, forcing, cover, vegetated, canopy_table, root_table, pressure,
    source, to_right, to_left, total, turned,
):
    total[...] = jnp.zeros_like(total)

    def owner(o, carry):
        index = cols[pl.ds(o, 1), :]
        row_hit = iota((ROWS, COLS), 0) == (index // COLS)
        col_hit = iota((COLS, COLS), 0) == (index % COLS)
        onehot = jnp.where(col_hit, 1.0, 0.0).astype(BF16)
        wanted = jnp.logical_and(row_hit, iota((ROWS, COLS), 1) < counts[o])
        block = arrived[o]
        parts = []
        for c in (6, 7):
            value = jnp.where(wanted, block[c : c + 1, :], 0.0)
            parts.extend(pieces(value))
        stacked = jnp.concatenate(parts, axis=0)
        placed = lax.dot_general(
            stacked, onehot, (((1,), (1,)), ((), ())), preferred_element_type=F32
        )
        total[...] += placed
        return carry

    lax.fori_loop(0, cols.shape[0], owner, 0)

    def piece(k):
        return total[k * ROWS : (k + 1) * ROWS, :]

    water = piece(0) + piece(1) + piece(2)
    start = piece(3) + piece(4) + piece(5)
    kinds = cover[...]
    weights = [jnp.zeros((ROWS, COLS), F32) for _ in range(FORC)]
    roots = [jnp.zeros((ROWS, COLS), F32) for _ in range(ROOT)]
    for kind in range(canopy_table.shape[0]):
        hit = kinds == kind
        for m in range(FORC):
            weights[m] = jnp.where(hit, canopy_table[kind, m], weights[m])
        for m in range(ROOT):
            roots[m] = jnp.where(hit, root_table[kind, m], roots[m])
    mixed = weights[0] * forcing[0]
    for m in range(1, FORC):
        mixed = mixed + weights[m] * forcing[m]
    conductance = 2.0 * jax.nn.sigmoid(mixed)
    temp = leaf(start, forcing[0], forcing[1], forcing[2], conductance)
    demand = conductance * softplus(temp - forcing[3]) / (1.0 + water * water)
    planted = vegetated[...] == 1
    demand = jnp.where(planted, demand, 0.0)
    dry = jnp.where(planted, 0.0, 0.5)
    for m in range(ROOT):
        moist = jax.nn.sigmoid(2.0 * (pressure[m] + 1.5))
        value = -(demand * roots[m] * moist)
        if m == 0:
            evaporation = dry * softplus(forcing[3] - forcing[2]) * moist
            value = value + (0.3 * softplus(forcing[4]) - evaporation)
        for t in range(2):
            turned[pl.ds(t * 128 + m * ROWS, ROWS), :] = value[:, t * 128 : t * 128 + 128]
    lane = iota((L, 128), 1)
    first = jnp.zeros((L, 128), F32)
    last = jnp.zeros((L, 128), F32)
    for x in range(ROWS):
        low = turned[pl.ds(x, L, stride=ROWS), :]
        high = turned[pl.ds(128 + x, L, stride=ROWS), :]
        source[x, :, :128] = low
        source[x, :, 128:] = high
        here = jnp.logical_and(lane >= 8 * x, lane < 8 * x + 8)
        first = jnp.where(here, lanes(low, 8 * x), first)
        last = jnp.where(here, lanes(high, 8 * x - 120), last)
    to_left[...] = first
    to_right[...] = last


def canopy_source(arrived, cols, counts, forcing, cover, vegetated, canopy_table, root_table, pressure):
    smem = pl.BlockSpec(memory_space=pltpu.SMEM)
    v = vmem()[0]
    return pl.pallas_call(
        source_kernel,
        out_shape=(shaped(ROWS, ROOT, COLS), shaped(L, 128), shaped(L, 128)),
        in_specs=[v, v, smem, v, v, v, smem, smem, v],
        out_specs=(v, v, v),
        scratch_shapes=[pltpu.VMEM((6 * ROWS, COLS), F32), pltpu.VMEM((2 * 128, 128), F32)],
        compiler_params=params(8),
        name="canopy_source",
    )(arrived, cols, counts, forcing, cover, vegetated, canopy_table, root_table, pressure)


def owner_kernel(arrived, state, updated):
    def slot(i, carry):
        block = arrived[i]
        old = state[i]
        temp = leaf(old[1:2], block[0:1], block[1:2], block[2:3], block[4:5])
        sub = iota(old.shape, 0)
        base = jnp.where(sub == 1, temp, old)
        upper = pltpu.roll(base, 1, 0)
        lower = pltpu.roll(base, base.shape[0] - 1, 0)
        lower = jnp.where(sub == base.shape[0] - 1, base, lower)
        fresh = 0.6 * base + 0.2 * upper + 0.2 * lower
        fresh = jnp.where(sub == 1, temp, fresh)
        fresh = jnp.where(sub == 0, 0.8 * old + 0.2 * block[3:4], fresh)
        updated[i] = jnp.where(block[5:6] > 0.5, fresh, old)
        return carry

    lax.fori_loop(0, arrived.shape[0], slot, 0)


def owner_update(arrived, state):
    return pl.pallas_call(
        owner_kernel,
        out_shape=shaped(*state.shape),
        in_specs=vmem(2),
        out_specs=vmem()[0],
        compiler_params=params(8),
        name="owner_update",
    )(arrived, state)


def flat(v):
    return v.reshape(LEV, 2, 8, 2, 128).transpose(0, 1, 3, 2, 4).reshape(32 * LEV, 128)


def unflat(v):
    return v.reshape(LEV, 2, 2, 8, 128).transpose(0, 1, 3, 2, 4).reshape(LEV, ROWS, COLS)


def chunk(x, l, t):
    return pl.ds(32 * l + 16 * (x // 8) + 8 * t + x % 8, 8, stride=32 * L)


def turn_kernel(pressure, conductivity, q, k, to_right, to_left):
    lane = iota((8, 128), 1)

    def layer(l, carry):
        for f, (field, target) in enumerate(((pressure, q), (conductivity, k))):
            first = jnp.zeros((8, 128), F32)
            last = jnp.zeros((8, 128), F32)
            for x in range(ROWS):
                low = field[chunk(x, l, 0), :]
                high = field[chunk(x, l, 1), :]
                target[x, l, :, :128] = low
                target[x, l, :, 128:] = high
                here = jnp.logical_and(lane >= 8 * x, lane < 8 * x + 8)
                first = jnp.where(here, lanes(low, 8 * x), first)
                last = jnp.where(here, lanes(high, 8 * x - 120), last)
            to_left[f, l] = first
            to_right[f, l] = last
        return carry

    lax.fori_loop(0, L, layer, 0)


def turn(pressure, conductivity):
    own_shape = shaped(ROWS, L, 8, COLS)
    return pl.pallas_call(
        turn_kernel,
        out_shape=(own_shape, own_shape, shaped(2, L, 8, 128), shaped(2, L, 8, 128)),
        in_specs=vmem(2),
        out_specs=tuple(vmem(4)),
        compiler_params=params(16),
        name="turn",
    )(pressure, conductivity)


RIM = 2 * HALO * 2 + 2


def rim_kernel(q, k, from_left, from_right, to_next, to_prev):
    low = iota((8, 128), 1) < 64

    def layer(l, carry):
        for f, field in enumerate((q, k)):
            for i in range(HALO):
                for t in range(2):
                    part = pl.ds(128 * t, 128)
                    to_next[2 * (f * HALO + i) + t, l] = field[ROWS - HALO + i, l, :, part]
                    to_prev[2 * (f * HALO + i) + t, l] = field[i, l, :, part]
            a, b = from_left[f, l], from_right[f, l]
            to_next[4 * HALO + f, l] = jnp.where(low, lanes(a, 64), b)
            to_prev[4 * HALO + f, l] = jnp.where(low, a, lanes(b, 64))
        return carry

    lax.fori_loop(0, L, layer, 0)


def rim(*arrays):
    outs = (shaped(RIM, L, 8, 128), shaped(RIM, L, 8, 128))
    return pl.pallas_call(
        rim_kernel,
        out_shape=outs,
        in_specs=vmem(4),
        out_specs=tuple(vmem(2)),
        compiler_params=params(16),
        name="rim",
    )(*arrays)


BHALO = 6
SRIM = 2 * BHALO + 1


def source_rim_kernel(source, from_left, from_right, to_next, to_prev):
    low = iota((L, 128), 1) < 64
    for i in range(BHALO):
        for t in range(2):
            part = pl.ds(128 * t, 128)
            to_next[2 * i + t] = source[ROWS - BHALO + i, :, part]
            to_prev[2 * i + t] = source[i, :, part]
    a, b = from_left[...], from_right[...]
    to_next[2 * BHALO] = jnp.where(low, lanes(a, 64), b)
    to_prev[2 * BHALO] = jnp.where(low, a, lanes(b, 64))


def source_rim(*arrays):
    outs = (shaped(SRIM, L, 128), shaped(SRIM, L, 128))
    return pl.pallas_call(
        source_rim_kernel,
        out_shape=outs,
        in_specs=vmem(3),
        out_specs=tuple(vmem(2)),
        compiler_params=params(8),
        name="source_rim",
    )(*arrays)


def halo_tile(from_left, from_right, lane, at_left, at_right):
    tile = jnp.where(lane < 8, lanes(from_right, -at_right), 0.0)
    return jnp.where(lane >= 120, lanes(from_left, 120 - at_left), tile)


def own(v):
    return v[:, :COLS]


def mobilities(q, k, resist, diag, rows, block):
    def step(i, carry):
        for j in range(block):
            r = rows[0] + i * block + j
            for l in range(L):
                s = 0.5 + 0.5 * jnp.tanh(q[r, l])
                m = k[r, l] * (0.1 + 0.9 * s)
                resist[r, l] = jnp.where(m > 0.0, 0.5 / m, OUTSIDE)
                diag[r, l] = 1.4 * s * (1.0 - s) + STORE
        return carry

    lax.fori_loop(0, (rows[1] - rows[0]) // block, step, 0)


def couplings(q, resist, right_hand, cx, cy, cyl, cz, diag, v0, rows, block):
    last = iota((8, XC), 0) == 7

    def row(r):
        q_0, m_0, q_7, m_7 = q[r, 0], resist[r, 0], q[r, 7], resist[r, 7]
        c_7 = jnp.where(last, 0.0, 1.0 / (m_7 + deeper(m_0)))
        f_7 = c_7 * (q_7 - deeper(q_0) + GRAV)
        cz[r, 7] = c_7
        c_up, f_up = higher(c_7), higher(f_7)
        v, m = q_0, m_0
        for l in range(L):
            if l < L - 1:
                m_n, v_n = resist[r, l + 1], q[r, l + 1]
                c = 1.0 / (m + m_n)
                f = c * (v - v_n + GRAV)
                cz[r, l] = c
            else:
                c, f = c_7, f_7
            y = 1.0 / (m + right(m))
            yl = 1.0 / (m + left(m))
            x = 1.0 / (m + resist[r + 1, l])
            xp = cx[r - 1, l]
            cy[r, l] = y
            cyl[r, l] = yl
            cx[r, l] = x
            out = y * (v - right(v)) + yl * (v - left(v))
            out = out + (x * (v - q[r + 1, l]) + xp * (v - q[r - 1, l])) + (f - f_up)
            diag[r, l] = diag[r, l] + ((y + yl) + (x + xp) + (c + c_up))
            v0[r, l] = right_hand(r, l, v) - out
            c_up, f_up = c, f
            if l < L - 1:
                v, m = v_n, m_n

    def step(i, carry):
        for j in range(block):
            row(rows[0] + i * block + j)
        return carry

    for l in range(L):
        cx[rows[0] - 1, l] = 1.0 / (resist[rows[0] - 1, l] + resist[rows[0], l])
    lax.fori_loop(0, (rows[1] - rows[0]) // block, step, 0)


def apply(v_in, v_out, cx, cy, cyl, cz, diag, rows, block, first):
    zero = jnp.zeros((8, COLS), F32)

    def row(r, held):
        c_up, v_up = higher(cz[r, 7]), higher(v_in[r, 7])
        v_0 = v_in[r, 0]
        v = v_0
        here = jnp.logical_and(r >= HALO, r < HALO + ROWS)
        square, cross = zero, zero
        for l in range(L):
            v_n = v_in[r, l + 1] if l < L - 1 else deeper(v_0)
            c = cz[r, l]
            image = diag[r, l] * v - cy[r, l] * right(v) - cyl[r, l] * left(v)
            image = image - cx[r, l] * v_in[r + 1, l] - cx[r - 1, l] * v_in[r - 1, l]
            image = image - c * v_n - c_up * v_up
            if v_out is not None:
                v_out[r, l] = image
            a, b = own(v), own(image)
            square = square + a * a
            cross = cross + a * b
            v_up, c_up, v = v, c, v_n
        if not first:
            square = jnp.where(here, square, 0.0)
            cross = jnp.where(here, cross, 0.0)
        return held[0] + square, held[1] + cross

    def step(i, held):
        for j in range(block):
            held = row(rows[0] + i * block + j, held)
        return held

    return lax.fori_loop(0, (rows[1] - rows[0]) // block, step, (zero, zero))


def chain(cx, cy, cyl, cz, diag, v0, v1, v2, moments, spans, blocks):
    coefs = (cx, cy, cyl, cz, diag)
    sums = []
    sums += apply(v0, v1, *coefs, spans[0], blocks[0], False)
    sums += apply(v1, v2, *coefs, spans[1], blocks[1], False)
    sums += apply(v2, None, *coefs, spans[2], blocks[2], True)
    row = jnp.zeros((1, 128), F32)
    lane = iota((1, 128), 1)
    for k, held in enumerate(sums):
        value = jnp.sum(jnp.sum(held, axis=0, keepdims=True), axis=1, keepdims=True)
        row = jnp.where(lane == k, value, row)
    moments[...] = jnp.broadcast_to(row, moments.shape)


def coefficients(gathered):
    row = jnp.sum(gathered[...], axis=0, keepdims=True)
    lane = iota((1, 128), 1)
    m = [jnp.sum(jnp.where(lane == k, row, 0.0), axis=1, keepdims=True) for k in range(6)]

    def dot(a, b, shift):
        total = jnp.zeros((1, 1), F32)
        for i, p in enumerate(a):
            for j, q in enumerate(b):
                total = total + p * q * m[i + j + shift]
        return total

    one = jnp.ones((1, 1), F32)
    a0 = m[0] / m[1]
    r1 = [one, -a0]
    n1 = dot(r1, r1, 0)
    b0 = n1 / m[0]
    p1 = [one + b0, -a0]
    a1 = n1 / dot(p1, p1, 1)
    r2 = [one, -a0 - a1 * p1[0], -a1 * p1[1]]
    n2 = dot(r2, r2, 0)
    b1 = n2 / n1
    p2 = [r2[0] + b1 * p1[0], r2[1] + b1 * p1[1], r2[2]]
    a2 = n2 / dot(p2, p2, 1)
    return (
        a0 + a1 * p1[0] + a2 * p2[0],
        a1 * p1[1] + a2 * p2[1],
        a2 * p2[2],
    )


def source_at(b, r, l, sub):
    return jnp.where(sub == 0, pltpu.roll(b[r], (8 - l) % 8, 0), 0.0)


def first_kernel(
    q_own, k_own, from_left, from_right, from_prev, from_next,
    source, source_left, source_right, source_prev, source_next,
    q, k, b, v0, v1, v2, moments,
    resist, cx, cy, cyl, cz, diag,
):
    lane = iota((8, 128), 1)

    def fill(l, carry):
        for f, (field, target) in enumerate(((q_own, q), (k_own, k))):
            for x in range(ROWS):
                target[HALO + x, l, :, :COLS] = field[x, l]
                target[HALO + x, l, :, COLS:] = halo_tile(
                    from_left[f, l], from_right[f, l], lane, 8 * x, 8 * x
                )
            for i in range(HALO):
                for side, r, at in (
                    (from_prev, i, 8 * (8 - HALO + i)),
                    (from_next, HALO + ROWS + i, 8 * i),
                ):
                    for t in range(2):
                        target[r, l, :, 128 * t : 128 * t + 128] = side[2 * (f * HALO + i) + t, l]
                    corner = side[4 * HALO + f, l]
                    target[r, l, :, COLS:] = halo_tile(corner, corner, lane, at, 64 + at)
        return carry

    lax.fori_loop(0, L, fill, 0)

    for x in range(ROWS):
        b[HALO + x, :, :COLS] = source[x]
        b[HALO + x, :, COLS:] = halo_tile(source_left[...], source_right[...], lane, 8 * x, 8 * x)
    gap = HALO - BHALO
    for i in range(BHALO):
        for side, r, at in (
            (source_prev, gap + i, 8 * (8 - BHALO + i)),
            (source_next, HALO + ROWS + i, 8 * i),
        ):
            for t in range(2):
                b[r, :, 128 * t : 128 * t + 128] = side[2 * i + t]
            corner = side[2 * BHALO]
            b[r, :, COLS:] = halo_tile(corner, corner, lane, at, 64 + at)

    sub = iota((8, XC), 0)

    def right_hand(r, l, v):
        return source_at(b, r, l, sub)

    mobilities(q, k, resist, diag, (0, XR), 2)
    couplings(q, resist, right_hand, cx, cy, cyl, cz, diag, v0, (1, XR - 1), 4)
    chain(
        cx, cy, cyl, cz, diag, v0, v1, v2, moments,
        ((2, XR - 2), (3, XR - 3), (HALO, HALO + ROWS)), (13, 8, 8),
    )


def wide():
    return shaped(XR, L, 8, XC)


def scratch(n):
    return [pltpu.VMEM((XR, L, 8, XC), F32)] * n


def first_newton(*arrays):
    w = wide()
    outs = (w, w, shaped(XR, L, XC), w, w, w, shaped(128, 128))
    return pl.pallas_call(
        first_kernel,
        out_shape=outs,
        in_specs=vmem(len(arrays)),
        out_specs=tuple(vmem(len(outs))),
        scratch_shapes=scratch(6),
        compiler_params=params(44),
        name="first_newton",
    )(*arrays)


def second_kernel(
    q, k, b, u0, u1, u2, gathered,
    q_own, w0, w1, w2, moments,
    q1, resist, cx, cy, cyl, cz, diag, v0, v1, v2,
):
    c0, c1, c2 = coefficients(gathered)

    def update(r, carry):
        for l in range(L):
            q1[r, l] = q[r, l] + c0 * u0[r, l] + c1 * u1[r, l] + c2 * u2[r, l]
        return carry

    lax.fori_loop(3, XR - 3, update, 0, unroll=2)
    sub = iota((8, XC), 0)

    def right_hand(r, l, v):
        before = q[r, l]
        stored = 0.35 * (jnp.tanh(v) - jnp.tanh(before)) + STORE * (v - before)
        return source_at(b, r, l, sub) - stored

    mobilities(q1, k, resist, diag, (3, XR - 3), 2)
    couplings(q1, resist, right_hand, cx, cy, cyl, cz, diag, v0, (4, XR - 4), 2)
    chain(
        cx, cy, cyl, cz, diag, v0, v1, v2, moments,
        ((5, XR - 5), (6, XR - 6), (HALO, HALO + ROWS)), (10, 9, 8),
    )

    def keep(x, carry):
        for l in range(L):
            for source, target in ((q1, q_own), (v0, w0), (v1, w1), (v2, w2)):
                target[x, l] = source[HALO + x, l, :, :COLS]
        return carry

    lax.fori_loop(0, ROWS, keep, 0)


def second_newton(*arrays):
    o = shaped(ROWS, L, 8, COLS)
    outs = (o, o, o, o, shaped(128, 128))
    return pl.pallas_call(
        second_kernel,
        out_shape=outs,
        in_specs=vmem(len(arrays)),
        out_specs=tuple(vmem(len(outs))),
        scratch_shapes=scratch(10),
        compiler_params=params(54),
        name="second_newton",
    )(*arrays)


def final_kernel(q, v0, v1, v2, gathered, out):
    c0, c1, c2 = coefficients(gathered)

    def row(x, carry):
        for l in range(L):
            value = q[x, l] + c0 * v0[x, l] + c1 * v1[x, l] + c2 * v2[x, l]
            out[chunk(x, l, 0), :] = value[:, :128]
            out[chunk(x, l, 1), :] = value[:, 128:]
        return carry

    lax.fori_loop(0, ROWS, row, 0)


def final_update(*arrays):
    return pl.pallas_call(
        final_kernel,
        out_shape=shaped(32 * LEV, 128),
        in_specs=vmem(len(arrays)),
        out_specs=vmem()[0],
        compiler_params=params(16),
        name="final_update",
    )(*arrays)


def exchange(to_high, to_low, axis):
    count = lax.axis_size(axis)
    up = [(i, i + 1) for i in range(count - 1)]
    down = [(i + 1, i) for i in range(count - 1)]
    return lax.ppermute(to_high, axis, up), lax.ppermute(to_low, axis, down)


def share(moments):
    return lax.all_to_all(moments, ("gx", "gy"), split_axis=0, concat_axis=0, tiled=True)


def body(
    pressure_old,
    conductivity,
    forcing,
    vegetated,
    cover_type,
    canopy_table,
    root_table,
    pair_counts,
    send_cols,
    canopy_state,
):
    owners = send_cols.shape[1]
    cols = send_cols.reshape(owners, COLS)
    counts = pair_counts.reshape(owners)
    state = canopy_state.reshape(owners, 16, COLS)

    q_own, k_own, to_right, to_left = turn(flat(pressure_old), flat(conductivity))
    from_left, from_right = exchange(to_right, to_left, "gy")
    payload = canopy_send(forcing, cover_type, canopy_table, counts, cols, state)
    to_next, to_prev = rim(q_own, k_own, from_left, from_right)
    from_prev, from_next = exchange(to_next, to_prev, "gx")
    arrived = lax.all_to_all(payload, "gx", split_axis=0, concat_axis=0, tiled=True)

    source, to_right, to_left = canopy_source(
        arrived, cols, counts, forcing, cover_type, vegetated, canopy_table, root_table, pressure_old[:ROOT]
    )
    source_left, source_right = exchange(to_right, to_left, "gy")
    to_next, to_prev = source_rim(source, source_left, source_right)
    source_prev, source_next = exchange(to_next, to_prev, "gx")
    new_state = owner_update(arrived, state).reshape(canopy_state.shape)

    q, k, b, v0, v1, v2, moments = first_newton(
        q_own, k_own, from_left, from_right, from_prev, from_next,
        source, source_left, source_right, source_prev, source_next,
    )
    q1, w0, w1, w2, moments = second_newton(q, k, b, v0, v1, v2, share(moments))
    pressure = unflat(final_update(q1, w0, w1, w2, share(moments)))
    return pressure, new_state


def solution(mesh):
    placed = (
        P(None, "gx", "gy"),
        P(None, "gx", "gy"),
        P(None, "gx", "gy"),
        P("gx", "gy"),
        P("gx", "gy"),
        P(),
        P(),
        P("gx", None, "gy"),
        P("gx", None, "gy", None),
        P("gx", None, "gy", None, None),
    )
    return jax.shard_map(
        body,
        mesh=mesh,
        in_specs=placed,
        out_specs=(P(None, "gx", "gy"), P("gx", None, "gy", None, None)),
        check_vma=False,
    )
```

```python
import jax
import jax.numpy as jnp
from jax import lax
from jax.experimental import pallas as pl
from jax.experimental.pallas import tpu as pltpu
from jax.sharding import PartitionSpec as P

FORC = 8
ROOT = 8
LEV = 64
ROWS = 16
COLS = 256
L = 8
HALO = 7
XR = ROWS + 2 * HALO
XC = 384
OUTSIDE = 1e37
BHALO = 6
SRIM = 2 * BHALO
STORE = 0.05
GRAV = 0.5
F32 = jnp.float32
BF16 = jnp.bfloat16


def vmem(n=1):
    return [pl.BlockSpec(memory_space=pltpu.VMEM)] * n


def params(mib):
    return pltpu.CompilerParams(vmem_limit_bytes=mib * 1024 * 1024)


def shaped(*shape):
    return jax.ShapeDtypeStruct(shape, F32)


def iota(shape, dim):
    return lax.broadcasted_iota(jnp.int32, shape, dim)


def right(v):
    return pltpu.roll(v, v.shape[1] - 1, 1)


def left(v):
    return pltpu.roll(v, 1, 1)


def deeper(v):
    return pltpu.roll(v, v.shape[0] - 1, 0)


def higher(v):
    return pltpu.roll(v, 1, 0)


def lanes(v, shift):
    return v if shift % 128 == 0 else pltpu.roll(v, shift % 128, v.ndim - 1)


def pieces(v):
    high = v.astype(BF16)
    rest = v - high.astype(F32)
    mid = rest.astype(BF16)
    low = (rest - mid.astype(F32)).astype(BF16)
    return high, mid, low


def in_hbm(v):
    return pltpu.with_memory_space_constraint(v, pltpu.HBM)


def smem():
    return pl.BlockSpec(memory_space=pltpu.SMEM)


def looked_up(kinds, table):
    found = [jnp.zeros(kinds.shape, F32) for _ in range(table.shape[0])]
    for kind in range(table.shape[1]):
        hit = kinds == kind
        for m in range(table.shape[0]):
            found[m] = jnp.where(hit, table[m, kind], found[m])
    return found


def hits(index):
    row = lax.shift_right_logical(index, 8)
    col = jnp.bitwise_and(index, COLS - 1)
    row_hit = iota((ROWS, COLS), 0) == row
    col_hit = iota((COLS, COLS), 0) == col
    return row_hit, jnp.where(col_hit, 1.0, 0.0).astype(BF16)


def canopy_send_kernel(
    forcing, cover, canopy_table, counts, cols, state, payload, conductance, split
):
    weights = looked_up(cover[...], canopy_table)
    total = weights[0] * forcing[0]
    for m in range(1, FORC):
        total = total + weights[m] * forcing[m]
    g = 2.0 * jax.nn.sigmoid(total)
    conductance[...] = g
    channels = [forcing[0], forcing[1], forcing[2], jnp.tanh(forcing[4]), g]
    used = len(channels)
    for c, channel in enumerate(channels):
        for p, piece in enumerate(pieces(channel)):
            split[pl.ds((p * used + c) * ROWS, ROWS), :] = piece

    def owner(o, carry):
        row_hit, onehot = hits(cols[o])
        picked = jnp.dot(split[...], onehot, preferred_element_type=F32)
        span = used * ROWS
        picked = picked[:span] + picked[span : 2 * span] + picked[2 * span :]
        sub = iota((8, COLS), 0)
        out = pltpu.roll(state[o, 0:8, :], 6, 0)
        for c in range(used):
            chosen = jnp.where(row_hit, picked[c * ROWS : (c + 1) * ROWS], 0.0)
            chosen = jnp.sum(chosen, axis=0, keepdims=True)
            out = jnp.where(sub == c, chosen, out)
        live = jnp.where(iota((8, COLS), 1) < counts[o], 1.0, 0.0)
        payload[o] = jnp.where(sub == used, live, out)
        return carry

    lax.fori_loop(0, cols.shape[0], owner, 0, unroll=4)


def canopy_send(forcing, cover, canopy_table, counts, cols, state):
    owners = cols.shape[0]
    return pl.pallas_call(
        canopy_send_kernel,
        out_shape=(shaped(owners, 8, COLS), shaped(ROWS, COLS)),
        in_specs=vmem(2) + [smem(), smem()] + vmem(2),
        out_specs=tuple(vmem(2)),
        scratch_shapes=[pltpu.VMEM((15 * ROWS, COLS), BF16)],
        compiler_params=params(16),
        name="canopy_send",
    )(forcing, cover, canopy_table, counts, cols, state)


def softplus(v):
    return jnp.maximum(v, 0.0) + jnp.log1p(jnp.exp(-jnp.abs(v)))


def leaf(start, f0, f1, f2, g):
    temp = start
    for _ in range(3):
        temp = 0.5 * (start + f0) + 0.5 * jnp.tanh(f1 - g * (temp - f2))
    return temp


def source_kernel(
    arrived, cols, counts, forcing, conductance, uptake, surface,
    source, to_next, to_prev, total, turned,
):
    total[...] = jnp.zeros_like(total)

    def owner(o, carry):
        row_hit, onehot = hits(cols[o])
        wanted = jnp.logical_and(row_hit, iota((ROWS, COLS), 1) < counts[o])
        block = arrived[o]
        parts = []
        for c in (6, 7):
            value = jnp.where(wanted, block[c : c + 1, :], 0.0)
            parts.extend(pieces(value))
        stacked = jnp.concatenate(parts, axis=0)
        total[...] += lax.dot_general(
            stacked, onehot, (((1,), (1,)), ((), ())), preferred_element_type=F32
        )
        return carry

    lax.fori_loop(0, cols.shape[0], owner, 0, unroll=4)

    def piece(k):
        return total[k * ROWS : (k + 1) * ROWS, :]

    water = piece(0) + piece(1) + piece(2)
    start = piece(3) + piece(4) + piece(5)
    g = conductance[...]
    temp = leaf(start, forcing[0], forcing[1], forcing[2], g)
    demand = g * softplus(temp - forcing[3]) / (1.0 + water * water)
    for m in range(ROOT):
        value = -(demand * uptake[m])
        if m == 0:
            value = value + surface[...]
        for t in range(2):
            turned[pl.ds(t * 128 + m * ROWS, ROWS), :] = value[:, t * 128 : t * 128 + 128]
    for x in range(ROWS):
        for t in range(2):
            part = turned[pl.ds(128 * t + x, L, stride=ROWS), :]
            source[x, :, 128 * t : 128 * t + 128] = part
            if x < BHALO:
                to_prev[2 * x + t] = part
            if x >= ROWS - BHALO:
                to_next[2 * (x - ROWS + BHALO) + t] = part


def canopy_source(*arrays):
    v = vmem()[0]
    return pl.pallas_call(
        source_kernel,
        out_shape=(shaped(ROWS, ROOT, COLS), shaped(SRIM, L, 128), shaped(SRIM, L, 128)),
        in_specs=[v, v, smem(), v, v, v, v],
        out_specs=(v, v, v),
        scratch_shapes=[pltpu.VMEM((6 * ROWS, COLS), F32), pltpu.VMEM((2 * 128, 128), F32)],
        compiler_params=params(16),
        name="canopy_source",
    )(*arrays)


def owner_kernel(arrived, state, updated):
    def slot(i, carry):
        block = arrived[i]
        old = state[i]
        temp = leaf(old[1:2], block[0:1], block[1:2], block[2:3], block[4:5])
        sub = iota(old.shape, 0)
        base = jnp.where(sub == 1, temp, old)
        upper = pltpu.roll(base, 1, 0)
        lower = pltpu.roll(base, base.shape[0] - 1, 0)
        lower = jnp.where(sub == base.shape[0] - 1, base, lower)
        fresh = 0.6 * base + 0.2 * upper + 0.2 * lower
        fresh = jnp.where(sub == 1, temp, fresh)
        fresh = jnp.where(sub == 0, 0.8 * old + 0.2 * block[3:4], fresh)
        updated[i] = jnp.where(block[5:6] > 0.5, fresh, old)
        return carry

    lax.fori_loop(0, arrived.shape[0], slot, 0)


def owner_update(arrived, state):
    return pl.pallas_call(
        owner_kernel,
        out_shape=shaped(*state.shape),
        in_specs=vmem(2),
        out_specs=vmem()[0],
        compiler_params=params(8),
        name="owner_update",
    )(arrived, state)


def flat(v):
    return v.reshape(LEV, 2, 8, 2, 128).transpose(0, 1, 3, 2, 4).reshape(32 * LEV, 128)


def unflat(v):
    return v.reshape(LEV, 2, 2, 8, 128).transpose(0, 1, 3, 2, 4).reshape(LEV, ROWS, COLS)


def chunk(x, l, t):
    return pl.ds(32 * l + 16 * (x // 8) + 8 * t + x % 8, 8, stride=32 * L)


RIM = 2 * HALO * 2


def turn_kernel(
    pressure, conductivity, forcing, cover, vegetated, root_table, after,
    q, k, to_next, to_prev, edge_left, edge_right, uptake, surface,
):
    lane = iota((8, 128), 1)

    def layer(l, carry):
        for f, (field, target) in enumerate(((pressure, q), (conductivity, k))):
            first = jnp.zeros((8, 128), F32)
            last = jnp.zeros((8, 128), F32)
            for x in range(ROWS):
                for t in range(2):
                    part = field[chunk(x, l, t), :]
                    target[x, l, :, 128 * t : 128 * t + 128] = part
                    if x < HALO:
                        to_prev[2 * (f * HALO + x) + t, l] = part
                    if x >= ROWS - HALO:
                        to_next[2 * (f * HALO + x - ROWS + HALO) + t, l] = part
                    here = jnp.logical_and(lane >= 8 * x, lane < 8 * x + 8)
                    if t == 0:
                        first = jnp.where(here, lanes(part, 8 * x), first)
                    else:
                        last = jnp.where(here, lanes(part, 8 * x - 120), last)
            edge_left[f, l] = first
            edge_right[f, l] = last
        return carry

    lax.fori_loop(0, L, layer, 0)
    roots = looked_up(cover[...], root_table)
    planted = vegetated[...] == 1
    for m in range(ROOT):
        top = jnp.concatenate(
            [
                jnp.concatenate([pressure[pl.ds(32 * m + 16 * xt + 8 * t, 8), :] for t in range(2)], axis=1)
                for xt in range(2)
            ],
            axis=0,
        )
        moist = jax.nn.sigmoid(2.0 * (top + 1.5))
        uptake[m] = jnp.where(planted, roots[m] * moist, 0.0)
        if m == 0:
            evaporation = jnp.where(planted, 0.0, 0.5) * softplus(forcing[3] - forcing[2]) * moist
            surface[...] = 0.3 * softplus(forcing[4]) - evaporation


def turn(*arrays):
    own_shape = shaped(ROWS, L, 8, COLS)
    rim = shaped(RIM, L, 8, 128)
    edge = shaped(2, L, 8, 128)
    outs = (own_shape, own_shape, rim, rim, edge, edge, shaped(ROOT, ROWS, COLS), shaped(ROWS, COLS))
    return pl.pallas_call(
        turn_kernel,
        out_shape=outs,
        in_specs=vmem(5) + [smem(), pl.BlockSpec(memory_space=pl.ANY)],
        out_specs=tuple(vmem(len(outs))),
        compiler_params=params(24),
        name="turn",
    )(*arrays)


EDGE = 4 * L + 2


def edge_kernel(edge_left, edge_right, from_prev, from_next, source, source_prev, source_next, to_right, to_left):
    lane = iota((8, 128), 1)

    def packed(parts, shift):
        tile = jnp.zeros((8, 128), F32)
        for at, part in parts:
            here = jnp.logical_and(lane >= at, lane < at + 8)
            tile = jnp.where(here, lanes(part, at - shift), tile)
        return tile

    def layer(l, carry):
        for f in range(2):
            at = 2 * (8 * f + l)
            to_left[at] = edge_left[f, l]
            to_right[at] = edge_right[f, l]
            for t, target, shift in ((0, to_left, 0), (1, to_right, 120)):
                parts = []
                for i in range(HALO):
                    parts.append((8 * i, from_prev[2 * (f * HALO + i) + t, l]))
                    parts.append((64 + 8 * i, from_next[2 * (f * HALO + i) + t, l]))
                target[at + 1] = packed(parts, shift)
        return carry

    lax.fori_loop(0, L, layer, 0)
    for t, target, shift in ((0, to_left, 0), (1, to_right, 120)):
        part = pl.ds(128 * t, 128)
        target[4 * L] = packed([(8 * x, source[x, :, part]) for x in range(ROWS)], shift)
        parts = []
        for i in range(BHALO):
            parts.append((8 * i, source_prev[2 * i + t]))
            parts.append((64 + 8 * i, source_next[2 * i + t]))
        target[4 * L + 1] = packed(parts, shift)


def edges(*arrays):
    outs = (shaped(EDGE, 8, 128), shaped(EDGE, 8, 128))
    return pl.pallas_call(
        edge_kernel,
        out_shape=outs,
        in_specs=vmem(len(arrays)),
        out_specs=tuple(vmem(2)),
        compiler_params=params(16),
        name="edges",
    )(*arrays)


def halo_tile(from_left, from_right, lane, at):
    tile = jnp.where(lane < 8, lanes(from_right, -at), 0.0)
    return jnp.where(lane >= 120, lanes(from_left, 120 - at), tile)


def own(v):
    return v[:, :COLS]


def mobilities(q, k, resist, diag, rows, block):
    def step(i, carry):
        for j in range(block):
            r = rows[0] + i * block + j
            for l in range(L):
                s = 0.5 + 0.5 * jnp.tanh(q[r, l])
                m = k[r, l] * (0.1 + 0.9 * s)
                resist[r, l] = jnp.where(m > 0.0, 0.5 / m, OUTSIDE)
                diag[r, l] = 1.4 * s * (1.0 - s) + STORE
        return carry

    lax.fori_loop(0, (rows[1] - rows[0]) // block, step, 0)


def couplings(q, resist, right_hand, cx, cy, cyl, cz, diag, v0, rows, block):
    last = iota((8, XC), 0) == 7

    def row(r):
        q_0, m_0, q_7, m_7 = q[r, 0], resist[r, 0], q[r, 7], resist[r, 7]
        c_7 = jnp.where(last, 0.0, 1.0 / (m_7 + deeper(m_0)))
        f_7 = c_7 * (q_7 - deeper(q_0) + GRAV)
        cz[r, 7] = c_7
        c_up, f_up = higher(c_7), higher(f_7)
        v, m = q_0, m_0
        for l in range(L):
            if l < L - 1:
                m_n, v_n = resist[r, l + 1], q[r, l + 1]
                c = 1.0 / (m + m_n)
                f = c * (v - v_n + GRAV)
                cz[r, l] = c
            else:
                c, f = c_7, f_7
            y = 1.0 / (m + right(m))
            yl = 1.0 / (m + left(m))
            x = 1.0 / (m + resist[r + 1, l])
            xp = cx[r - 1, l]
            cy[r, l] = y
            cyl[r, l] = yl
            cx[r, l] = x
            out = y * (v - right(v)) + yl * (v - left(v))
            out = out + (x * (v - q[r + 1, l]) + xp * (v - q[r - 1, l])) + (f - f_up)
            diag[r, l] = diag[r, l] + ((y + yl) + (x + xp) + (c + c_up))
            v0[r, l] = right_hand(r, l, v) - out
            c_up, f_up = c, f
            if l < L - 1:
                v, m = v_n, m_n

    def step(i, carry):
        for j in range(block):
            row(rows[0] + i * block + j)
        return carry

    for l in range(L):
        cx[rows[0] - 1, l] = 1.0 / (resist[rows[0] - 1, l] + resist[rows[0], l])
    lax.fori_loop(0, (rows[1] - rows[0]) // block, step, 0)


def apply(v_in, v_out, cx, cy, cyl, cz, diag, rows, block, first):
    zero = jnp.zeros((8, COLS), F32)

    def row(r, held):
        c_up, v_up = higher(cz[r, 7]), higher(v_in[r, 7])
        v_0 = v_in[r, 0]
        v = v_0
        here = jnp.logical_and(r >= HALO, r < HALO + ROWS)
        square, cross = zero, zero
        for l in range(L):
            v_n = v_in[r, l + 1] if l < L - 1 else deeper(v_0)
            c = cz[r, l]
            image = diag[r, l] * v - cy[r, l] * right(v) - cyl[r, l] * left(v)
            image = image - cx[r, l] * v_in[r + 1, l] - cx[r - 1, l] * v_in[r - 1, l]
            image = image - c * v_n - c_up * v_up
            if v_out is not None:
                v_out[r, l] = image
            a, b = own(v), own(image)
            square = square + a * a
            cross = cross + a * b
            v_up, c_up, v = v, c, v_n
        if not first:
            square = jnp.where(here, square, 0.0)
            cross = jnp.where(here, cross, 0.0)
        return held[0] + square, held[1] + cross

    def step(i, held):
        for j in range(block):
            held = row(rows[0] + i * block + j, held)
        return held

    return lax.fori_loop(0, (rows[1] - rows[0]) // block, step, (zero, zero))


def chain(cx, cy, cyl, cz, diag, v0, v1, v2, moments, spans, blocks):
    coefs = (cx, cy, cyl, cz, diag)
    sums = []
    sums += apply(v0, v1, *coefs, spans[0], blocks[0], False)
    sums += apply(v1, v2, *coefs, spans[1], blocks[1], False)
    sums += apply(v2, None, *coefs, spans[2], blocks[2], True)
    row = jnp.zeros((1, 128), F32)
    lane = iota((1, 128), 1)
    for k, held in enumerate(sums):
        value = jnp.sum(jnp.sum(held, axis=0, keepdims=True), axis=1, keepdims=True)
        row = jnp.where(lane == k, value, row)
    moments[...] = jnp.broadcast_to(row, moments.shape)


def coefficients(gathered):
    row = jnp.sum(gathered[...], axis=0, keepdims=True)
    lane = iota((1, 128), 1)
    m = [jnp.sum(jnp.where(lane == k, row, 0.0), axis=1, keepdims=True) for k in range(6)]

    def dot(a, b, shift):
        total = jnp.zeros((1, 1), F32)
        for i, p in enumerate(a):
            for j, q in enumerate(b):
                total = total + p * q * m[i + j + shift]
        return total

    one = jnp.ones((1, 1), F32)
    a0 = m[0] / m[1]
    r1 = [one, -a0]
    n1 = dot(r1, r1, 0)
    b0 = n1 / m[0]
    p1 = [one + b0, -a0]
    a1 = n1 / dot(p1, p1, 1)
    r2 = [one, -a0 - a1 * p1[0], -a1 * p1[1]]
    n2 = dot(r2, r2, 0)
    b1 = n2 / n1
    p2 = [r2[0] + b1 * p1[0], r2[1] + b1 * p1[1], r2[2]]
    a2 = n2 / dot(p2, p2, 1)
    return (
        a0 + a1 * p1[0] + a2 * p2[0],
        a1 * p1[1] + a2 * p2[1],
        a2 * p2[2],
    )


def source_at(b, r, l, sub):
    return jnp.where(sub == 0, pltpu.roll(b[r], (8 - l) % 8, 0), 0.0)


def first_kernel(
    q_own, k_own, from_prev, from_next, source, source_prev, source_next, from_left, from_right,
    q, k, b, v0, v1, v2, moments,
    resist, cx, cy, cyl, cz, diag,
):
    lane = iota((8, 128), 1)

    def fill(l, carry):
        for f, (field, target) in enumerate(((q_own, q), (k_own, k))):
            at = 2 * (8 * f + l)
            a, c = from_left[at], from_right[at]
            for x in range(ROWS):
                target[HALO + x, l, :, :COLS] = field[x, l]
                target[HALO + x, l, :, COLS:] = halo_tile(a, c, lane, 8 * x)
            a, c = from_left[at + 1], from_right[at + 1]
            for i in range(HALO):
                for side, r, spot in ((from_prev, i, 8 * i), (from_next, HALO + ROWS + i, 64 + 8 * i)):
                    for t in range(2):
                        target[r, l, :, 128 * t : 128 * t + 128] = side[2 * (f * HALO + i) + t, l]
                    target[r, l, :, COLS:] = halo_tile(a, c, lane, spot)
        return carry

    lax.fori_loop(0, L, fill, 0)

    a, c = from_left[4 * L], from_right[4 * L]
    for x in range(ROWS):
        b[HALO + x, :, :COLS] = source[x]
        b[HALO + x, :, COLS:] = halo_tile(a, c, lane, 8 * x)
    a, c = from_left[4 * L + 1], from_right[4 * L + 1]
    for i in range(BHALO):
        for side, r, spot in (
            (source_prev, HALO - BHALO + i, 8 * i),
            (source_next, HALO + ROWS + i, 64 + 8 * i),
        ):
            for t in range(2):
                b[r, :, 128 * t : 128 * t + 128] = side[2 * i + t]
            b[r, :, COLS:] = halo_tile(a, c, lane, spot)

    sub = iota((8, XC), 0)

    def right_hand(r, l, v):
        return source_at(b, r, l, sub)

    mobilities(q, k, resist, diag, (0, XR), 2)
    couplings(q, resist, right_hand, cx, cy, cyl, cz, diag, v0, (1, XR - 1), 4)
    chain(
        cx, cy, cyl, cz, diag, v0, v1, v2, moments,
        ((2, XR - 2), (3, XR - 3), (HALO, HALO + ROWS)), (13, 8, 8),
    )


def wide():
    return shaped(XR, L, 8, XC)


def scratch(n):
    return [pltpu.VMEM((XR, L, 8, XC), F32)] * n


def first_newton(*arrays):
    w = wide()
    outs = (w, w, shaped(XR, L, XC), w, w, w, shaped(128, 128))
    return pl.pallas_call(
        first_kernel,
        out_shape=outs,
        in_specs=vmem(len(arrays)),
        out_specs=tuple(vmem(len(outs))),
        scratch_shapes=scratch(6),
        compiler_params=params(22),
        name="first_newton",
    )(*arrays)


def second_kernel(
    q, k, b, u0, u1, u2, gathered,
    q_own, w0, w1, w2, moments,
    q1, resist, cx, cy, cyl, cz, diag, v0, v2,
):
    v1 = resist
    c0, c1, c2 = coefficients(gathered)

    def update(r, carry):
        for l in range(L):
            q1[r, l] = q[r, l] + c0 * u0[r, l] + c1 * u1[r, l] + c2 * u2[r, l]
        return carry

    lax.fori_loop(3, XR - 3, update, 0, unroll=2)
    sub = iota((8, XC), 0)

    def right_hand(r, l, v):
        before = q[r, l]
        stored = 0.35 * (jnp.tanh(v) - jnp.tanh(before)) + STORE * (v - before)
        return source_at(b, r, l, sub) - stored

    mobilities(q1, k, resist, diag, (3, XR - 3), 2)
    couplings(q1, resist, right_hand, cx, cy, cyl, cz, diag, v0, (4, XR - 4), 2)
    chain(
        cx, cy, cyl, cz, diag, v0, v1, v2, moments,
        ((5, XR - 5), (6, XR - 6), (HALO, HALO + ROWS)), (10, 9, 8),
    )

    def keep(x, carry):
        for l in range(L):
            for source, target in ((q1, q_own), (v0, w0), (v1, w1), (v2, w2)):
                target[x, l] = source[HALO + x, l, :, :COLS]
        return carry

    lax.fori_loop(0, ROWS, keep, 0)


def second_newton(*arrays):
    o = shaped(ROWS, L, 8, COLS)
    outs = (o, o, o, o, shaped(128, 128))
    return pl.pallas_call(
        second_kernel,
        out_shape=outs,
        in_specs=vmem(len(arrays)),
        out_specs=tuple(vmem(len(outs))),
        scratch_shapes=scratch(9),
        compiler_params=params(28),
        name="second_newton",
    )(*arrays)


def final_kernel(q, v0, v1, v2, gathered, out):
    c0, c1, c2 = coefficients(gathered)

    def row(x, carry):
        for l in range(L):
            value = q[x, l] + c0 * v0[x, l] + c1 * v1[x, l] + c2 * v2[x, l]
            out[chunk(x, l, 0), :] = value[:, :128]
            out[chunk(x, l, 1), :] = value[:, 128:]
        return carry

    lax.fori_loop(0, ROWS, row, 0)


def final_update(*arrays):
    return pl.pallas_call(
        final_kernel,
        out_shape=shaped(32 * LEV, 128),
        in_specs=vmem(len(arrays)),
        out_specs=vmem()[0],
        compiler_params=params(16),
        name="final_update",
    )(*arrays)


def exchange(to_high, to_low, axis):
    count = lax.axis_size(axis)
    up = [(i, i + 1) for i in range(count - 1)]
    down = [(i + 1, i) for i in range(count - 1)]
    return lax.ppermute(to_high, axis, up), lax.ppermute(to_low, axis, down)


def share(moments):
    return lax.all_to_all(moments, ("gx", "gy"), split_axis=0, concat_axis=0, tiled=True)


def body(
    pressure_old,
    conductivity,
    forcing,
    vegetated,
    cover_type,
    canopy_table,
    root_table,
    pair_counts,
    send_cols,
    canopy_state,
):
    owners = send_cols.shape[1]
    cols = in_hbm(send_cols.reshape(owners, 1, COLS))
    counts = in_hbm(pair_counts.reshape(owners))
    state = in_hbm(canopy_state.reshape(owners, 16, COLS))
    forcing, cover_type, vegetated = in_hbm(forcing), in_hbm(cover_type), in_hbm(vegetated)
    old, conductivity = in_hbm(flat(pressure_old)), in_hbm(flat(conductivity))
    canopy_table, root_table = in_hbm(canopy_table.T), in_hbm(root_table.T)

    payload, conductance = canopy_send(forcing, cover_type, canopy_table, counts, cols, state)
    arrived = lax.all_to_all(payload, "gx", split_axis=0, concat_axis=0, tiled=True)
    q_own, k_own, to_next, to_prev, edge_left, edge_right, uptake, surface = turn(
        old, conductivity, forcing, cover_type, vegetated, root_table, payload
    )
    to_next, to_prev, arrived = lax.optimization_barrier((to_next, to_prev, arrived))
    from_prev, from_next = exchange(to_next, to_prev, "gx")
    source, to_next, to_prev = canopy_source(
        arrived, cols, counts, forcing, conductance, uptake, surface
    )
    source_prev, source_next = exchange(to_next, to_prev, "gx")
    to_right, to_left = edges(
        edge_left, edge_right, from_prev, from_next, source, source_prev, source_next
    )
    from_left, from_right = exchange(to_right, to_left, "gy")
    new_state = owner_update(arrived, state).reshape(canopy_state.shape)

    q, k, b, v0, v1, v2, moments = first_newton(
        q_own, k_own, from_prev, from_next, source, source_prev, source_next, from_left, from_right
    )
    q1, w0, w1, w2, moments = second_newton(q, k, b, v0, v1, v2, share(moments))
    pressure = unflat(final_update(q1, w0, w1, w2, share(moments)))
    return pressure, new_state


def solution(mesh):
    placed = (
        P(None, "gx", "gy"),
        P(None, "gx", "gy"),
        P(None, "gx", "gy"),
        P("gx", "gy"),
        P("gx", "gy"),
        P(),
        P(),
        P("gx", None, "gy"),
        P("gx", None, "gy", None),
        P("gx", None, "gy", None, None),
    )
    return jax.shard_map(
        body,
        mesh=mesh,
        in_specs=placed,
        out_specs=(P(None, "gx", "gy"), P("gx", None, "gy", None, None)),
        check_vma=False,
    )
```

```python
import jax
import jax.numpy as jnp
from jax import lax
from jax.experimental import pallas as pl
from jax.experimental.pallas import tpu as pltpu
from jax.sharding import PartitionSpec as P

FORC = 8
ROOT = 8
LEV = 64
ROWS = 16
COLS = 256
L = 8
HALO = 7
XR = ROWS + 2 * HALO
XC = 384
OUTSIDE = 1e37
BHALO = 6
SIDE = 2 * L + 1
CORNER = 2 * BHALO + SIDE
STORE = 0.05
GRAV = 0.5
F32 = jnp.float32
BF16 = jnp.bfloat16


def vmem(n=1):
    return [pl.BlockSpec(memory_space=pltpu.VMEM)] * n


def params(mib):
    return pltpu.CompilerParams(vmem_limit_bytes=mib * 1024 * 1024)


def shaped(*shape):
    return jax.ShapeDtypeStruct(shape, F32)


def iota(shape, dim):
    return lax.broadcasted_iota(jnp.int32, shape, dim)


def right(v):
    return pltpu.roll(v, v.shape[1] - 1, 1)


def left(v):
    return pltpu.roll(v, 1, 1)


def deeper(v):
    return pltpu.roll(v, v.shape[0] - 1, 0)


def higher(v):
    return pltpu.roll(v, 1, 0)


def lanes(v, shift):
    return v if shift % 128 == 0 else pltpu.roll(v, shift % 128, v.ndim - 1)


def pieces(v):
    high = v.astype(BF16)
    rest = v - high.astype(F32)
    mid = rest.astype(BF16)
    low = (rest - mid.astype(F32)).astype(BF16)
    return high, mid, low


def in_hbm(v):
    return pltpu.with_memory_space_constraint(v, pltpu.HBM)


def smem():
    return pl.BlockSpec(memory_space=pltpu.SMEM)


def looked_up(kinds, table):
    found = [jnp.zeros(kinds.shape, F32) for _ in range(table.shape[0])]
    for kind in range(table.shape[1]):
        hit = kinds == kind
        for m in range(table.shape[0]):
            found[m] = jnp.where(hit, table[m, kind], found[m])
    return found


def hits(index):
    row = lax.shift_right_logical(index, 8)
    col = jnp.bitwise_and(index, COLS - 1)
    row_hit = iota((ROWS, COLS), 0) == row
    col_hit = iota((COLS, COLS), 0) == col
    return row_hit, jnp.where(col_hit, 1.0, 0.0).astype(BF16)


def canopy_send_kernel(
    forcing, cover, canopy_table, counts, cols, state, payload, conductance, split
):
    weights = looked_up(cover[...], canopy_table)
    total = weights[0] * forcing[0]
    for m in range(1, FORC):
        total = total + weights[m] * forcing[m]
    g = 2.0 * jax.nn.sigmoid(total)
    conductance[...] = g
    channels = [forcing[0], forcing[1], forcing[2], jnp.tanh(forcing[4]), g]
    used = len(channels)
    for c, channel in enumerate(channels):
        for p, piece in enumerate(pieces(channel)):
            split[pl.ds((p * used + c) * ROWS, ROWS), :] = piece

    def owner(o, carry):
        row_hit, onehot = hits(cols[o])
        picked = jnp.dot(split[...], onehot, preferred_element_type=F32)
        span = used * ROWS
        picked = picked[:span] + picked[span : 2 * span] + picked[2 * span :]
        sub = iota((8, COLS), 0)
        out = pltpu.roll(state[o, 0:8, :], 6, 0)
        for c in range(used):
            chosen = jnp.where(row_hit, picked[c * ROWS : (c + 1) * ROWS], 0.0)
            chosen = jnp.sum(chosen, axis=0, keepdims=True)
            out = jnp.where(sub == c, chosen, out)
        live = jnp.where(iota((8, COLS), 1) < counts[o], 1.0, 0.0)
        payload[o] = jnp.where(sub == used, live, out)
        return carry

    lax.fori_loop(0, cols.shape[0], owner, 0, unroll=4)


def canopy_send(forcing, cover, canopy_table, counts, cols, state):
    owners = cols.shape[0]
    return pl.pallas_call(
        canopy_send_kernel,
        out_shape=(shaped(owners, 8, COLS), shaped(ROWS, COLS)),
        in_specs=vmem(2) + [smem(), smem()] + vmem(2),
        out_specs=tuple(vmem(2)),
        scratch_shapes=[pltpu.VMEM((15 * ROWS, COLS), BF16)],
        compiler_params=params(16),
        name="canopy_send",
    )(forcing, cover, canopy_table, counts, cols, state)


def softplus(v):
    return jnp.maximum(v, 0.0) + jnp.log1p(jnp.exp(-jnp.abs(v)))


def leaf(start, f0, f1, f2, g):
    temp = start
    for _ in range(3):
        temp = 0.5 * (start + f0) + 0.5 * jnp.tanh(f1 - g * (temp - f2))
    return temp


def source_kernel(
    arrived, cols, counts, forcing, conductance, uptake, surface, edge_left, edge_right,
    source, to_right, to_left, total, turned,
):
    total[...] = jnp.zeros_like(total)

    def owner(o, carry):
        row_hit, onehot = hits(cols[o])
        wanted = jnp.logical_and(row_hit, iota((ROWS, COLS), 1) < counts[o])
        block = arrived[o]
        parts = []
        for c in (6, 7):
            value = jnp.where(wanted, block[c : c + 1, :], 0.0)
            parts.extend(pieces(value))
        stacked = jnp.concatenate(parts, axis=0)
        total[...] += lax.dot_general(
            stacked, onehot, (((1,), (1,)), ((), ())), preferred_element_type=F32
        )
        return carry

    lax.fori_loop(0, cols.shape[0], owner, 0, unroll=4)

    def piece(k):
        return total[k * ROWS : (k + 1) * ROWS, :]

    water = piece(0) + piece(1) + piece(2)
    start = piece(3) + piece(4) + piece(5)
    g = conductance[...]
    temp = leaf(start, forcing[0], forcing[1], forcing[2], g)
    demand = g * softplus(temp - forcing[3]) / (1.0 + water * water)
    for m in range(ROOT):
        value = -(demand * uptake[m])
        if m == 0:
            value = value + surface[...]
        for t in range(2):
            turned[pl.ds(t * 128 + m * ROWS, ROWS), :] = value[:, t * 128 : t * 128 + 128]
    lane = iota((L, 128), 1)
    first = jnp.zeros((L, 128), F32)
    last = jnp.zeros((L, 128), F32)
    for x in range(ROWS):
        low = turned[pl.ds(x, L, stride=ROWS), :]
        high = turned[pl.ds(128 + x, L, stride=ROWS), :]
        source[x, :, :128] = low
        source[x, :, 128:] = high
        here = jnp.logical_and(lane >= 8 * x, lane < 8 * x + 8)
        first = jnp.where(here, lanes(low, 8 * x), first)
        last = jnp.where(here, lanes(high, 8 * x - 120), last)
    for target, edge, own_edge in ((to_left, edge_left, first), (to_right, edge_right, last)):
        target[0 : 2 * L] = edge[...]
        target[2 * L] = own_edge


def canopy_source(*arrays):
    v = vmem()[0]
    return pl.pallas_call(
        source_kernel,
        out_shape=(shaped(ROWS, ROOT, COLS), shaped(SIDE, L, 128), shaped(SIDE, L, 128)),
        in_specs=[v, v, smem(), v, v, v, v, v, v],
        out_specs=(v, v, v),
        scratch_shapes=[pltpu.VMEM((6 * ROWS, COLS), F32), pltpu.VMEM((2 * 128, 128), F32)],
        compiler_params=params(16),
        name="canopy_source",
    )(*arrays)


def owner_kernel(arrived, state, updated):
    def slot(i, carry):
        block = arrived[i]
        old = state[i]
        temp = leaf(old[1:2], block[0:1], block[1:2], block[2:3], block[4:5])
        sub = iota(old.shape, 0)
        base = jnp.where(sub == 1, temp, old)
        upper = pltpu.roll(base, 1, 0)
        lower = pltpu.roll(base, base.shape[0] - 1, 0)
        lower = jnp.where(sub == base.shape[0] - 1, base, lower)
        fresh = 0.6 * base + 0.2 * upper + 0.2 * lower
        fresh = jnp.where(sub == 1, temp, fresh)
        fresh = jnp.where(sub == 0, 0.8 * old + 0.2 * block[3:4], fresh)
        updated[i] = jnp.where(block[5:6] > 0.5, fresh, old)
        return carry

    lax.fori_loop(0, arrived.shape[0], slot, 0)


def owner_update(arrived, state):
    return pl.pallas_call(
        owner_kernel,
        out_shape=shaped(*state.shape),
        in_specs=vmem(2),
        out_specs=vmem()[0],
        compiler_params=params(8),
        name="owner_update",
    )(arrived, state)


def flat(v):
    return v.reshape(LEV, 2, 8, 2, 128).transpose(0, 1, 3, 2, 4).reshape(32 * LEV, 128)


def unflat(v):
    return v.reshape(LEV, 2, 2, 8, 128).transpose(0, 1, 3, 2, 4).reshape(LEV, ROWS, COLS)


def chunk(x, l, t):
    return pl.ds(32 * l + 16 * (x // 8) + 8 * t + x % 8, 8, stride=32 * L)


RIM = 2 * HALO * 2


def turn_kernel(
    pressure, conductivity, forcing, cover, vegetated, root_table, after,
    q, k, to_next, to_prev, edge_left, edge_right, uptake, surface,
):
    lane = iota((8, 128), 1)

    def layer(l, carry):
        for f, (field, target) in enumerate(((pressure, q), (conductivity, k))):
            first = jnp.zeros((8, 128), F32)
            last = jnp.zeros((8, 128), F32)
            for x in range(ROWS):
                for t in range(2):
                    part = field[chunk(x, l, t), :]
                    target[x, l, :, 128 * t : 128 * t + 128] = part
                    if x < HALO:
                        to_prev[2 * (f * HALO + x) + t, l] = part
                    if x >= ROWS - HALO:
                        to_next[2 * (f * HALO + x - ROWS + HALO) + t, l] = part
                    here = jnp.logical_and(lane >= 8 * x, lane < 8 * x + 8)
                    if t == 0:
                        first = jnp.where(here, lanes(part, 8 * x), first)
                    else:
                        last = jnp.where(here, lanes(part, 8 * x - 120), last)
            edge_left[f * L + l] = first
            edge_right[f * L + l] = last
        return carry

    lax.fori_loop(0, L, layer, 0)
    roots = looked_up(cover[...], root_table)
    planted = vegetated[...] == 1
    for m in range(ROOT):
        top = jnp.concatenate(
            [
                jnp.concatenate([pressure[pl.ds(32 * m + 16 * xt + 8 * t, 8), :] for t in range(2)], axis=1)
                for xt in range(2)
            ],
            axis=0,
        )
        moist = jax.nn.sigmoid(2.0 * (top + 1.5))
        uptake[m] = jnp.where(planted, roots[m] * moist, 0.0)
        if m == 0:
            evaporation = jnp.where(planted, 0.0, 0.5) * softplus(forcing[3] - forcing[2]) * moist
            surface[...] = 0.3 * softplus(forcing[4]) - evaporation


def turn(*arrays):
    own_shape = shaped(ROWS, L, 8, COLS)
    rim = shaped(RIM, L, 8, 128)
    edge = shaped(2 * L, 8, 128)
    outs = (own_shape, own_shape, rim, rim, edge, edge, shaped(ROOT, ROWS, COLS), shaped(ROWS, COLS))
    return pl.pallas_call(
        turn_kernel,
        out_shape=outs,
        in_specs=vmem(5) + [smem(), pl.BlockSpec(memory_space=pl.ANY)],
        out_specs=tuple(vmem(len(outs))),
        compiler_params=params(24),
        name="turn",
    )(*arrays)


def corner_kernel(source, from_left, from_right, after, to_next, to_prev):
    low = iota((8, 128), 1) < 64
    for i in range(BHALO):
        for t in range(2):
            part = pl.ds(128 * t, 128)
            to_next[2 * i + t] = source[ROWS - BHALO + i, :, part]
            to_prev[2 * i + t] = source[i, :, part]
    for j in range(SIDE):
        a, b = from_left[j], from_right[j]
        to_next[2 * BHALO + j] = jnp.where(low, lanes(a, 64), b)
        to_prev[2 * BHALO + j] = jnp.where(low, a, lanes(b, 64))


def corners(*arrays):
    outs = (shaped(CORNER, 8, 128), shaped(CORNER, 8, 128))
    return pl.pallas_call(
        corner_kernel,
        out_shape=outs,
        in_specs=vmem(3) + [pl.BlockSpec(memory_space=pl.ANY)],
        out_specs=tuple(vmem(2)),
        compiler_params=params(16),
        name="corners",
    )(*arrays)


def halo_tile(from_left, from_right, lane, at_left, at_right):
    tile = jnp.where(lane < 8, lanes(from_right, -at_right), 0.0)
    return jnp.where(lane >= 120, lanes(from_left, 120 - at_left), tile)


def own(v):
    return v[:, :COLS]


def local_terms(q, k):
    bend = jnp.tanh(q)
    s = 0.5 + 0.5 * bend
    m = k * (0.1 + 0.9 * s)
    return bend, jnp.where(m > 0.0, 0.5 / m, OUTSIDE), 1.4 * s * (1.0 - s) + STORE


def blocks(rows, block, row, carry=None):
    def step(i, held):
        for j in range(block):
            held = row(rows[0] + i * block + j, held)
        return held

    return lax.fori_loop(0, (rows[1] - rows[0]) // block, step, carry)


def couplings(q, resist, cx, cy, cyl, cz, diag, rows, block, emit):
    last = iota((8, XC), 0) == 7

    def row(r, carry):
        q_0, m_0, q_7, m_7 = q[r, 0], resist[r, 0], q[r, 7], resist[r, 7]
        c_7 = jnp.where(last, 0.0, 1.0 / (m_7 + deeper(m_0)))
        f_7 = c_7 * (q_7 - deeper(q_0) + GRAV)
        cz[r, 7] = c_7
        c_up, f_up = higher(c_7), higher(f_7)
        v, m = q_0, m_0
        for l in range(L):
            if l < L - 1:
                m_n, v_n = resist[r, l + 1], q[r, l + 1]
                c = 1.0 / (m + m_n)
                f = c * (v - v_n + GRAV)
                cz[r, l] = c
            else:
                c, f = c_7, f_7
            y = 1.0 / (m + right(m))
            yl = 1.0 / (m + left(m))
            x = 1.0 / (m + resist[r + 1, l])
            xp = cx[r - 1, l]
            cy[r, l] = y
            cyl[r, l] = yl
            cx[r, l] = x
            out = y * (v - right(v)) + yl * (v - left(v))
            out = out + (x * (v - q[r + 1, l]) + xp * (v - q[r - 1, l])) + (f - f_up)
            diag[r, l] = diag[r, l] + ((y + yl) + (x + xp) + (c + c_up))
            emit(r, l, out)
            c_up, f_up = c, f
            if l < L - 1:
                v, m = v_n, m_n
        return carry

    for l in range(L):
        cx[rows[0] - 1, l] = 1.0 / (resist[rows[0] - 1, l] + resist[rows[0], l])
    blocks(rows, block, row, 0)


def apply(v_in, v_out, coefs, shift, rows, block, held, counted):
    cx, cy, cyl, cz, diag = coefs

    def row(r, held):
        at = r - shift
        c_up, v_up = higher(cz[at, 7]), higher(v_in[r, 7])
        v_0 = v_in[r, 0]
        v = v_0
        square, cross = held
        for l in range(L):
            v_n = v_in[r, l + 1] if l < L - 1 else deeper(v_0)
            c = cz[at, l]
            image = diag[at, l] * v - cy[at, l] * right(v) - cyl[at, l] * left(v)
            image = image - cx[at, l] * v_in[r + 1, l] - cx[at - 1, l] * v_in[r - 1, l]
            image = image - c * v_n - c_up * v_up
            if v_out is not None:
                v_out[r, l] = image
            if counted:
                a, b = own(v), own(image)
                square = square + a * a
                cross = cross + a * b
            v_up, c_up, v = v, c, v_n
        return square, cross

    return blocks(rows, block, row, held)


def write_moments(sums, moments):
    row = jnp.zeros((1, 128), F32)
    lane = iota((1, 128), 1)
    for k, held in enumerate(sums):
        value = jnp.sum(jnp.sum(held, axis=0, keepdims=True), axis=1, keepdims=True)
        row = jnp.where(lane == k, value, row)
    moments[...] = jnp.broadcast_to(row, moments.shape)


def no_sums():
    zero = jnp.zeros((8, COLS), F32)
    return zero, zero


def coefficients(gathered):
    row = jnp.sum(gathered[...], axis=0, keepdims=True)
    lane = iota((1, 128), 1)
    m = [jnp.sum(jnp.where(lane == k, row, 0.0), axis=1, keepdims=True) for k in range(6)]

    def dot(a, b, shift):
        total = jnp.zeros((1, 1), F32)
        for i, p in enumerate(a):
            for j, q in enumerate(b):
                total = total + p * q * m[i + j + shift]
        return total

    one = jnp.ones((1, 1), F32)
    a0 = m[0] / m[1]
    r1 = [one, -a0]
    n1 = dot(r1, r1, 0)
    b0 = n1 / m[0]
    p1 = [one + b0, -a0]
    a1 = n1 / dot(p1, p1, 1)
    r2 = [one, -a0 - a1 * p1[0], -a1 * p1[1]]
    n2 = dot(r2, r2, 0)
    b1 = n2 / n1
    p2 = [r2[0] + b1 * p1[0], r2[1] + b1 * p1[1], r2[2]]
    a2 = n2 / dot(p2, p2, 1)
    return (
        a0 + a1 * p1[0] + a2 * p2[0],
        a1 * p1[1] + a2 * p2[1],
        a2 * p2[2],
    )


def source_at(b, r, l, sub):
    return jnp.where(sub == 0, pltpu.roll(b[r], (8 - l) % 8, 0), 0.0)


def prepare_kernel(
    q_own, k_own, from_left, from_right,
    q, k, resist, cx, cy, cyl, cz, diag, base,
):
    lane = iota((8, 128), 1)

    def fill(l, carry):
        for f, (field, target) in enumerate(((q_own, q), (k_own, k))):
            a, c = from_left[f * L + l], from_right[f * L + l]
            for x in range(ROWS):
                target[x, l, :, :COLS] = field[x, l]
                target[x, l, :, COLS:] = halo_tile(a, c, lane, 8 * x, 8 * x)
        for x in range(ROWS):
            _, resist[x, l], diag[x, l] = local_terms(q[x, l], k[x, l])
        return carry

    lax.fori_loop(0, L, fill, 0)

    def emit(r, l, out):
        base[r, l] = -out

    couplings(q, resist, cx, cy, cyl, cz, diag, (1, ROWS - 1), 2, emit)


def prepare(*arrays):
    outs = (shaped(ROWS, L, 8, XC),) * 9
    return pl.pallas_call(
        prepare_kernel,
        out_shape=outs,
        in_specs=vmem(4),
        out_specs=tuple(vmem(9)),
        compiler_params=params(4),
        name="prepare",
    )(*arrays)


RSHIFT = 12
RROWS = 18


def first_kernel(
    q_mid, k_mid, resist_mid, cx_mid, cy_mid, cyl_mid, cz_mid, diag_mid, base,
    from_prev, from_next, source, corner_prev, corner_next, from_left, from_right,
    q, k, b, v0, v1, v2, moments,
    resist, cx, cy, cyl, cz, diag,
):
    lane = iota((8, 128), 1)

    def fill(l, carry):
        for f, target in enumerate((q, k)):
            at = 2 * BHALO + f * L + l
            for side, corner, r, spot in (
                (from_prev, corner_prev, 0, 8 * (8 - HALO)),
                (from_next, corner_next, HALO + ROWS - RSHIFT, 0),
            ):
                tile = corner[at]
                for i in range(HALO):
                    for t in range(2):
                        target[r + i, l, :, 128 * t : 128 * t + 128] = side[2 * (f * HALO + i) + t, l]
                    left_at = spot + 8 * i
                    target[r + i, l, :, COLS:] = halo_tile(tile, tile, lane, left_at, 64 + left_at)
        for r in (*range(HALO), *range(RROWS - HALO, RROWS)):
            _, resist[r, l], diag[r, l] = local_terms(q[r, l], k[r, l])
        for r, x in ((7, 0), (8, 1), (9, ROWS - 2), (10, ROWS - 1)):
            q[r, l] = q_mid[x, l]
            resist[r, l] = resist_mid[x, l]
            diag[r, l] = diag_mid[x, l]
        return carry

    lax.fori_loop(0, L, fill, 0)

    a, c = from_left[2 * L], from_right[2 * L]
    for x in range(ROWS):
        b[HALO + x, :, :COLS] = source[x]
        b[HALO + x, :, COLS:] = halo_tile(a, c, lane, 8 * x, 8 * x)
    for side, r, spot in (
        (corner_prev, HALO - BHALO, 8 * (8 - BHALO)),
        (corner_next, HALO + ROWS, 0),
    ):
        tile = side[CORNER - 1]
        for i in range(BHALO):
            for t in range(2):
                b[r + i, :, 128 * t : 128 * t + 128] = side[2 * i + t]
            left_at = spot + 8 * i
            b[r + i, :, COLS:] = halo_tile(tile, tile, lane, left_at, 64 + left_at)

    sub = iota((8, XC), 0)
    coefs = (cx, cy, cyl, cz, diag)
    mids = (cx_mid, cy_mid, cyl_mid, cz_mid, diag_mid)

    for shift, rows in ((0, (1, HALO + 1)), (RSHIFT, (RROWS - HALO - 1, RROWS - 1))):

        def emit(r, l, out, shift=shift):
            v0[r + shift, l] = source_at(b, r + shift, l, sub) - out

        couplings(q, resist, *coefs, rows, 1, emit)

    def inner(r, carry):
        for l in range(L):
            v0[r, l] = source_at(b, r, l, sub) + base[r - HALO, l]
        return carry

    low, high = HALO, HALO + ROWS - 1
    blocks((low + 1, high), 2, inner, 0)

    sums = []
    for v_in, v_out, deep in ((v0, v1, 5), (v1, v2, 4), (v2, None, 0)):
        held = apply(v_in, v_out, mids, HALO, (low + 1, high), 7, no_sums(), True)
        held = apply(v_in, v_out, coefs, 0, (low, low + 1), 1, held, True)
        held = apply(v_in, v_out, coefs, RSHIFT, (high, high + 1), 1, held, True)
        if deep:
            apply(v_in, v_out, coefs, 0, (low - deep, low), deep, no_sums(), False)
            apply(v_in, v_out, coefs, RSHIFT, (high + 1, high + 1 + deep), deep, no_sums(), False)
        sums += held
    write_moments(sums, moments)


def first_newton(*arrays):
    w = shaped(XR, L, 8, XC)
    rim = shaped(RROWS, L, 8, XC)
    outs = (rim, rim, shaped(XR, L, XC), w, w, w, shaped(128, 128))
    return pl.pallas_call(
        first_kernel,
        out_shape=outs,
        in_specs=vmem(len(arrays)),
        out_specs=tuple(vmem(len(outs))),
        scratch_shapes=[pltpu.VMEM((RROWS, L, 8, XC), F32)] * 6,
        compiler_params=params(14),
        name="first_newton",
    )(*arrays)


def second_kernel(
    q_mid, k_mid, q_rim, k_rim, b, u0, u1, u2, gathered,
    q_own, w0, w1, w2, moments,
    q1, resist, cx, cy, cyl, cz, diag, v0, v2,
):
    v1 = resist
    c0, c1, c2 = coefficients(gathered)
    sub = iota((8, XC), 0)

    for q, k, shift, rows in (
        (q_rim, k_rim, 0, (3, HALO)),
        (q_mid, k_mid, HALO, (HALO, HALO + ROWS)),
        (q_rim, k_rim, RSHIFT, (HALO + ROWS, XR - 3)),
    ):

        def update(r, carry, q=q, k=k, shift=shift):
            for l in range(L):
                old = q[r - shift, l]
                step = c0 * u0[r, l] + c1 * u1[r, l] + c2 * u2[r, l]
                new = old + step
                q1[r, l] = new
                bend, resist[r, l], diag[r, l] = local_terms(new, k[r - shift, l])
                stored = 0.35 * (bend - jnp.tanh(old)) + STORE * step
                v0[r, l] = source_at(b, r, l, sub) - stored
            return carry

        blocks(rows, 2, update, 0)

    def emit(r, l, out):
        v0[r, l] = v0[r, l] - out

    coefs = (cx, cy, cyl, cz, diag)
    couplings(q1, resist, *coefs, (4, XR - 4), 2, emit)
    low, high = HALO, HALO + ROWS
    sums = []
    for v_in, v_out, deep in ((v0, v1, 2), (v1, v2, 1), (v2, None, 0)):
        sums += apply(v_in, v_out, coefs, 0, (low, high), 8, no_sums(), True)
        if deep:
            apply(v_in, v_out, coefs, 0, (low - deep, low), deep, no_sums(), False)
            apply(v_in, v_out, coefs, 0, (high, high + deep), deep, no_sums(), False)
    write_moments(sums, moments)

    def keep(x, carry):
        for l in range(L):
            for source, target in ((q1, q_own), (v0, w0), (v1, w1), (v2, w2)):
                target[x, l] = source[HALO + x, l, :, :COLS]
        return carry

    lax.fori_loop(0, ROWS, keep, 0)


def second_newton(*arrays):
    o = shaped(ROWS, L, 8, COLS)
    outs = (o, o, o, o, shaped(128, 128))
    return pl.pallas_call(
        second_kernel,
        out_shape=outs,
        in_specs=vmem(len(arrays)),
        out_specs=tuple(vmem(len(outs))),
        scratch_shapes=[pltpu.VMEM((XR, L, 8, XC), F32)] * 9,
        compiler_params=params(28),
        name="second_newton",
    )(*arrays)


def final_kernel(q, v0, v1, v2, gathered, out):
    c0, c1, c2 = coefficients(gathered)

    def row(x, carry):
        for l in range(L):
            value = q[x, l] + c0 * v0[x, l] + c1 * v1[x, l] + c2 * v2[x, l]
            out[chunk(x, l, 0), :] = value[:, :128]
            out[chunk(x, l, 1), :] = value[:, 128:]
        return carry

    lax.fori_loop(0, ROWS, row, 0)


def final_update(*arrays):
    return pl.pallas_call(
        final_kernel,
        out_shape=shaped(32 * LEV, 128),
        in_specs=vmem(len(arrays)),
        out_specs=vmem()[0],
        compiler_params=params(16),
        name="final_update",
    )(*arrays)


def exchange(to_high, to_low, axis):
    count = lax.axis_size(axis)
    up = [(i, i + 1) for i in range(count - 1)]
    down = [(i + 1, i) for i in range(count - 1)]
    return lax.ppermute(to_high, axis, up), lax.ppermute(to_low, axis, down)


def share(moments):
    return lax.all_to_all(moments, ("gx", "gy"), split_axis=0, concat_axis=0, tiled=True)


def body(
    pressure_old,
    conductivity,
    forcing,
    vegetated,
    cover_type,
    canopy_table,
    root_table,
    pair_counts,
    send_cols,
    canopy_state,
):
    owners = send_cols.shape[1]
    cols = in_hbm(send_cols.reshape(owners, 1, COLS))
    counts = in_hbm(pair_counts.reshape(owners))
    state = in_hbm(canopy_state.reshape(owners, 16, COLS))
    forcing, cover_type, vegetated = in_hbm(forcing), in_hbm(cover_type), in_hbm(vegetated)
    old, conductivity = in_hbm(flat(pressure_old)), in_hbm(flat(conductivity))
    canopy_table, root_table = in_hbm(canopy_table.T), in_hbm(root_table.T)

    payload, conductance = canopy_send(forcing, cover_type, canopy_table, counts, cols, state)
    arrived = lax.all_to_all(payload, "gx", split_axis=0, concat_axis=0, tiled=True)
    q_own, k_own, to_next, to_prev, edge_left, edge_right, uptake, surface = turn(
        old, conductivity, forcing, cover_type, vegetated, root_table, payload
    )
    from_prev, from_next = exchange(to_next, to_prev, "gx")
    source, to_right, to_left = canopy_source(
        arrived, cols, counts, forcing, conductance, uptake, surface, edge_left, edge_right
    )
    from_left, from_right = exchange(to_right, to_left, "gy")
    new_state = owner_update(arrived, state)
    to_next, to_prev = corners(source, from_left, from_right, in_hbm(new_state))
    corner_prev, corner_next = exchange(to_next, to_prev, "gx")

    mids = prepare(q_own, k_own, from_left, from_right)
    q, k, b, v0, v1, v2, moments = first_newton(
        *mids, from_prev, from_next, source, corner_prev, corner_next, from_left, from_right
    )
    q1, w0, w1, w2, moments = second_newton(mids[0], mids[1], q, k, b, v0, v1, v2, share(moments))
    pressure = unflat(final_update(q1, w0, w1, w2, share(moments)))
    return pressure, new_state.reshape(canopy_state.shape)


def solution(mesh):
    placed = (
        P(None, "gx", "gy"),
        P(None, "gx", "gy"),
        P(None, "gx", "gy"),
        P("gx", "gy"),
        P("gx", "gy"),
        P(),
        P(),
        P("gx", None, "gy"),
        P("gx", None, "gy", None),
        P("gx", None, "gy", None, None),
    )
    return jax.shard_map(
        body,
        mesh=mesh,
        in_specs=placed,
        out_specs=(P(None, "gx", "gy"), P("gx", None, "gy", None, None)),
        check_vma=False,
    )
```

```python
import jax
import jax.numpy as jnp
from jax import lax
from jax.experimental import pallas as pl
from jax.experimental.pallas import tpu as pltpu
from jax.sharding import PartitionSpec as P

FORC = 8
ROOT = 8
LEV = 64
ROWS = 16
COLS = 256
L = 8
HALO = 7
XR = ROWS + 2 * HALO
XC = 384
OUTSIDE = 1e37
BHALO = 6
SIDE = 2 * L + 1
CORNER = 2 * BHALO + SIDE
STORE = 0.05
GRAV = 0.5
F32 = jnp.float32
BF16 = jnp.bfloat16


def vmem(n=1):
    return [pl.BlockSpec(memory_space=pltpu.VMEM)] * n


def params(mib):
    return pltpu.CompilerParams(vmem_limit_bytes=mib * 1024 * 1024)


def shaped(*shape):
    return jax.ShapeDtypeStruct(shape, F32)


def iota(shape, dim):
    return lax.broadcasted_iota(jnp.int32, shape, dim)


def right(v):
    return pltpu.roll(v, v.shape[1] - 1, 1)


def left(v):
    return pltpu.roll(v, 1, 1)


def deeper(v):
    return pltpu.roll(v, v.shape[0] - 1, 0)


def higher(v):
    return pltpu.roll(v, 1, 0)


def lanes(v, shift):
    return v if shift % 128 == 0 else pltpu.roll(v, shift % 128, v.ndim - 1)


def pieces(v):
    high = v.astype(BF16)
    rest = v - high.astype(F32)
    mid = rest.astype(BF16)
    low = (rest - mid.astype(F32)).astype(BF16)
    return high, mid, low


def in_hbm(v):
    return pltpu.with_memory_space_constraint(v, pltpu.HBM)


def smem():
    return pl.BlockSpec(memory_space=pltpu.SMEM)


def looked_up(kinds, table):
    found = [jnp.zeros(kinds.shape, F32) for _ in range(table.shape[0])]
    for kind in range(table.shape[1]):
        hit = kinds == kind
        for m in range(table.shape[0]):
            found[m] = jnp.where(hit, table[m, kind], found[m])
    return found


def hits(index):
    row = lax.shift_right_logical(index, 8)
    col = jnp.bitwise_and(index, COLS - 1)
    row_hit = iota((ROWS, COLS), 0) == row
    col_hit = iota((COLS, COLS), 0) == col
    return row_hit, jnp.where(col_hit, 1.0, 0.0).astype(BF16)


def canopy_send_kernel(
    forcing, cover, canopy_table, counts, cols, state, payload, conductance, split
):
    weights = looked_up(cover[...], canopy_table)
    total = weights[0] * forcing[0]
    for m in range(1, FORC):
        total = total + weights[m] * forcing[m]
    g = 2.0 * jax.nn.sigmoid(total)
    conductance[...] = g
    channels = [forcing[0], forcing[1], forcing[2], jnp.tanh(forcing[4]), g]
    used = len(channels)
    for c, channel in enumerate(channels):
        for p, piece in enumerate(pieces(channel)):
            split[pl.ds((p * used + c) * ROWS, ROWS), :] = piece

    def owner(o, carry):
        row_hit, onehot = hits(cols[o])
        picked = jnp.dot(split[...], onehot, preferred_element_type=F32)
        span = used * ROWS
        picked = picked[:span] + picked[span : 2 * span] + picked[2 * span :]
        sub = iota((8, COLS), 0)
        out = pltpu.roll(state[o, 0:8, :], 6, 0)
        for c in range(used):
            chosen = jnp.where(row_hit, picked[c * ROWS : (c + 1) * ROWS], 0.0)
            chosen = jnp.sum(chosen, axis=0, keepdims=True)
            out = jnp.where(sub == c, chosen, out)
        live = jnp.where(iota((8, COLS), 1) < counts[o], 1.0, 0.0)
        payload[o] = jnp.where(sub == used, live, out)
        return carry

    lax.fori_loop(0, cols.shape[0], owner, 0, unroll=4)


def canopy_send(forcing, cover, canopy_table, counts, cols, state):
    owners = cols.shape[0]
    return pl.pallas_call(
        canopy_send_kernel,
        out_shape=(shaped(owners, 8, COLS), shaped(ROWS, COLS)),
        in_specs=vmem(2) + [smem(), smem()] + vmem(2),
        out_specs=tuple(vmem(2)),
        scratch_shapes=[pltpu.VMEM((15 * ROWS, COLS), BF16)],
        compiler_params=params(16),
        name="canopy_send",
    )(forcing, cover, canopy_table, counts, cols, state)


def softplus(v):
    return jnp.maximum(v, 0.0) + jnp.log1p(jnp.exp(-jnp.abs(v)))


def leaf(start, f0, f1, f2, g):
    temp = start
    for _ in range(3):
        temp = 0.5 * (start + f0) + 0.5 * jnp.tanh(f1 - g * (temp - f2))
    return temp


def source_kernel(
    arrived, cols, counts, forcing, conductance, uptake, surface, edge_left, edge_right,
    source, to_right, to_left, total, turned,
):
    total[...] = jnp.zeros_like(total)

    def owner(o, carry):
        row_hit, onehot = hits(cols[o])
        wanted = jnp.logical_and(row_hit, iota((ROWS, COLS), 1) < counts[o])
        block = arrived[o]
        parts = []
        for c in (6, 7):
            value = jnp.where(wanted, block[c : c + 1, :], 0.0)
            parts.extend(pieces(value))
        stacked = jnp.concatenate(parts, axis=0)
        total[...] += lax.dot_general(
            stacked, onehot, (((1,), (1,)), ((), ())), preferred_element_type=F32
        )
        return carry

    lax.fori_loop(0, cols.shape[0], owner, 0, unroll=4)

    def piece(k):
        return total[k * ROWS : (k + 1) * ROWS, :]

    water = piece(0) + piece(1) + piece(2)
    start = piece(3) + piece(4) + piece(5)
    g = conductance[...]
    temp = leaf(start, forcing[0], forcing[1], forcing[2], g)
    demand = g * softplus(temp - forcing[3]) / (1.0 + water * water)
    for m in range(ROOT):
        value = -(demand * uptake[m])
        if m == 0:
            value = value + surface[...]
        for t in range(2):
            turned[pl.ds(t * 128 + m * ROWS, ROWS), :] = value[:, t * 128 : t * 128 + 128]
    lane = iota((L, 128), 1)
    first = jnp.zeros((L, 128), F32)
    last = jnp.zeros((L, 128), F32)
    for x in range(ROWS):
        low = turned[pl.ds(x, L, stride=ROWS), :]
        high = turned[pl.ds(128 + x, L, stride=ROWS), :]
        source[x, :, :128] = low
        source[x, :, 128:] = high
        here = jnp.logical_and(lane >= 8 * x, lane < 8 * x + 8)
        first = jnp.where(here, lanes(low, 8 * x), first)
        last = jnp.where(here, lanes(high, 8 * x - 120), last)
    for target, edge, own_edge in ((to_left, edge_left, first), (to_right, edge_right, last)):
        target[0 : 2 * L] = edge[...]
        target[2 * L] = own_edge


def canopy_source(*arrays):
    v = vmem()[0]
    return pl.pallas_call(
        source_kernel,
        out_shape=(shaped(ROWS, ROOT, COLS), shaped(SIDE, L, 128), shaped(SIDE, L, 128)),
        in_specs=[v, v, smem(), v, v, v, v, v, v],
        out_specs=(v, v, v),
        scratch_shapes=[pltpu.VMEM((6 * ROWS, COLS), F32), pltpu.VMEM((2 * 128, 128), F32)],
        compiler_params=params(16),
        name="canopy_source",
    )(*arrays)


def owner_kernel(arrived, state, updated):
    def slot(i, carry):
        block = arrived[i]
        old = state[i]
        temp = leaf(old[1:2], block[0:1], block[1:2], block[2:3], block[4:5])
        sub = iota(old.shape, 0)
        base = jnp.where(sub == 1, temp, old)
        upper = pltpu.roll(base, 1, 0)
        lower = pltpu.roll(base, base.shape[0] - 1, 0)
        lower = jnp.where(sub == base.shape[0] - 1, base, lower)
        fresh = 0.6 * base + 0.2 * upper + 0.2 * lower
        fresh = jnp.where(sub == 1, temp, fresh)
        fresh = jnp.where(sub == 0, 0.8 * old + 0.2 * block[3:4], fresh)
        updated[i] = jnp.where(block[5:6] > 0.5, fresh, old)
        return carry

    lax.fori_loop(0, arrived.shape[0], slot, 0)


def owner_update(arrived, state):
    return pl.pallas_call(
        owner_kernel,
        out_shape=shaped(*state.shape),
        in_specs=vmem(2),
        out_specs=vmem()[0],
        compiler_params=params(8),
        name="owner_update",
    )(arrived, state)


def flat(v):
    return v.reshape(LEV, 2, 8, 2, 128).transpose(0, 1, 3, 2, 4).reshape(32 * LEV, 128)


def unflat(v):
    return v.reshape(LEV, 2, 2, 8, 128).transpose(0, 1, 3, 2, 4).reshape(LEV, ROWS, COLS)


def chunk(x, l, t):
    return pl.ds(32 * l + 16 * (x // 8) + 8 * t + x % 8, 8, stride=32 * L)


RIM = 2 * HALO * 2


def turn_kernel(
    pressure, conductivity, forcing, cover, vegetated, root_table, after,
    q, k, to_next, to_prev, edge_left, edge_right, uptake, surface,
):
    lane = iota((8, 128), 1)

    def layer(l, carry):
        for f, (field, target) in enumerate(((pressure, q), (conductivity, k))):
            first = jnp.zeros((8, 128), F32)
            last = jnp.zeros((8, 128), F32)
            for x in range(ROWS):
                for t in range(2):
                    part = field[chunk(x, l, t), :]
                    target[x, l, :, 128 * t : 128 * t + 128] = part
                    if x < HALO:
                        to_prev[2 * (f * HALO + x) + t, l] = part
                    if x >= ROWS - HALO:
                        to_next[2 * (f * HALO + x - ROWS + HALO) + t, l] = part
                    here = jnp.logical_and(lane >= 8 * x, lane < 8 * x + 8)
                    if t == 0:
                        first = jnp.where(here, lanes(part, 8 * x), first)
                    else:
                        last = jnp.where(here, lanes(part, 8 * x - 120), last)
            edge_left[f * L + l] = first
            edge_right[f * L + l] = last
        return carry

    lax.fori_loop(0, L, layer, 0)
    roots = looked_up(cover[...], root_table)
    planted = vegetated[...] == 1
    for m in range(ROOT):
        top = jnp.concatenate(
            [
                jnp.concatenate([pressure[pl.ds(32 * m + 16 * xt + 8 * t, 8), :] for t in range(2)], axis=1)
                for xt in range(2)
            ],
            axis=0,
        )
        moist = jax.nn.sigmoid(2.0 * (top + 1.5))
        uptake[m] = jnp.where(planted, roots[m] * moist, 0.0)
        if m == 0:
            evaporation = jnp.where(planted, 0.0, 0.5) * softplus(forcing[3] - forcing[2]) * moist
            surface[...] = 0.3 * softplus(forcing[4]) - evaporation


def turn(*arrays):
    own_shape = shaped(ROWS, L, 8, COLS)
    rim = shaped(RIM, L, 8, 128)
    edge = shaped(2 * L, 8, 128)
    outs = (own_shape, own_shape, rim, rim, edge, edge, shaped(ROOT, ROWS, COLS), shaped(ROWS, COLS))
    return pl.pallas_call(
        turn_kernel,
        out_shape=outs,
        in_specs=vmem(5) + [smem(), pl.BlockSpec(memory_space=pl.ANY)],
        out_specs=tuple(vmem(len(outs))),
        compiler_params=params(24),
        name="turn",
    )(*arrays)


def corner_kernel(source, from_left, from_right, to_next, to_prev):
    low = iota((8, 128), 1) < 64
    for i in range(BHALO):
        for t in range(2):
            part = pl.ds(128 * t, 128)
            to_next[2 * i + t] = source[ROWS - BHALO + i, :, part]
            to_prev[2 * i + t] = source[i, :, part]
    for j in range(SIDE):
        a, b = from_left[j], from_right[j]
        to_next[2 * BHALO + j] = jnp.where(low, lanes(a, 64), b)
        to_prev[2 * BHALO + j] = jnp.where(low, a, lanes(b, 64))


def corners(*arrays):
    outs = (shaped(CORNER, 8, 128), shaped(CORNER, 8, 128))
    return pl.pallas_call(
        corner_kernel,
        out_shape=outs,
        in_specs=vmem(3),
        out_specs=tuple(vmem(2)),
        compiler_params=params(16),
        name="corners",
    )(*arrays)


def halo_tile(from_left, from_right, lane, at_left, at_right):
    tile = jnp.where(lane < 8, lanes(from_right, -at_right), 0.0)
    return jnp.where(lane >= 120, lanes(from_left, 120 - at_left), tile)


def own(v):
    return v[:, :COLS]


def local_terms(q, k):
    bend = jnp.tanh(q)
    s = 0.5 + 0.5 * bend
    m = k * (0.1 + 0.9 * s)
    return bend, jnp.where(m > 0.0, 0.5 / m, OUTSIDE), 1.4 * s * (1.0 - s) + STORE


def blocks(rows, block, row, carry=None):
    def step(i, held):
        for j in range(block):
            held = row(rows[0] + i * block + j, held)
        return held

    return lax.fori_loop(0, (rows[1] - rows[0]) // block, step, carry)


def couplings(q, resist, cx, cy, cyl, cz, diag, rows, block, emit):
    last = iota((8, XC), 0) == 7

    def row(r, carry):
        q_0, m_0, q_7, m_7 = q[r, 0], resist[r, 0], q[r, 7], resist[r, 7]
        c_7 = jnp.where(last, 0.0, 1.0 / (m_7 + deeper(m_0)))
        f_7 = c_7 * (q_7 - deeper(q_0) + GRAV)
        cz[r, 7] = c_7
        c_up, f_up = higher(c_7), higher(f_7)
        v, m = q_0, m_0
        for l in range(L):
            if l < L - 1:
                m_n, v_n = resist[r, l + 1], q[r, l + 1]
                c = 1.0 / (m + m_n)
                f = c * (v - v_n + GRAV)
                cz[r, l] = c
            else:
                c, f = c_7, f_7
            y = 1.0 / (m + right(m))
            yl = 1.0 / (m + left(m))
            x = 1.0 / (m + resist[r + 1, l])
            xp = cx[r - 1, l]
            cy[r, l] = y
            cyl[r, l] = yl
            cx[r, l] = x
            out = y * (v - right(v)) + yl * (v - left(v))
            out = out + (x * (v - q[r + 1, l]) + xp * (v - q[r - 1, l])) + (f - f_up)
            diag[r, l] = diag[r, l] + ((y + yl) + (x + xp) + (c + c_up))
            emit(r, l, out)
            c_up, f_up = c, f
            if l < L - 1:
                v, m = v_n, m_n
        return carry

    for l in range(L):
        cx[rows[0] - 1, l] = 1.0 / (resist[rows[0] - 1, l] + resist[rows[0], l])
    blocks(rows, block, row, 0)


def apply(v_in, v_out, coefs, shift, rows, block, held, counted):
    cx, cy, cyl, cz, diag = coefs

    def row(r, held):
        at = r - shift
        c_up, v_up = higher(cz[at, 7]), higher(v_in[r, 7])
        v_0 = v_in[r, 0]
        v = v_0
        square, cross = held
        for l in range(L):
            v_n = v_in[r, l + 1] if l < L - 1 else deeper(v_0)
            c = cz[at, l]
            image = diag[at, l] * v - cy[at, l] * right(v) - cyl[at, l] * left(v)
            image = image - cx[at, l] * v_in[r + 1, l] - cx[at - 1, l] * v_in[r - 1, l]
            image = image - c * v_n - c_up * v_up
            if v_out is not None:
                v_out[r, l] = image
            if counted:
                a, b = own(v), own(image)
                square = square + a * a
                cross = cross + a * b
            v_up, c_up, v = v, c, v_n
        return square, cross

    return blocks(rows, block, row, held)


def write_moments(sums, moments):
    row = jnp.zeros((1, 128), F32)
    lane = iota((1, 128), 1)
    for k, held in enumerate(sums):
        value = jnp.sum(jnp.sum(held, axis=0, keepdims=True), axis=1, keepdims=True)
        row = jnp.where(lane == k, value, row)
    moments[...] = jnp.broadcast_to(row, moments.shape)


def no_sums():
    zero = jnp.zeros((8, COLS), F32)
    return zero, zero


def coefficients(gathered):
    row = jnp.sum(gathered[...], axis=0, keepdims=True)
    lane = iota((1, 128), 1)
    m = [jnp.sum(jnp.where(lane == k, row, 0.0), axis=1, keepdims=True) for k in range(6)]

    def dot(a, b, shift):
        total = jnp.zeros((1, 1), F32)
        for i, p in enumerate(a):
            for j, q in enumerate(b):
                total = total + p * q * m[i + j + shift]
        return total

    one = jnp.ones((1, 1), F32)
    a0 = m[0] / m[1]
    r1 = [one, -a0]
    n1 = dot(r1, r1, 0)
    b0 = n1 / m[0]
    p1 = [one + b0, -a0]
    a1 = n1 / dot(p1, p1, 1)
    r2 = [one, -a0 - a1 * p1[0], -a1 * p1[1]]
    n2 = dot(r2, r2, 0)
    b1 = n2 / n1
    p2 = [r2[0] + b1 * p1[0], r2[1] + b1 * p1[1], r2[2]]
    a2 = n2 / dot(p2, p2, 1)
    return (
        a0 + a1 * p1[0] + a2 * p2[0],
        a1 * p1[1] + a2 * p2[1],
        a2 * p2[2],
    )


def source_at(b, r, l, sub):
    return jnp.where(sub == 0, pltpu.roll(b[r], (8 - l) % 8, 0), 0.0)


def prepare_kernel(
    q_own, k_own, from_left, from_right,
    q, k, resist, cx, cy, cyl, cz, diag, base,
):
    lane = iota((8, 128), 1)

    def fill(l, carry):
        for f, (field, target) in enumerate(((q_own, q), (k_own, k))):
            a, c = from_left[f * L + l], from_right[f * L + l]
            for x in range(ROWS):
                target[x, l, :, :COLS] = field[x, l]
                target[x, l, :, COLS:] = halo_tile(a, c, lane, 8 * x, 8 * x)
        for x in range(ROWS):
            _, resist[x, l], diag[x, l] = local_terms(q[x, l], k[x, l])
        return carry

    lax.fori_loop(0, L, fill, 0)

    def emit(r, l, out):
        base[r, l] = -out

    couplings(q, resist, cx, cy, cyl, cz, diag, (1, ROWS - 1), 2, emit)


def prepare(*arrays):
    outs = (shaped(ROWS, L, 8, XC),) * 9
    return pl.pallas_call(
        prepare_kernel,
        out_shape=outs,
        in_specs=vmem(4),
        out_specs=tuple(vmem(9)),
        compiler_params=params(4),
        name="prepare",
    )(*arrays)


RSHIFT = 12
RROWS = 18


def first_kernel(
    q_mid, k_mid, resist_mid, cx_mid, cy_mid, cyl_mid, cz_mid, diag_mid, base,
    from_prev, from_next, source, corner_prev, corner_next, from_left, from_right,
    q, k, b, v0, v1, v2, moments,
    resist, cx, cy, cyl, cz, diag,
):
    lane = iota((8, 128), 1)

    def fill(l, carry):
        for f, target in enumerate((q, k)):
            at = 2 * BHALO + f * L + l
            for side, corner, r, spot in (
                (from_prev, corner_prev, 0, 8 * (8 - HALO)),
                (from_next, corner_next, HALO + ROWS - RSHIFT, 0),
            ):
                tile = corner[at]
                for i in range(HALO):
                    for t in range(2):
                        target[r + i, l, :, 128 * t : 128 * t + 128] = side[2 * (f * HALO + i) + t, l]
                    left_at = spot + 8 * i
                    target[r + i, l, :, COLS:] = halo_tile(tile, tile, lane, left_at, 64 + left_at)
        for r in (*range(HALO), *range(RROWS - HALO, RROWS)):
            _, resist[r, l], diag[r, l] = local_terms(q[r, l], k[r, l])
        for r, x in ((7, 0), (8, 1), (9, ROWS - 2), (10, ROWS - 1)):
            q[r, l] = q_mid[x, l]
            resist[r, l] = resist_mid[x, l]
            diag[r, l] = diag_mid[x, l]
        return carry

    lax.fori_loop(0, L, fill, 0)

    a, c = from_left[2 * L], from_right[2 * L]
    for x in range(ROWS):
        b[HALO + x, :, :COLS] = source[x]
        b[HALO + x, :, COLS:] = halo_tile(a, c, lane, 8 * x, 8 * x)
    for side, r, spot in (
        (corner_prev, HALO - BHALO, 8 * (8 - BHALO)),
        (corner_next, HALO + ROWS, 0),
    ):
        tile = side[CORNER - 1]
        for i in range(BHALO):
            for t in range(2):
                b[r + i, :, 128 * t : 128 * t + 128] = side[2 * i + t]
            left_at = spot + 8 * i
            b[r + i, :, COLS:] = halo_tile(tile, tile, lane, left_at, 64 + left_at)

    sub = iota((8, XC), 0)
    coefs = (cx, cy, cyl, cz, diag)
    mids = (cx_mid, cy_mid, cyl_mid, cz_mid, diag_mid)

    for shift, rows in ((0, (1, HALO + 1)), (RSHIFT, (RROWS - HALO - 1, RROWS - 1))):

        def emit(r, l, out, shift=shift):
            v0[r + shift, l] = source_at(b, r + shift, l, sub) - out

        couplings(q, resist, *coefs, rows, 1, emit)

    def inner(r, carry):
        for l in range(L):
            v0[r, l] = source_at(b, r, l, sub) + base[r - HALO, l]
        return carry

    low, high = HALO, HALO + ROWS - 1
    blocks((low + 1, high), 2, inner, 0)

    sums = []
    for v_in, v_out, deep in ((v0, v1, 5), (v1, v2, 4), (v2, None, 0)):
        held = apply(v_in, v_out, mids, HALO, (low + 1, high), 7, no_sums(), True)
        held = apply(v_in, v_out, coefs, 0, (low, low + 1), 1, held, True)
        held = apply(v_in, v_out, coefs, RSHIFT, (high, high + 1), 1, held, True)
        if deep:
            apply(v_in, v_out, coefs, 0, (low - deep, low), deep, no_sums(), False)
            apply(v_in, v_out, coefs, RSHIFT, (high + 1, high + 1 + deep), deep, no_sums(), False)
        sums += held
    write_moments(sums, moments)


def first_newton(*arrays):
    w = shaped(XR, L, 8, XC)
    rim = shaped(RROWS, L, 8, XC)
    outs = (rim, rim, shaped(XR, L, XC), w, w, w, shaped(128, 128))
    return pl.pallas_call(
        first_kernel,
        out_shape=outs,
        in_specs=vmem(len(arrays)),
        out_specs=tuple(vmem(len(outs))),
        scratch_shapes=[pltpu.VMEM((RROWS, L, 8, XC), F32)] * 6,
        compiler_params=params(14),
        name="first_newton",
    )(*arrays)


def second_kernel(
    q_mid, k_mid, q_rim, k_rim, b, u0, u1, u2, gathered,
    q_own, w0, w1, w2, moments,
    q1, resist, cx, cy, cyl, cz, diag, v0, v2,
):
    v1 = resist
    c0, c1, c2 = coefficients(gathered)
    sub = iota((8, XC), 0)

    for q, k, shift, rows in (
        (q_rim, k_rim, 0, (3, HALO)),
        (q_mid, k_mid, HALO, (HALO, HALO + ROWS)),
        (q_rim, k_rim, RSHIFT, (HALO + ROWS, XR - 3)),
    ):

        def update(r, carry, q=q, k=k, shift=shift):
            for l in range(L):
                old = q[r - shift, l]
                step = c0 * u0[r, l] + c1 * u1[r, l] + c2 * u2[r, l]
                new = old + step
                q1[r, l] = new
                bend, resist[r, l], diag[r, l] = local_terms(new, k[r - shift, l])
                stored = 0.35 * (bend - jnp.tanh(old)) + STORE * step
                v0[r, l] = source_at(b, r, l, sub) - stored
            return carry

        blocks(rows, 2, update, 0)

    def emit(r, l, out):
        v0[r, l] = v0[r, l] - out

    coefs = (cx, cy, cyl, cz, diag)
    couplings(q1, resist, *coefs, (4, XR - 4), 2, emit)
    low, high = HALO, HALO + ROWS
    sums = []
    for v_in, v_out, deep in ((v0, v1, 2), (v1, v2, 1), (v2, None, 0)):
        sums += apply(v_in, v_out, coefs, 0, (low, high), 8, no_sums(), True)
        if deep:
            apply(v_in, v_out, coefs, 0, (low - deep, low), deep, no_sums(), False)
            apply(v_in, v_out, coefs, 0, (high, high + deep), deep, no_sums(), False)
    write_moments(sums, moments)

    def keep(x, carry):
        for l in range(L):
            for source, target in ((q1, q_own), (v0, w0), (v1, w1), (v2, w2)):
                target[x, l] = source[HALO + x, l, :, :COLS]
        return carry

    lax.fori_loop(0, ROWS, keep, 0)


def second_newton(*arrays):
    o = shaped(ROWS, L, 8, COLS)
    outs = (o, o, o, o, shaped(128, 128))
    return pl.pallas_call(
        second_kernel,
        out_shape=outs,
        in_specs=vmem(len(arrays)),
        out_specs=tuple(vmem(len(outs))),
        scratch_shapes=[pltpu.VMEM((XR, L, 8, XC), F32)] * 9,
        compiler_params=params(28),
        name="second_newton",
    )(*arrays)


def final_kernel(q, v0, v1, v2, gathered, out, held, sems):
    c0, c1, c2 = coefficients(gathered)

    def send(l):
        part = pl.ds(32 * l, 32)
        return pltpu.make_async_copy(held.at[:, part], out.at[:, part], sems.at[l])

    for l in range(L):

        def row(x, carry, l=l):
            value = q[x, l] + c0 * v0[x, l] + c1 * v1[x, l] + c2 * v2[x, l]
            at = 32 * l + 16 * (x // 8) + x % 8
            held[:, at, :] = value[:, :128]
            held[:, at + 8, :] = value[:, 128:]
            return carry

        lax.fori_loop(0, ROWS, row, 0, unroll=4)
        send(l).start()
    for l in range(L):
        send(l).wait()


def final_update(*arrays):
    return pl.pallas_call(
        final_kernel,
        out_shape=shaped(8, 32 * L, 128),
        in_specs=vmem(len(arrays)),
        out_specs=pl.BlockSpec(memory_space=pltpu.HBM),
        scratch_shapes=[pltpu.VMEM((8, 32 * L, 128), F32), pltpu.SemaphoreType.DMA((L,))],
        compiler_params=params(4),
        name="final_update",
    )(*arrays)


def exchange(to_high, to_low, axis):
    count = lax.axis_size(axis)
    up = [(i, i + 1) for i in range(count - 1)]
    down = [(i + 1, i) for i in range(count - 1)]
    return lax.ppermute(to_high, axis, up), lax.ppermute(to_low, axis, down)


def share(moments):
    return lax.all_to_all(moments, ("gx", "gy"), split_axis=0, concat_axis=0, tiled=True)


def body(
    pressure_old,
    conductivity,
    forcing,
    vegetated,
    cover_type,
    canopy_table,
    root_table,
    pair_counts,
    send_cols,
    canopy_state,
):
    owners = send_cols.shape[1]
    cols = in_hbm(send_cols.reshape(owners, 1, COLS))
    counts = in_hbm(pair_counts.reshape(owners))
    state = in_hbm(canopy_state.reshape(owners, 16, COLS))
    forcing, cover_type, vegetated = in_hbm(forcing), in_hbm(cover_type), in_hbm(vegetated)
    old, conductivity = in_hbm(flat(pressure_old)), in_hbm(flat(conductivity))
    canopy_table, root_table = in_hbm(canopy_table.T), in_hbm(root_table.T)

    payload, conductance = canopy_send(forcing, cover_type, canopy_table, counts, cols, state)
    arrived = lax.all_to_all(payload, "gx", split_axis=0, concat_axis=0, tiled=True)
    q_own, k_own, to_next, to_prev, edge_left, edge_right, uptake, surface = turn(
        old, conductivity, forcing, cover_type, vegetated, root_table, payload
    )
    to_next, to_prev, arrived = lax.optimization_barrier((to_next, to_prev, arrived))
    from_prev, from_next = exchange(to_next, to_prev, "gx")
    source, to_right, to_left = canopy_source(
        arrived, cols, counts, forcing, conductance, uptake, surface, edge_left, edge_right
    )
    from_left, from_right = exchange(to_right, to_left, "gy")
    to_next, to_prev = corners(source, from_left, from_right)
    corner_prev, corner_next = exchange(to_next, to_prev, "gx")

    mids = prepare(q_own, k_own, from_left, from_right)
    q, k, b, v0, v1, v2, moments = first_newton(
        *mids, from_prev, from_next, source, corner_prev, corner_next, from_left, from_right
    )
    moments, arrived = lax.optimization_barrier((moments, arrived))
    new_state = owner_update(arrived, state)
    q1, w0, w1, w2, moments = second_newton(mids[0], mids[1], q, k, b, v0, v1, v2, share(moments))
    pressure = unflat(final_update(q1, w0, w1, w2, share(moments)))
    return pressure, new_state.reshape(canopy_state.shape)


def solution(mesh):
    placed = (
        P(None, "gx", "gy"),
        P(None, "gx", "gy"),
        P(None, "gx", "gy"),
        P("gx", "gy"),
        P("gx", "gy"),
        P(),
        P(),
        P("gx", None, "gy"),
        P("gx", None, "gy", None),
        P("gx", None, "gy", None, None),
    )
    return jax.shard_map(
        body,
        mesh=mesh,
        in_specs=placed,
        out_specs=(P(None, "gx", "gy"), P("gx", None, "gy", None, None)),
        check_vma=False,
    )
```

```python
import jax
import jax.numpy as jnp
from jax import lax
from jax.experimental import pallas as pl
from jax.experimental.pallas import tpu as pltpu
from jax.sharding import PartitionSpec as P

FORC = 8
ROOT = 8
LEV = 64
ROWS = 16
COLS = 256
L = 8
HALO = 7
XR = ROWS + 2 * HALO
XC = 384
OUTSIDE = 1e37
BHALO = 6
SIDE = 2 * L + 1
CORNER = 2 * BHALO + SIDE
STORE = 0.05
GRAV = 0.5
F32 = jnp.float32
BF16 = jnp.bfloat16


def vmem(n=1):
    return [pl.BlockSpec(memory_space=pltpu.VMEM)] * n


def params(mib):
    return pltpu.CompilerParams(vmem_limit_bytes=mib * 1024 * 1024)


def shaped(*shape):
    return jax.ShapeDtypeStruct(shape, F32)


def iota(shape, dim):
    return lax.broadcasted_iota(jnp.int32, shape, dim)


def right(v):
    return pltpu.roll(v, v.shape[1] - 1, 1)


def left(v):
    return pltpu.roll(v, 1, 1)


def deeper(v):
    return pltpu.roll(v, v.shape[0] - 1, 0)


def higher(v):
    return pltpu.roll(v, 1, 0)


def lanes(v, shift):
    return v if shift % 128 == 0 else pltpu.roll(v, shift % 128, v.ndim - 1)


def pieces(v):
    high = v.astype(BF16)
    rest = v - high.astype(F32)
    mid = rest.astype(BF16)
    low = (rest - mid.astype(F32)).astype(BF16)
    return high, mid, low


def in_hbm(v):
    return pltpu.with_memory_space_constraint(v, pltpu.HBM)


def smem():
    return pl.BlockSpec(memory_space=pltpu.SMEM)


def looked_up(kinds, table):
    found = [jnp.zeros(kinds.shape, F32) for _ in range(table.shape[0])]
    for kind in range(table.shape[1]):
        hit = kinds == kind
        for m in range(table.shape[0]):
            found[m] = jnp.where(hit, table[m, kind], found[m])
    return found


def hits(index):
    row = lax.shift_right_logical(index, 8)
    col = jnp.bitwise_and(index, COLS - 1)
    row_hit = iota((ROWS, COLS), 0) == row
    col_hit = iota((COLS, COLS), 0) == col
    return row_hit, jnp.where(col_hit, 1.0, 0.0).astype(BF16)


def canopy_send_kernel(
    forcing, cover, canopy_table, counts, cols, state, payload, conductance, split
):
    weights = looked_up(cover[...], canopy_table)
    total = weights[0] * forcing[0]
    for m in range(1, FORC):
        total = total + weights[m] * forcing[m]
    g = 2.0 * jax.nn.sigmoid(total)
    conductance[...] = g
    channels = [forcing[0], forcing[1], forcing[2], jnp.tanh(forcing[4]), g]
    used = len(channels)
    for c, channel in enumerate(channels):
        for p, piece in enumerate(pieces(channel)):
            split[pl.ds((p * used + c) * ROWS, ROWS), :] = piece

    def owner(o, carry):
        row_hit, onehot = hits(cols[o])
        picked = jnp.dot(split[...], onehot, preferred_element_type=F32)
        span = used * ROWS
        picked = picked[:span] + picked[span : 2 * span] + picked[2 * span :]
        sub = iota((8, COLS), 0)
        out = pltpu.roll(state[o, 0:8, :], 6, 0)
        for c in range(used):
            chosen = jnp.where(row_hit, picked[c * ROWS : (c + 1) * ROWS], 0.0)
            chosen = jnp.sum(chosen, axis=0, keepdims=True)
            out = jnp.where(sub == c, chosen, out)
        live = jnp.where(iota((8, COLS), 1) < counts[o], 1.0, 0.0)
        payload[o] = jnp.where(sub == used, live, out)
        return carry

    lax.fori_loop(0, cols.shape[0], owner, 0, unroll=4)


def canopy_send(forcing, cover, canopy_table, counts, cols, state):
    owners = cols.shape[0]
    return pl.pallas_call(
        canopy_send_kernel,
        out_shape=(shaped(owners, 8, COLS), shaped(ROWS, COLS)),
        in_specs=vmem(2) + [smem(), smem()] + vmem(2),
        out_specs=tuple(vmem(2)),
        scratch_shapes=[pltpu.VMEM((15 * ROWS, COLS), BF16)],
        compiler_params=params(16),
        name="canopy_send",
    )(forcing, cover, canopy_table, counts, cols, state)


def softplus(v):
    return jnp.maximum(v, 0.0) + jnp.log1p(jnp.exp(-jnp.abs(v)))


def leaf(start, f0, f1, f2, g):
    temp = start
    for _ in range(3):
        temp = 0.5 * (start + f0) + 0.5 * jnp.tanh(f1 - g * (temp - f2))
    return temp


def source_kernel(
    arrived, cols, counts, forcing, conductance, uptake, surface, edge_left, edge_right,
    source, to_right, to_left, total, turned,
):
    total[...] = jnp.zeros_like(total)

    def owner(o, carry):
        row_hit, onehot = hits(cols[o])
        wanted = jnp.logical_and(row_hit, iota((ROWS, COLS), 1) < counts[o])
        block = arrived[o]
        parts = []
        for c in (6, 7):
            value = jnp.where(wanted, block[c : c + 1, :], 0.0)
            parts.extend(pieces(value))
        stacked = jnp.concatenate(parts, axis=0)
        total[...] += lax.dot_general(
            stacked, onehot, (((1,), (1,)), ((), ())), preferred_element_type=F32
        )
        return carry

    lax.fori_loop(0, cols.shape[0], owner, 0, unroll=4)

    def piece(k):
        return total[k * ROWS : (k + 1) * ROWS, :]

    water = piece(0) + piece(1) + piece(2)
    start = piece(3) + piece(4) + piece(5)
    g = conductance[...]
    temp = leaf(start, forcing[0], forcing[1], forcing[2], g)
    demand = g * softplus(temp - forcing[3]) / (1.0 + water * water)
    for m in range(ROOT):
        value = -(demand * uptake[m])
        if m == 0:
            value = value + surface[...]
        for t in range(2):
            turned[pl.ds(t * 128 + m * ROWS, ROWS), :] = value[:, t * 128 : t * 128 + 128]
    lane = iota((L, 128), 1)
    first = jnp.zeros((L, 128), F32)
    last = jnp.zeros((L, 128), F32)
    for x in range(ROWS):
        low = turned[pl.ds(x, L, stride=ROWS), :]
        high = turned[pl.ds(128 + x, L, stride=ROWS), :]
        source[x, :, :128] = low
        source[x, :, 128:] = high
        here = jnp.logical_and(lane >= 8 * x, lane < 8 * x + 8)
        first = jnp.where(here, lanes(low, 8 * x), first)
        last = jnp.where(here, lanes(high, 8 * x - 120), last)
    for target, edge, own_edge in ((to_left, edge_left, first), (to_right, edge_right, last)):
        target[0 : 2 * L] = edge[...]
        target[2 * L] = own_edge


def canopy_source(*arrays):
    v = vmem()[0]
    return pl.pallas_call(
        source_kernel,
        out_shape=(shaped(ROWS, ROOT, COLS), shaped(SIDE, L, 128), shaped(SIDE, L, 128)),
        in_specs=[v, v, smem(), v, v, v, v, v, v],
        out_specs=(v, v, v),
        scratch_shapes=[pltpu.VMEM((6 * ROWS, COLS), F32), pltpu.VMEM((2 * 128, 128), F32)],
        compiler_params=params(16),
        name="canopy_source",
    )(*arrays)


def owner_kernel(arrived, state, updated):
    def slot(i, carry):
        block = arrived[i]
        old = state[i]
        temp = leaf(old[1:2], block[0:1], block[1:2], block[2:3], block[4:5])
        sub = iota(old.shape, 0)
        base = jnp.where(sub == 1, temp, old)
        upper = pltpu.roll(base, 1, 0)
        lower = pltpu.roll(base, base.shape[0] - 1, 0)
        lower = jnp.where(sub == base.shape[0] - 1, base, lower)
        fresh = 0.6 * base + 0.2 * upper + 0.2 * lower
        fresh = jnp.where(sub == 1, temp, fresh)
        fresh = jnp.where(sub == 0, 0.8 * old + 0.2 * block[3:4], fresh)
        updated[i] = jnp.where(block[5:6] > 0.5, fresh, old)
        return carry

    lax.fori_loop(0, arrived.shape[0], slot, 0)


def owner_update(arrived, state):
    return pl.pallas_call(
        owner_kernel,
        out_shape=shaped(*state.shape),
        in_specs=vmem(2),
        out_specs=vmem()[0],
        compiler_params=params(8),
        name="owner_update",
    )(arrived, state)


def flat(v):
    return v.reshape(LEV, 2, 8, 2, 128).transpose(0, 1, 3, 2, 4).reshape(32 * LEV, 128)


def unflat(v):
    return v.reshape(LEV, 2, 2, 8, 128).transpose(0, 1, 3, 2, 4).reshape(LEV, ROWS, COLS)


def chunk(x, l, t):
    return pl.ds(32 * l + 16 * (x // 8) + 8 * t + x % 8, 8, stride=32 * L)


RIM = 2 * HALO * 2


def turn_kernel(
    pressure, conductivity, forcing, cover, vegetated, root_table, after,
    q, k, to_next, to_prev, edge_left, edge_right, uptake, surface,
    next_rim, prev_rim, sems,
):
    lane = iota((8, 128), 1)

    def layer(l, carry):
        for f, (field, target) in enumerate(((pressure, q), (conductivity, k))):
            first = jnp.zeros((8, 128), F32)
            last = jnp.zeros((8, 128), F32)
            for x in range(ROWS):
                for t in range(2):
                    part = field[chunk(x, l, t), :]
                    target[x, l, :, 128 * t : 128 * t + 128] = part
                    if x < HALO:
                        prev_rim[2 * (f * HALO + x) + t, l] = part
                    if x >= ROWS - HALO:
                        next_rim[2 * (f * HALO + x - ROWS + HALO) + t, l] = part
                    here = jnp.logical_and(lane >= 8 * x, lane < 8 * x + 8)
                    if t == 0:
                        first = jnp.where(here, lanes(part, 8 * x), first)
                    else:
                        last = jnp.where(here, lanes(part, 8 * x - 120), last)
            edge_left[f * L + l] = first
            edge_right[f * L + l] = last
        return carry

    lax.fori_loop(0, L, layer, 0)
    sends = [
        pltpu.make_async_copy(next_rim, to_next, sems.at[0]),
        pltpu.make_async_copy(prev_rim, to_prev, sems.at[1]),
    ]
    for send in sends:
        send.start()
    roots = looked_up(cover[...], root_table)
    planted = vegetated[...] == 1
    for m in range(ROOT):
        top = jnp.concatenate(
            [
                jnp.concatenate([pressure[pl.ds(32 * m + 16 * xt + 8 * t, 8), :] for t in range(2)], axis=1)
                for xt in range(2)
            ],
            axis=0,
        )
        moist = jax.nn.sigmoid(2.0 * (top + 1.5))
        uptake[m] = jnp.where(planted, roots[m] * moist, 0.0)
        if m == 0:
            evaporation = jnp.where(planted, 0.0, 0.5) * softplus(forcing[3] - forcing[2]) * moist
            surface[...] = 0.3 * softplus(forcing[4]) - evaporation
    for send in sends:
        send.wait()


def turn(*arrays):
    own_shape = shaped(ROWS, L, 8, COLS)
    rim = shaped(RIM, L, 8, 128)
    edge = shaped(2 * L, 8, 128)
    outs = (own_shape, own_shape, rim, rim, edge, edge, shaped(ROOT, ROWS, COLS), shaped(ROWS, COLS))
    return pl.pallas_call(
        turn_kernel,
        out_shape=outs,
        in_specs=vmem(5) + [smem(), pl.BlockSpec(memory_space=pl.ANY)],
        out_specs=(*vmem(2), *[pl.BlockSpec(memory_space=pltpu.HBM)] * 2, *vmem(4)),
        scratch_shapes=[
            pltpu.VMEM((RIM, L, 8, 128), F32),
            pltpu.VMEM((RIM, L, 8, 128), F32),
            pltpu.SemaphoreType.DMA((2,)),
        ],
        compiler_params=params(24),
        name="turn",
    )(*arrays)


def corner_kernel(source, from_left, from_right, after, to_next, to_prev):
    low = iota((8, 128), 1) < 64
    for i in range(BHALO):
        for t in range(2):
            part = pl.ds(128 * t, 128)
            to_next[2 * i + t] = source[ROWS - BHALO + i, :, part]
            to_prev[2 * i + t] = source[i, :, part]
    for j in range(SIDE):
        a, b = from_left[j], from_right[j]
        to_next[2 * BHALO + j] = jnp.where(low, lanes(a, 64), b)
        to_prev[2 * BHALO + j] = jnp.where(low, a, lanes(b, 64))


def corners(*arrays):
    outs = (shaped(CORNER, 8, 128), shaped(CORNER, 8, 128))
    return pl.pallas_call(
        corner_kernel,
        out_shape=outs,
        in_specs=vmem(3) + [pl.BlockSpec(memory_space=pl.ANY)],
        out_specs=tuple(vmem(2)),
        compiler_params=params(16),
        name="corners",
    )(*arrays)


def inside(axis):
    at, count = lax.axis_index(axis), lax.axis_size(axis)
    return jnp.where(at > 0, 1.0, 0.0), jnp.where(at < count - 1, 1.0, 0.0)


def side_mask(lane):
    has_left, has_right = inside("gy")
    return jnp.where(lane < 8, has_right, jnp.where(lane >= 120, has_left, 0.0))


def halo_tile(from_left, from_right, lane, at_left, at_right):
    tile = jnp.where(lane < 8, lanes(from_right, -at_right), 0.0)
    return jnp.where(lane >= 120, lanes(from_left, 120 - at_left), tile)


def own(v):
    return v[:, :COLS]


def local_terms(q, k):
    bend = jnp.tanh(q)
    s = 0.5 + 0.5 * bend
    m = k * (0.1 + 0.9 * s)
    return bend, jnp.where(m > 0.0, 0.5 / m, OUTSIDE), 1.4 * s * (1.0 - s) + STORE


def blocks(rows, block, row, carry=None):
    def step(i, held):
        for j in range(block):
            held = row(rows[0] + i * block + j, held)
        return held

    return lax.fori_loop(0, (rows[1] - rows[0]) // block, step, carry)


def couplings(q, resist, cx, cy, cyl, cz, diag, rows, block, emit):
    last = iota((8, XC), 0) == 7

    def row(r, carry):
        q_0, m_0, q_7, m_7 = q[r, 0], resist[r, 0], q[r, 7], resist[r, 7]
        c_7 = jnp.where(last, 0.0, 1.0 / (m_7 + deeper(m_0)))
        f_7 = c_7 * (q_7 - deeper(q_0) + GRAV)
        cz[r, 7] = c_7
        c_up, f_up = higher(c_7), higher(f_7)
        v, m = q_0, m_0
        for l in range(L):
            if l < L - 1:
                m_n, v_n = resist[r, l + 1], q[r, l + 1]
                c = 1.0 / (m + m_n)
                f = c * (v - v_n + GRAV)
                cz[r, l] = c
            else:
                c, f = c_7, f_7
            y = 1.0 / (m + right(m))
            yl = 1.0 / (m + left(m))
            x = 1.0 / (m + resist[r + 1, l])
            xp = cx[r - 1, l]
            cy[r, l] = y
            cyl[r, l] = yl
            cx[r, l] = x
            out = y * (v - right(v)) + yl * (v - left(v))
            out = out + (x * (v - q[r + 1, l]) + xp * (v - q[r - 1, l])) + (f - f_up)
            diag[r, l] = diag[r, l] + ((y + yl) + (x + xp) + (c + c_up))
            emit(r, l, out)
            c_up, f_up = c, f
            if l < L - 1:
                v, m = v_n, m_n
        return carry

    for l in range(L):
        cx[rows[0] - 1, l] = 1.0 / (resist[rows[0] - 1, l] + resist[rows[0], l])
    blocks(rows, block, row, 0)


def apply(v_in, v_out, coefs, shift, rows, block, held, counted):
    cx, cy, cyl, cz, diag = coefs

    def row(r, held):
        at = r - shift
        c_up, v_up = higher(cz[at, 7]), higher(v_in[r, 7])
        v_0 = v_in[r, 0]
        v = v_0
        square, cross = held
        for l in range(L):
            v_n = v_in[r, l + 1] if l < L - 1 else deeper(v_0)
            c = cz[at, l]
            image = diag[at, l] * v - cy[at, l] * right(v) - cyl[at, l] * left(v)
            image = image - cx[at, l] * v_in[r + 1, l] - cx[at - 1, l] * v_in[r - 1, l]
            image = image - c * v_n - c_up * v_up
            if v_out is not None:
                v_out[r, l] = image
            if counted:
                a, b = own(v), own(image)
                square = square + a * a
                cross = cross + a * b
            v_up, c_up, v = v, c, v_n
        return square, cross

    return blocks(rows, block, row, held)


def write_moments(sums, moments):
    row = jnp.zeros((1, 128), F32)
    lane = iota((1, 128), 1)
    for k, held in enumerate(sums):
        value = jnp.sum(jnp.sum(held, axis=0, keepdims=True), axis=1, keepdims=True)
        row = jnp.where(lane == k, value, row)
    moments[...] = jnp.broadcast_to(row, moments.shape)


def no_sums():
    zero = jnp.zeros((8, COLS), F32)
    return zero, zero


def coefficients(gathered):
    row = jnp.sum(gathered[...], axis=0, keepdims=True)
    lane = iota((1, 128), 1)
    m = [jnp.sum(jnp.where(lane == k, row, 0.0), axis=1, keepdims=True) for k in range(6)]

    def dot(a, b, shift):
        total = jnp.zeros((1, 1), F32)
        for i, p in enumerate(a):
            for j, q in enumerate(b):
                total = total + p * q * m[i + j + shift]
        return total

    one = jnp.ones((1, 1), F32)
    a0 = m[0] / m[1]
    r1 = [one, -a0]
    n1 = dot(r1, r1, 0)
    b0 = n1 / m[0]
    p1 = [one + b0, -a0]
    a1 = n1 / dot(p1, p1, 1)
    r2 = [one, -a0 - a1 * p1[0], -a1 * p1[1]]
    n2 = dot(r2, r2, 0)
    b1 = n2 / n1
    p2 = [r2[0] + b1 * p1[0], r2[1] + b1 * p1[1], r2[2]]
    a2 = n2 / dot(p2, p2, 1)
    return (
        a0 + a1 * p1[0] + a2 * p2[0],
        a1 * p1[1] + a2 * p2[1],
        a2 * p2[2],
    )


def source_at(b, r, l, sub):
    return jnp.where(sub == 0, pltpu.roll(b[r], (8 - l) % 8, 0), 0.0)


def prepare_kernel(
    q_own, k_own, from_left, from_right,
    q, k, resist, cx, cy, cyl, cz, diag, base,
):
    lane = iota((8, 128), 1)
    keep = side_mask(lane)

    def fill(l, carry):
        for f, (field, target) in enumerate(((q_own, q), (k_own, k))):
            a, c = from_left[f * L + l], from_right[f * L + l]
            for x in range(ROWS):
                target[x, l, :, :COLS] = field[x, l]
                tile = halo_tile(a, c, lane, 8 * x, 8 * x)
                target[x, l, :, COLS:] = tile * keep if f == 1 else tile
        for x in range(ROWS):
            _, resist[x, l], diag[x, l] = local_terms(q[x, l], k[x, l])
        return carry

    lax.fori_loop(0, L, fill, 0)

    def emit(r, l, out):
        base[r, l] = -out

    couplings(q, resist, cx, cy, cyl, cz, diag, (1, ROWS - 1), 2, emit)


def prepare(*arrays):
    outs = (shaped(ROWS, L, 8, XC),) * 9
    return pl.pallas_call(
        prepare_kernel,
        out_shape=outs,
        in_specs=vmem(4),
        out_specs=tuple(vmem(9)),
        compiler_params=params(4),
        name="prepare",
    )(*arrays)


RSHIFT = 12
RROWS = 18


def first_kernel(
    q_mid, k_mid, resist_mid, cx_mid, cy_mid, cyl_mid, cz_mid, diag_mid, base,
    from_prev, from_next, source, corner_prev, corner_next, from_left, from_right,
    q, k, b, v0, v1, v2, moments,
    resist, cx, cy, cyl, cz, diag,
):
    lane = iota((8, 128), 1)
    keep = side_mask(lane)
    has_prev, has_next = inside("gx")

    def fill(l, carry):
        for f, target in enumerate((q, k)):
            at = 2 * BHALO + f * L + l
            for side, corner, r, spot, here in (
                (from_prev, corner_prev, 0, 8 * (8 - HALO), has_prev),
                (from_next, corner_next, HALO + ROWS - RSHIFT, 0, has_next),
            ):
                tile = corner[at]
                for i in range(HALO):
                    left_at = spot + 8 * i
                    row = [side[2 * (f * HALO + i) + t, l] for t in range(2)]
                    row.append(halo_tile(tile, tile, lane, left_at, 64 + left_at))
                    for t in range(3):
                        part = row[t]
                        if f == 1:
                            part = part * (here * keep if t == 2 else here)
                        target[r + i, l, :, 128 * t : 128 * t + 128] = part
        for r in (*range(HALO), *range(RROWS - HALO, RROWS)):
            _, resist[r, l], diag[r, l] = local_terms(q[r, l], k[r, l])
        for r, x in ((7, 0), (8, 1), (9, ROWS - 2), (10, ROWS - 1)):
            q[r, l] = q_mid[x, l]
            resist[r, l] = resist_mid[x, l]
            diag[r, l] = diag_mid[x, l]
        return carry

    lax.fori_loop(0, L, fill, 0)

    a, c = from_left[2 * L], from_right[2 * L]
    for x in range(ROWS):
        b[HALO + x, :, :COLS] = source[x]
        b[HALO + x, :, COLS:] = halo_tile(a, c, lane, 8 * x, 8 * x)
    for side, r, spot in (
        (corner_prev, HALO - BHALO, 8 * (8 - BHALO)),
        (corner_next, HALO + ROWS, 0),
    ):
        tile = side[CORNER - 1]
        for i in range(BHALO):
            for t in range(2):
                b[r + i, :, 128 * t : 128 * t + 128] = side[2 * i + t]
            left_at = spot + 8 * i
            b[r + i, :, COLS:] = halo_tile(tile, tile, lane, left_at, 64 + left_at)

    sub = iota((8, XC), 0)
    coefs = (cx, cy, cyl, cz, diag)
    mids = (cx_mid, cy_mid, cyl_mid, cz_mid, diag_mid)

    for shift, rows in ((0, (1, HALO + 1)), (RSHIFT, (RROWS - HALO - 1, RROWS - 1))):

        def emit(r, l, out, shift=shift):
            v0[r + shift, l] = source_at(b, r + shift, l, sub) - out

        couplings(q, resist, *coefs, rows, 1, emit)

    def inner(r, carry):
        for l in range(L):
            v0[r, l] = source_at(b, r, l, sub) + base[r - HALO, l]
        return carry

    low, high = HALO, HALO + ROWS - 1
    blocks((low + 1, high), 2, inner, 0)

    sums = []
    for v_in, v_out, deep in ((v0, v1, 5), (v1, v2, 4), (v2, None, 0)):
        held = apply(v_in, v_out, mids, HALO, (low + 1, high), 7, no_sums(), True)
        held = apply(v_in, v_out, coefs, 0, (low, low + 1), 1, held, True)
        held = apply(v_in, v_out, coefs, RSHIFT, (high, high + 1), 1, held, True)
        if deep:
            apply(v_in, v_out, coefs, 0, (low - deep, low), deep, no_sums(), False)
            apply(v_in, v_out, coefs, RSHIFT, (high + 1, high + 1 + deep), deep, no_sums(), False)
        sums += held
    write_moments(sums, moments)


def first_newton(*arrays):
    w = shaped(XR, L, 8, XC)
    rim = shaped(RROWS, L, 8, XC)
    outs = (rim, rim, shaped(XR, L, XC), w, w, w, shaped(128, 128))
    return pl.pallas_call(
        first_kernel,
        out_shape=outs,
        in_specs=vmem(len(arrays)),
        out_specs=tuple(vmem(len(outs))),
        scratch_shapes=[pltpu.VMEM((RROWS, L, 8, XC), F32)] * 6,
        compiler_params=params(14),
        name="first_newton",
    )(*arrays)


def second_kernel(
    q_mid, k_mid, q_rim, k_rim, b, u0, u1, u2, gathered,
    q_own, w0, w1, w2, moments,
    q1, resist, cx, cy, cyl, cz, diag, v0, v2,
):
    v1 = resist
    c0, c1, c2 = coefficients(gathered)
    sub = iota((8, XC), 0)

    for q, k, shift, rows in (
        (q_rim, k_rim, 0, (3, HALO)),
        (q_mid, k_mid, HALO, (HALO, HALO + ROWS)),
        (q_rim, k_rim, RSHIFT, (HALO + ROWS, XR - 3)),
    ):

        def update(r, carry, q=q, k=k, shift=shift):
            for l in range(L):
                old = q[r - shift, l]
                step = c0 * u0[r, l] + c1 * u1[r, l] + c2 * u2[r, l]
                new = old + step
                q1[r, l] = new
                bend, resist[r, l], diag[r, l] = local_terms(new, k[r - shift, l])
                stored = 0.35 * (bend - jnp.tanh(old)) + STORE * step
                v0[r, l] = source_at(b, r, l, sub) - stored
            return carry

        blocks(rows, 2, update, 0)

    def emit(r, l, out):
        v0[r, l] = v0[r, l] - out

    coefs = (cx, cy, cyl, cz, diag)
    couplings(q1, resist, *coefs, (4, XR - 4), 2, emit)
    low, high = HALO, HALO + ROWS
    sums = []
    for v_in, v_out, deep in ((v0, v1, 2), (v1, v2, 1), (v2, None, 0)):
        sums += apply(v_in, v_out, coefs, 0, (low, high), 8, no_sums(), True)
        if deep:
            apply(v_in, v_out, coefs, 0, (low - deep, low), deep, no_sums(), False)
            apply(v_in, v_out, coefs, 0, (high, high + deep), deep, no_sums(), False)
    write_moments(sums, moments)

    def keep(x, carry):
        for l in range(L):
            for source, target in ((q1, q_own), (v0, w0), (v1, w1), (v2, w2)):
                target[x, l] = source[HALO + x, l, :, :COLS]
        return carry

    lax.fori_loop(0, ROWS, keep, 0)


def second_newton(*arrays):
    o = shaped(ROWS, L, 8, COLS)
    outs = (o, o, o, o, shaped(128, 128))
    return pl.pallas_call(
        second_kernel,
        out_shape=outs,
        in_specs=vmem(len(arrays)),
        out_specs=tuple(vmem(len(outs))),
        scratch_shapes=[pltpu.VMEM((XR, L, 8, XC), F32)] * 9,
        compiler_params=params(28),
        name="second_newton",
    )(*arrays)


def final_kernel(q, v0, v1, v2, gathered, out, held, sems):
    c0, c1, c2 = coefficients(gathered)

    def send(l):
        part = pl.ds(32 * l, 32)
        return pltpu.make_async_copy(held.at[:, part], out.at[:, part], sems.at[l])

    for l in range(L):

        def row(x, carry, l=l):
            value = q[x, l] + c0 * v0[x, l] + c1 * v1[x, l] + c2 * v2[x, l]
            at = 32 * l + 16 * (x // 8) + x % 8
            held[:, at, :] = value[:, :128]
            held[:, at + 8, :] = value[:, 128:]
            return carry

        lax.fori_loop(0, ROWS, row, 0, unroll=4)
        send(l).start()
    for l in range(L):
        send(l).wait()


def final_update(*arrays):
    return pl.pallas_call(
        final_kernel,
        out_shape=shaped(8, 32 * L, 128),
        in_specs=vmem(len(arrays)),
        out_specs=pl.BlockSpec(memory_space=pltpu.HBM),
        scratch_shapes=[pltpu.VMEM((8, 32 * L, 128), F32), pltpu.SemaphoreType.DMA((L,))],
        compiler_params=params(4),
        name="final_update",
    )(*arrays)


def exchange(to_high, to_low, axis):
    count = lax.axis_size(axis)
    up = [(i, (i + 1) % count) for i in range(count)]
    down = [((i + 1) % count, i) for i in range(count)]
    return lax.ppermute(to_high, axis, up), lax.ppermute(to_low, axis, down)


def share(moments):
    return lax.all_to_all(moments, ("gx", "gy"), split_axis=0, concat_axis=0, tiled=True)


def body(
    pressure_old,
    conductivity,
    forcing,
    vegetated,
    cover_type,
    canopy_table,
    root_table,
    pair_counts,
    send_cols,
    canopy_state,
):
    owners = send_cols.shape[1]
    cols = in_hbm(send_cols.reshape(owners, 1, COLS))
    counts = in_hbm(pair_counts.reshape(owners))
    state = in_hbm(canopy_state.reshape(owners, 16, COLS))
    forcing, cover_type, vegetated = in_hbm(forcing), in_hbm(cover_type), in_hbm(vegetated)
    old, conductivity = in_hbm(flat(pressure_old)), in_hbm(flat(conductivity))
    canopy_table, root_table = in_hbm(canopy_table.T), in_hbm(root_table.T)

    payload, conductance = canopy_send(forcing, cover_type, canopy_table, counts, cols, state)
    arrived = lax.all_to_all(payload, "gx", split_axis=0, concat_axis=0, tiled=True)
    q_own, k_own, to_next, to_prev, edge_left, edge_right, uptake, surface = turn(
        old, conductivity, forcing, cover_type, vegetated, root_table, payload
    )
    to_next, to_prev, arrived = lax.optimization_barrier((to_next, to_prev, arrived))
    from_prev, from_next = exchange(to_next, to_prev, "gx")
    source, to_right, to_left = canopy_source(
        arrived, cols, counts, forcing, conductance, uptake, surface, edge_left, edge_right
    )
    from_left, from_right = exchange(to_right, to_left, "gy")
    new_state = owner_update(arrived, state)
    to_next, to_prev = corners(source, from_left, from_right, in_hbm(new_state))
    corner_prev, corner_next = exchange(to_next, to_prev, "gx")

    mids = prepare(q_own, k_own, from_left, from_right)
    q, k, b, v0, v1, v2, moments = first_newton(
        *mids, from_prev, from_next, source, corner_prev, corner_next, from_left, from_right
    )
    q1, w0, w1, w2, moments = second_newton(mids[0], mids[1], q, k, b, v0, v1, v2, share(moments))
    pressure = unflat(final_update(q1, w0, w1, w2, share(moments)))
    return pressure, new_state.reshape(canopy_state.shape)


def solution(mesh):
    placed = (
        P(None, "gx", "gy"),
        P(None, "gx", "gy"),
        P(None, "gx", "gy"),
        P("gx", "gy"),
        P("gx", "gy"),
        P(),
        P(),
        P("gx", None, "gy"),
        P("gx", None, "gy", None),
        P("gx", None, "gy", None, None),
    )
    return jax.shard_map(
        body,
        mesh=mesh,
        in_specs=placed,
        out_specs=(P(None, "gx", "gy"), P("gx", None, "gy", None, None)),
        check_vma=False,
    )
```

```python
import jax
import jax.numpy as jnp
from jax import lax
from jax.experimental import pallas as pl
from jax.experimental.pallas import tpu as pltpu
from jax.sharding import PartitionSpec as P

FORC = 8
ROOT = 8
LEV = 64
ROWS = 16
COLS = 256
L = 8
HALO = 7
NEAR = 4
FAR = HALO - NEAR
XR = ROWS + 2 * HALO
XC = 384
OUTSIDE = 1e37
BHALO = 6
SIDE = 2 * L + 1
CORNER = 2 * BHALO + SIDE
STORE = 0.05
GRAV = 0.5
F32 = jnp.float32
BF16 = jnp.bfloat16


def vmem(n=1):
    return [pl.BlockSpec(memory_space=pltpu.VMEM)] * n


def params(mib):
    return pltpu.CompilerParams(vmem_limit_bytes=mib * 1024 * 1024)


def work(micros):
    return pl.CostEstimate(flops=0, transcendentals=0, bytes_accessed=int(3e6 * micros))


def shaped(*shape):
    return jax.ShapeDtypeStruct(shape, F32)


def iota(shape, dim):
    return lax.broadcasted_iota(jnp.int32, shape, dim)


def right(v):
    return pltpu.roll(v, v.shape[1] - 1, 1)


def left(v):
    return pltpu.roll(v, 1, 1)


def deeper(v):
    return pltpu.roll(v, v.shape[0] - 1, 0)


def higher(v):
    return pltpu.roll(v, 1, 0)


def lanes(v, shift):
    return v if shift % 128 == 0 else pltpu.roll(v, shift % 128, v.ndim - 1)


def pieces(v):
    high = v.astype(BF16)
    rest = v - high.astype(F32)
    mid = rest.astype(BF16)
    low = (rest - mid.astype(F32)).astype(BF16)
    return high, mid, low


def in_hbm(v):
    return pltpu.with_memory_space_constraint(v, pltpu.HBM)


def smem():
    return pl.BlockSpec(memory_space=pltpu.SMEM)


def looked_up(kinds, table):
    found = [jnp.zeros(kinds.shape, F32) for _ in range(table.shape[0])]
    for kind in range(table.shape[1]):
        hit = kinds == kind
        for m in range(table.shape[0]):
            found[m] = jnp.where(hit, table[m, kind], found[m])
    return found


def hits(index):
    row = lax.shift_right_logical(index, 8)
    col = jnp.bitwise_and(index, COLS - 1)
    row_hit = iota((ROWS, COLS), 0) == row
    col_hit = iota((COLS, COLS), 0) == col
    return row_hit, jnp.where(col_hit, 1.0, 0.0).astype(BF16)


def canopy_send_kernel(
    forcing, cover, canopy_table, counts, cols, state, payload, conductance, split
):
    weights = looked_up(cover[...], canopy_table)
    total = weights[0] * forcing[0]
    for m in range(1, FORC):
        total = total + weights[m] * forcing[m]
    g = 2.0 * jax.nn.sigmoid(total)
    conductance[...] = g
    channels = [forcing[0], forcing[1], forcing[2], jnp.tanh(forcing[4]), g]
    used = len(channels)
    for c, channel in enumerate(channels):
        for p, piece in enumerate(pieces(channel)):
            split[pl.ds((p * used + c) * ROWS, ROWS), :] = piece

    def owner(o, carry):
        row_hit, onehot = hits(cols[o])
        picked = jnp.dot(split[...], onehot, preferred_element_type=F32)
        span = used * ROWS
        picked = picked[:span] + picked[span : 2 * span] + picked[2 * span :]
        sub = iota((8, COLS), 0)
        out = pltpu.roll(state[o, 0:8, :], 6, 0)
        for c in range(used):
            chosen = jnp.where(row_hit, picked[c * ROWS : (c + 1) * ROWS], 0.0)
            chosen = jnp.sum(chosen, axis=0, keepdims=True)
            out = jnp.where(sub == c, chosen, out)
        live = jnp.where(iota((8, COLS), 1) < counts[o], 1.0, 0.0)
        payload[o] = jnp.where(sub == used, live, out)
        return carry

    lax.fori_loop(0, cols.shape[0], owner, 0, unroll=8)


def canopy_send(forcing, cover, canopy_table, counts, cols, state):
    owners = cols.shape[0]
    return pl.pallas_call(
        canopy_send_kernel,
        out_shape=(shaped(owners, 8, COLS), shaped(ROWS, COLS)),
        in_specs=vmem(2) + [smem(), smem()] + vmem(2),
        out_specs=tuple(vmem(2)),
        scratch_shapes=[pltpu.VMEM((15 * ROWS, COLS), BF16)],
        compiler_params=params(16),
        cost_estimate=work(3),
        name="canopy_send",
    )(forcing, cover, canopy_table, counts, cols, state)


def softplus(v):
    return jnp.maximum(v, 0.0) + jnp.log1p(jnp.exp(-jnp.abs(v)))


def leaf(start, f0, f1, f2, g):
    temp = start
    for _ in range(3):
        temp = 0.5 * (start + f0) + 0.5 * jnp.tanh(f1 - g * (temp - f2))
    return temp


def source_kernel(
    arrived, cols, counts, forcing, conductance, uptake, surface, edge_left, edge_right,
    source, to_right, to_left, total, turned,
):
    total[...] = jnp.zeros_like(total)

    def owner(o, carry):
        row_hit, onehot = hits(cols[o])
        wanted = jnp.logical_and(row_hit, iota((ROWS, COLS), 1) < counts[o])
        block = arrived[o]
        parts = []
        for c in (6, 7):
            value = jnp.where(wanted, block[c : c + 1, :], 0.0)
            parts.extend(pieces(value))
        stacked = jnp.concatenate(parts, axis=0)
        total[...] += lax.dot_general(
            stacked, onehot, (((1,), (1,)), ((), ())), preferred_element_type=F32
        )
        return carry

    lax.fori_loop(0, cols.shape[0], owner, 0, unroll=8)

    def piece(k):
        return total[k * ROWS : (k + 1) * ROWS, :]

    water = piece(0) + piece(1) + piece(2)
    start = piece(3) + piece(4) + piece(5)
    g = conductance[...]
    temp = leaf(start, forcing[0], forcing[1], forcing[2], g)
    demand = g * softplus(temp - forcing[3]) / (1.0 + water * water)
    for m in range(ROOT):
        value = -(demand * uptake[m])
        if m == 0:
            value = value + surface[...]
        for t in range(2):
            turned[pl.ds(t * 128 + m * ROWS, ROWS), :] = value[:, t * 128 : t * 128 + 128]
    lane = iota((L, 128), 1)
    first = jnp.zeros((L, 128), F32)
    last = jnp.zeros((L, 128), F32)
    for x in range(ROWS):
        low = turned[pl.ds(x, L, stride=ROWS), :]
        high = turned[pl.ds(128 + x, L, stride=ROWS), :]
        source[x, :, :128] = low
        source[x, :, 128:] = high
        here = jnp.logical_and(lane >= 8 * x, lane < 8 * x + 8)
        first = jnp.where(here, lanes(low, 8 * x), first)
        last = jnp.where(here, lanes(high, 8 * x - 120), last)
    for target, edge, own_edge in ((to_left, edge_left, first), (to_right, edge_right, last)):
        target[0 : 2 * L] = edge[...]
        target[2 * L] = own_edge


def canopy_source(*arrays):
    v = vmem()[0]
    return pl.pallas_call(
        source_kernel,
        out_shape=(shaped(ROWS, ROOT, COLS), shaped(SIDE, L, 128), shaped(SIDE, L, 128)),
        in_specs=[v, v, smem(), v, v, v, v, v, v],
        out_specs=(v, v, v),
        scratch_shapes=[pltpu.VMEM((6 * ROWS, COLS), F32), pltpu.VMEM((2 * 128, 128), F32)],
        compiler_params=params(16),
        cost_estimate=work(2.5),
        name="canopy_source",
    )(*arrays)


def owner_kernel(arrived, state, updated):
    def slot(i, carry):
        block = arrived[i]
        old = state[i]
        temp = leaf(old[1:2], block[0:1], block[1:2], block[2:3], block[4:5])
        sub = iota(old.shape, 0)
        base = jnp.where(sub == 1, temp, old)
        upper = pltpu.roll(base, 1, 0)
        lower = pltpu.roll(base, base.shape[0] - 1, 0)
        lower = jnp.where(sub == base.shape[0] - 1, base, lower)
        fresh = 0.6 * base + 0.2 * upper + 0.2 * lower
        fresh = jnp.where(sub == 1, temp, fresh)
        fresh = jnp.where(sub == 0, 0.8 * old + 0.2 * block[3:4], fresh)
        updated[i] = jnp.where(block[5:6] > 0.5, fresh, old)
        return carry

    lax.fori_loop(0, arrived.shape[0], slot, 0, unroll=8)


def owner_update(arrived, state):
    return pl.pallas_call(
        owner_kernel,
        out_shape=shaped(*state.shape),
        in_specs=vmem(2),
        out_specs=vmem()[0],
        compiler_params=params(8),
        cost_estimate=work(2),
        name="owner_update",
    )(arrived, state)


def flat(v):
    return v.reshape(LEV, 2, 8, 2, 128).transpose(0, 1, 3, 2, 4).reshape(32 * LEV, 128)


def unflat(v):
    return v.reshape(LEV, 2, 2, 8, 128).transpose(0, 1, 3, 2, 4).reshape(LEV, ROWS, COLS)


def chunk(x, l, t):
    return pl.ds(32 * l + 16 * (x // 8) + 8 * t + x % 8, 8, stride=32 * L)


def rim_shape(rows):
    return 2 * rows * 2, L, 8, 128


def turn_kernel(
    pressure, conductivity, forcing, cover, vegetated, root_table, after,
    q, k, near_next, near_prev, far_next, far_prev, edge_left, edge_right, uptake, surface,
    near_next_rim, near_prev_rim, far_next_rim, far_prev_rim, sems,
):
    lane = iota((8, 128), 1)

    def layer(l, carry):
        for f, (field, target) in enumerate(((pressure, q), (conductivity, k))):
            first = jnp.zeros((8, 128), F32)
            last = jnp.zeros((8, 128), F32)
            for x in range(ROWS):
                for t in range(2):
                    part = field[chunk(x, l, t), :]
                    target[x, l, :, 128 * t : 128 * t + 128] = part
                    if x < NEAR:
                        near_prev_rim[2 * (f * NEAR + x) + t, l] = part
                    elif x < HALO:
                        far_prev_rim[2 * (f * FAR + x - NEAR) + t, l] = part
                    if x >= ROWS - NEAR:
                        near_next_rim[2 * (f * NEAR + x - ROWS + NEAR) + t, l] = part
                    elif x >= ROWS - HALO:
                        far_next_rim[2 * (f * FAR + x - ROWS + HALO) + t, l] = part
                    here = jnp.logical_and(lane >= 8 * x, lane < 8 * x + 8)
                    if t == 0:
                        first = jnp.where(here, lanes(part, 8 * x), first)
                    else:
                        last = jnp.where(here, lanes(part, 8 * x - 120), last)
            edge_left[f * L + l] = first
            edge_right[f * L + l] = last
        return carry

    lax.fori_loop(0, L, layer, 0)
    sends = [
        pltpu.make_async_copy(near_next_rim, near_next, sems.at[0]),
        pltpu.make_async_copy(near_prev_rim, near_prev, sems.at[1]),
        pltpu.make_async_copy(far_next_rim, far_next, sems.at[2]),
        pltpu.make_async_copy(far_prev_rim, far_prev, sems.at[3]),
    ]
    for send in sends:
        send.start()
    roots = looked_up(cover[...], root_table)
    planted = vegetated[...] == 1
    for m in range(ROOT):
        top = jnp.concatenate(
            [
                jnp.concatenate([pressure[pl.ds(32 * m + 16 * xt + 8 * t, 8), :] for t in range(2)], axis=1)
                for xt in range(2)
            ],
            axis=0,
        )
        moist = jax.nn.sigmoid(2.0 * (top + 1.5))
        uptake[m] = jnp.where(planted, roots[m] * moist, 0.0)
        if m == 0:
            evaporation = jnp.where(planted, 0.0, 0.5) * softplus(forcing[3] - forcing[2]) * moist
            surface[...] = 0.3 * softplus(forcing[4]) - evaporation
    for send in sends:
        send.wait()


def turn(*arrays):
    own_shape = shaped(ROWS, L, 8, COLS)
    near, far = rim_shape(NEAR), rim_shape(FAR)
    rims = (pltpu.HBM(near, F32), pltpu.HBM(near, F32), pltpu.HBM(far, F32), pltpu.HBM(far, F32))
    edge = shaped(2 * L, 8, 128)
    outs = (own_shape, own_shape, *rims, edge, edge, shaped(ROOT, ROWS, COLS), shaped(ROWS, COLS))
    return pl.pallas_call(
        turn_kernel,
        out_shape=outs,
        in_specs=vmem(5) + [smem(), pl.BlockSpec(memory_space=pl.ANY)],
        out_specs=(*vmem(2), *[pl.BlockSpec(memory_space=pltpu.HBM)] * 4, *vmem(4)),
        scratch_shapes=[pltpu.VMEM(shape, F32) for shape in (near, near, far, far)]
        + [pltpu.SemaphoreType.DMA((4,))],
        compiler_params=params(24),
        cost_estimate=work(4),
        name="turn",
    )(*arrays)


def corner_kernel(source, from_left, from_right, after, to_next, to_prev):
    low = iota((8, 128), 1) < 64
    for i in range(BHALO):
        for t in range(2):
            part = pl.ds(128 * t, 128)
            to_next[2 * i + t] = source[ROWS - BHALO + i, :, part]
            to_prev[2 * i + t] = source[i, :, part]
    for j in range(SIDE):
        a, b = from_left[j], from_right[j]
        to_next[2 * BHALO + j] = jnp.where(low, lanes(a, 64), b)
        to_prev[2 * BHALO + j] = jnp.where(low, a, lanes(b, 64))


def corners(*arrays):
    outs = (shaped(CORNER, 8, 128), shaped(CORNER, 8, 128))
    return pl.pallas_call(
        corner_kernel,
        out_shape=outs,
        in_specs=vmem(3) + [pl.BlockSpec(memory_space=pl.ANY)],
        out_specs=tuple(vmem(2)),
        compiler_params=params(16),
        cost_estimate=work(0.4),
        name="corners",
    )(*arrays)


def inside(axis):
    at, count = lax.axis_index(axis), lax.axis_size(axis)
    return jnp.where(at > 0, 1.0, 0.0), jnp.where(at < count - 1, 1.0, 0.0)


def side_mask(lane):
    has_left, has_right = inside("gy")
    return jnp.where(lane < 8, has_right, jnp.where(lane >= 120, has_left, 0.0))


def halo_tile(from_left, from_right, lane, at_left, at_right):
    tile = jnp.where(lane < 8, lanes(from_right, -at_right), 0.0)
    return jnp.where(lane >= 120, lanes(from_left, 120 - at_left), tile)


def own(v):
    return v[:, :COLS]


def local_terms(q, k):
    bend = jnp.tanh(q)
    s = 0.5 + 0.5 * bend
    m = k * (0.1 + 0.9 * s)
    return bend, jnp.where(m > 0.0, 0.5 / m, OUTSIDE), 1.4 * s * (1.0 - s) + STORE


def blocks(rows, block, row, carry=None):
    def step(i, held):
        for j in range(block):
            held = row(rows[0] + i * block + j, held)
        return held

    return lax.fori_loop(0, (rows[1] - rows[0]) // block, step, carry)


def couplings(q, resist, cx, cy, cyl, cz, diag, rows, block, emit):
    last = iota((8, XC), 0) == 7

    def row(r, carry):
        q_0, m_0, q_7, m_7 = q[r, 0], resist[r, 0], q[r, 7], resist[r, 7]
        c_7 = jnp.where(last, 0.0, 1.0 / (m_7 + deeper(m_0)))
        f_7 = c_7 * (q_7 - deeper(q_0) + GRAV)
        cz[r, 7] = c_7
        c_up, f_up = higher(c_7), higher(f_7)
        v, m = q_0, m_0
        for l in range(L):
            if l < L - 1:
                m_n, v_n = resist[r, l + 1], q[r, l + 1]
                c = 1.0 / (m + m_n)
                f = c * (v - v_n + GRAV)
                cz[r, l] = c
            else:
                c, f = c_7, f_7
            y = 1.0 / (m + right(m))
            yl = 1.0 / (m + left(m))
            x = 1.0 / (m + resist[r + 1, l])
            xp = cx[r - 1, l]
            cy[r, l] = y
            cyl[r, l] = yl
            cx[r, l] = x
            out = y * (v - right(v)) + yl * (v - left(v))
            out = out + (x * (v - q[r + 1, l]) + xp * (v - q[r - 1, l])) + (f - f_up)
            diag[r, l] = diag[r, l] + ((y + yl) + (x + xp) + (c + c_up))
            emit(r, l, out)
            c_up, f_up = c, f
            if l < L - 1:
                v, m = v_n, m_n
        return carry

    for l in range(L):
        cx[rows[0] - 1, l] = 1.0 / (resist[rows[0] - 1, l] + resist[rows[0], l])
    blocks(rows, block, row, 0)


def apply(v_in, v_out, coefs, shift, rows, block, held, counted):
    cx, cy, cyl, cz, diag = coefs

    def row(r, held):
        at = r - shift
        c_up, v_up = higher(cz[at, 7]), higher(v_in[r, 7])
        v_0 = v_in[r, 0]
        v = v_0
        square, cross = held
        for l in range(L):
            v_n = v_in[r, l + 1] if l < L - 1 else deeper(v_0)
            c = cz[at, l]
            image = diag[at, l] * v - cy[at, l] * right(v) - cyl[at, l] * left(v)
            image = image - cx[at, l] * v_in[r + 1, l] - cx[at - 1, l] * v_in[r - 1, l]
            image = image - c * v_n - c_up * v_up
            if v_out is not None:
                v_out[r, l] = image
            if counted:
                a, b = own(v), own(image)
                square = square + a * a
                cross = cross + a * b
            v_up, c_up, v = v, c, v_n
        return square, cross

    return blocks(rows, block, row, held)


def write_moments(sums, moments):
    row = jnp.zeros((1, 128), F32)
    lane = iota((1, 128), 1)
    for k, held in enumerate(sums):
        value = jnp.sum(jnp.sum(held, axis=0, keepdims=True), axis=1, keepdims=True)
        row = jnp.where(lane == k, value, row)
    moments[...] = jnp.broadcast_to(row, moments.shape)


def no_sums():
    zero = jnp.zeros((8, COLS), F32)
    return zero, zero


def coefficients(gathered):
    row = jnp.sum(gathered[...], axis=0, keepdims=True)
    lane = iota((1, 128), 1)
    m = [jnp.sum(jnp.where(lane == k, row, 0.0), axis=1, keepdims=True) for k in range(6)]

    def dot(a, b, shift):
        total = jnp.zeros((1, 1), F32)
        for i, p in enumerate(a):
            for j, q in enumerate(b):
                total = total + p * q * m[i + j + shift]
        return total

    one = jnp.ones((1, 1), F32)
    a0 = m[0] / m[1]
    r1 = [one, -a0]
    n1 = dot(r1, r1, 0)
    b0 = n1 / m[0]
    p1 = [one + b0, -a0]
    a1 = n1 / dot(p1, p1, 1)
    r2 = [one, -a0 - a1 * p1[0], -a1 * p1[1]]
    n2 = dot(r2, r2, 0)
    b1 = n2 / n1
    p2 = [r2[0] + b1 * p1[0], r2[1] + b1 * p1[1], r2[2]]
    a2 = n2 / dot(p2, p2, 1)
    return (
        a0 + a1 * p1[0] + a2 * p2[0],
        a1 * p1[1] + a2 * p2[1],
        a2 * p2[2],
    )


def source_at(b, r, l, sub):
    return jnp.where(sub == 0, pltpu.roll(b[r], (8 - l) % 8, 0), 0.0)


def prepare_kernel(
    q_own, k_own, from_left, from_right,
    q, k, resist, cx, cy, cyl, cz, diag, base,
):
    lane = iota((8, 128), 1)
    keep = side_mask(lane)

    def fill(l, carry):
        for f, (field, target) in enumerate(((q_own, q), (k_own, k))):
            a, c = from_left[f * L + l], from_right[f * L + l]
            for x in range(ROWS):
                target[x, l, :, :COLS] = field[x, l]
                tile = halo_tile(a, c, lane, 8 * x, 8 * x)
                target[x, l, :, COLS:] = tile * keep if f == 1 else tile
        for x in range(ROWS):
            _, resist[x, l], diag[x, l] = local_terms(q[x, l], k[x, l])
        return carry

    lax.fori_loop(0, L, fill, 0)

    def emit(r, l, out):
        base[r, l] = -out

    couplings(q, resist, cx, cy, cyl, cz, diag, (1, ROWS - 1), 2, emit)


def prepare(*arrays):
    outs = (shaped(ROWS, L, 8, XC),) * 9
    return pl.pallas_call(
        prepare_kernel,
        out_shape=outs,
        in_specs=vmem(4),
        out_specs=tuple(vmem(9)),
        compiler_params=params(4),
        cost_estimate=work(3.4),
        name="prepare",
    )(*arrays)


LSHIFT = 3
HSHIFT = 15
RROWS = 12


def rim_row(parts, lane, spot, inside_flags):
    low, high, corner = parts
    beside = halo_tile(corner, corner, lane, spot, 64 + spot)
    if inside_flags is not None:
        here, keep = inside_flags
        low, high, beside = low * here, high * here, beside * (here * keep)
    return jnp.concatenate([low, high, beside], axis=1)


def first_kernel(
    q_mid, k_mid, resist_mid, cx_mid, cy_mid, cyl_mid, cz_mid, diag_mid, base,
    from_prev, from_next, source, corner_prev, corner_next, from_left, from_right,
    q, k, b, v0, v1, v2, moments,
    resist, cx, cy, cyl, cz, diag,
):
    lane = iota((8, 128), 1)
    keep = side_mask(lane)
    has_prev, has_next = inside("gx")

    def fill(l, carry):
        for f, target in enumerate((q, k)):
            at = 2 * BHALO + f * L + l
            for side, corner, r, spot, here in (
                (from_prev, corner_prev, 0, 8 * (8 - NEAR), has_prev),
                (from_next, corner_next, RROWS - NEAR, 0, has_next),
            ):
                for i in range(NEAR):
                    parts = side[2 * (f * NEAR + i), l], side[2 * (f * NEAR + i) + 1, l], corner[at]
                    target[r + i, l] = rim_row(parts, lane, spot + 8 * i, (here, keep) if f == 1 else None)
        for r in (*range(NEAR), *range(RROWS - NEAR, RROWS)):
            _, resist[r, l], diag[r, l] = local_terms(q[r, l], k[r, l])
        for r, x in ((4, 0), (5, 1), (6, ROWS - 2), (7, ROWS - 1)):
            q[r, l] = q_mid[x, l]
            resist[r, l] = resist_mid[x, l]
            diag[r, l] = diag_mid[x, l]
        return carry

    lax.fori_loop(0, L, fill, 0)

    a, c = from_left[2 * L], from_right[2 * L]
    for x in range(ROWS):
        b[HALO + x, :, :COLS] = source[x]
        b[HALO + x, :, COLS:] = halo_tile(a, c, lane, 8 * x, 8 * x)
    for side, r, spot in (
        (corner_prev, HALO - BHALO, 8 * (8 - BHALO)),
        (corner_next, HALO + ROWS, 0),
    ):
        tile = side[CORNER - 1]
        for i in range(BHALO):
            for t in range(2):
                b[r + i, :, 128 * t : 128 * t + 128] = side[2 * i + t]
            left_at = spot + 8 * i
            b[r + i, :, COLS:] = halo_tile(tile, tile, lane, left_at, 64 + left_at)

    sub = iota((8, XC), 0)
    coefs = (cx, cy, cyl, cz, diag)
    mids = (cx_mid, cy_mid, cyl_mid, cz_mid, diag_mid)

    for shift, rows in ((LSHIFT, (1, NEAR + 1)), (HSHIFT, (RROWS - NEAR - 1, RROWS - 1))):

        def emit(r, l, out, shift=shift):
            v0[r + shift, l] = source_at(b, r + shift, l, sub) - out

        couplings(q, resist, *coefs, rows, 1, emit)

    def inner(r, carry):
        for l in range(L):
            v0[r, l] = source_at(b, r, l, sub) + base[r - HALO, l]
        return carry

    low, high = HALO, HALO + ROWS - 1
    blocks((low + 1, high), 2, inner, 0)

    sums = []
    for v_in, v_out, deep in ((v0, v1, 2), (v1, v2, 1), (v2, None, 0)):
        held = apply(v_in, v_out, mids, HALO, (low + 1, high), 7, no_sums(), True)
        held = apply(v_in, v_out, coefs, LSHIFT, (low, low + 1), 1, held, True)
        held = apply(v_in, v_out, coefs, HSHIFT, (high, high + 1), 1, held, True)
        if deep:
            apply(v_in, v_out, coefs, LSHIFT, (low - deep, low), deep, no_sums(), False)
            apply(v_in, v_out, coefs, HSHIFT, (high + 1, high + 1 + deep), deep, no_sums(), False)
        sums += held
    write_moments(sums, moments)


def first_newton(*arrays):
    w = shaped(XR, L, 8, XC)
    rim = shaped(RROWS, L, 8, XC)
    outs = (rim, rim, shaped(XR, L, XC), w, w, w, shaped(128, 128))
    return pl.pallas_call(
        first_kernel,
        out_shape=outs,
        in_specs=vmem(len(arrays)),
        out_specs=tuple(vmem(len(outs))),
        scratch_shapes=[pltpu.VMEM((RROWS, L, 8, XC), F32)] * 6,
        compiler_params=params(14),
        cost_estimate=work(7.5),
        name="first_newton",
    )(*arrays)


def second_kernel(
    q_mid, k_mid, q_rim, k_rim, b, u0, u1, u2, far_prev, far_next, corner_prev, corner_next, gathered,
    q_own, w0, w1, w2, moments,
    q1, resist, cx, cy, cyl, cz, diag, v0, v2,
):
    v1 = resist
    coefs = (cx, cy, cyl, cz, diag)
    sub = iota((8, XC), 0)

    lane = iota((8, 128), 1)
    keep = side_mask(lane)
    has_prev, has_next = inside("gx")

    def far_rows(l, carry):
        for side, corner, r, spot, here in (
            (far_prev, corner_prev, 0, 8 * (8 - HALO), has_prev),
            (far_next, corner_next, XR - FAR, 8 * NEAR, has_next),
        ):
            for i in range(FAR):
                row = []
                for f in range(2):
                    at = 2 * (f * FAR + i)
                    parts = side[at, l], side[at + 1, l], corner[2 * BHALO + f * L + l]
                    row.append(rim_row(parts, lane, spot + 8 * i, (here, keep) if f == 1 else None))
                q1[r + i, l] = row[0]
                _, resist[r + i, l], diag[r + i, l] = local_terms(*row)
        for r, shift in ((FAR, LSHIFT), (HALO + ROWS, HSHIFT)):
            for i in range(NEAR):
                old = q_rim[r + i - shift, l]
                q1[r + i, l] = old
                _, resist[r + i, l], diag[r + i, l] = local_terms(old, k_rim[r + i - shift, l])
        for r in (5, 6, XR - 7, XR - 6):
            v2[r, l] = u1[r, l]
        return carry

    lax.fori_loop(0, L, far_rows, 0)

    def far_right_hand(r, l, out):
        v0[r, l] = source_at(b, r, l, sub) - out

    for rows in ((1, 6), (XR - 6, XR - 1)):
        couplings(q1, resist, *coefs, rows, 1, far_right_hand)
    for v_in, v_out, r in ((v0, v2, 2), (v2, q1, 3)):
        for rows in ((r, r + 3), (XR - r - 3, XR - r)):
            apply(v_in, v_out, coefs, 0, rows, 3, no_sums(), False)

    c0, c1, c2 = coefficients(gathered)
    for q, k, shift, rows, block, held in (
        (q_rim, k_rim, LSHIFT, (3, 6), 3, (v0, v2, q1)),
        (q_rim, k_rim, LSHIFT, (6, 7), 1, (u0, u1, u2)),
        (q_mid, k_mid, HALO, (HALO, HALO + ROWS), 2, (u0, u1, u2)),
        (q_rim, k_rim, HSHIFT, (XR - 7, XR - 6), 1, (u0, u1, u2)),
        (q_rim, k_rim, HSHIFT, (XR - 6, XR - 3), 3, (v0, v2, q1)),
    ):

        def update(r, carry, q=q, k=k, shift=shift, held=held):
            for l in range(L):
                old = q[r - shift, l]
                step = c0 * held[0][r, l] + c1 * held[1][r, l] + c2 * held[2][r, l]
                new = old + step
                q1[r, l] = new
                bend, resist[r, l], diag[r, l] = local_terms(new, k[r - shift, l])
                stored = 0.35 * (bend - jnp.tanh(old)) + STORE * step
                v0[r, l] = source_at(b, r, l, sub) - stored
            return carry

        blocks(rows, block, update, 0)

    def emit(r, l, out):
        v0[r, l] = v0[r, l] - out

    couplings(q1, resist, *coefs, (4, XR - 4), 2, emit)
    low, high = HALO, HALO + ROWS
    sums = []
    for v_in, v_out, deep in ((v0, v1, 2), (v1, v2, 1), (v2, None, 0)):
        sums += apply(v_in, v_out, coefs, 0, (low, high), 8, no_sums(), True)
        if deep:
            apply(v_in, v_out, coefs, 0, (low - deep, low), deep, no_sums(), False)
            apply(v_in, v_out, coefs, 0, (high, high + deep), deep, no_sums(), False)
    write_moments(sums, moments)

    def keep(x, carry):
        for l in range(L):
            for source, target in ((q1, q_own), (v0, w0), (v1, w1), (v2, w2)):
                target[x, l] = source[HALO + x, l, :, :COLS]
        return carry

    lax.fori_loop(0, ROWS, keep, 0)


def second_newton(*arrays):
    o = shaped(ROWS, L, 8, COLS)
    outs = (o, o, o, o, shaped(128, 128))
    return pl.pallas_call(
        second_kernel,
        out_shape=outs,
        in_specs=vmem(len(arrays)),
        out_specs=tuple(vmem(len(outs))),
        scratch_shapes=[pltpu.VMEM((XR, L, 8, XC), F32)] * 9,
        compiler_params=params(30),
        cost_estimate=work(12),
        name="second_newton",
    )(*arrays)


def final_kernel(q, v0, v1, v2, gathered, out):
    c0, c1, c2 = coefficients(gathered)

    def row(x, carry):
        for l in range(L):
            value = q[x, l] + c0 * v0[x, l] + c1 * v1[x, l] + c2 * v2[x, l]
            out[chunk(x, l, 0), :] = value[:, :128]
            out[chunk(x, l, 1), :] = value[:, 128:]
        return carry

    lax.fori_loop(0, ROWS, row, 0, unroll=2)


def final_update(*arrays):
    return pl.pallas_call(
        final_kernel,
        out_shape=shaped(32 * LEV, 128),
        in_specs=vmem(len(arrays)),
        out_specs=vmem()[0],
        compiler_params=params(4),
        cost_estimate=work(2),
        name="final_update",
    )(*arrays)


def exchange(to_high, to_low, axis):
    count = lax.axis_size(axis)
    up = [(i, (i + 1) % count) for i in range(count)]
    down = [((i + 1) % count, i) for i in range(count)]
    return lax.ppermute(to_high, axis, up), lax.ppermute(to_low, axis, down)


def share(moments):
    return lax.all_to_all(moments, ("gx", "gy"), split_axis=0, concat_axis=0, tiled=True)


def body(
    pressure_old,
    conductivity,
    forcing,
    vegetated,
    cover_type,
    canopy_table,
    root_table,
    pair_counts,
    send_cols,
    canopy_state,
):
    owners = send_cols.shape[1]
    cols = in_hbm(send_cols.reshape(owners, 1, COLS))
    counts = in_hbm(pair_counts.reshape(owners))
    state = in_hbm(canopy_state.reshape(owners, 16, COLS))
    forcing, cover_type, vegetated = in_hbm(forcing), in_hbm(cover_type), in_hbm(vegetated)
    old, conductivity = in_hbm(flat(pressure_old)), in_hbm(flat(conductivity))
    canopy_table, root_table = in_hbm(canopy_table.T), in_hbm(root_table.T)

    payload, conductance = canopy_send(forcing, cover_type, canopy_table, counts, cols, state)
    arrived = lax.all_to_all(payload, "gx", split_axis=0, concat_axis=0, tiled=True)
    q_own, k_own, *rims, edge_left, edge_right, uptake, surface = turn(
        old, conductivity, forcing, cover_type, vegetated, root_table, payload
    )
    near_next, near_prev, far_next, far_prev, arrived = lax.optimization_barrier((*rims, arrived))
    near_prev, near_next = exchange(near_next, near_prev, "gx")
    source, to_right, to_left = canopy_source(
        arrived, cols, counts, forcing, conductance, uptake, surface, edge_left, edge_right
    )
    from_left, from_right = exchange(to_right, to_left, "gy")
    new_state = owner_update(arrived, state)
    to_next, to_prev = corners(source, from_left, from_right, in_hbm(new_state))
    corner_prev, corner_next = exchange(to_next, to_prev, "gx")
    far_next, far_prev, near_prev, near_next, corner_prev, corner_next = lax.optimization_barrier(
        (far_next, far_prev, near_prev, near_next, corner_prev, corner_next)
    )
    mids = prepare(q_own, k_own, from_left, from_right)
    far_prev, far_next = exchange(far_next, far_prev, "gx")
    q, k, b, v0, v1, v2, moments = first_newton(
        *mids, near_prev, near_next, source, corner_prev, corner_next, from_left, from_right
    )
    moments, far_prev, far_next = lax.optimization_barrier((moments, far_prev, far_next))
    q1, w0, w1, w2, moments = second_newton(
        mids[0], mids[1], q, k, b, v0, v1, v2, far_prev, far_next, corner_prev, corner_next, share(moments)
    )
    pressure = unflat(final_update(q1, w0, w1, w2, share(moments)))
    return pressure, new_state.reshape(canopy_state.shape)


def solution(mesh):
    placed = (
        P(None, "gx", "gy"),
        P(None, "gx", "gy"),
        P(None, "gx", "gy"),
        P("gx", "gy"),
        P("gx", "gy"),
        P(),
        P(),
        P("gx", None, "gy"),
        P("gx", None, "gy", None),
        P("gx", None, "gy", None, None),
    )
    return jax.shard_map(
        body,
        mesh=mesh,
        in_specs=placed,
        out_specs=(P(None, "gx", "gy"), P("gx", None, "gy", None, None)),
        check_vma=False,
    )
```

```python
import jax
import jax.numpy as jnp
from jax import lax
from jax.experimental import pallas as pl
from jax.experimental.pallas import tpu as pltpu
from jax.sharding import PartitionSpec as P

FORC = 8
ROOT = 8
LEV = 64
ROWS = 16
COLS = 256
L = 8
HALO = 7
XR = ROWS + 2 * HALO
XC = 384
OUTSIDE = 1e37
BHALO = 6
SIDE = 2 * L + 1
CORNER = 2 * BHALO + SIDE
STORE = 0.05
GRAV = 0.5
F32 = jnp.float32
BF16 = jnp.bfloat16


def vmem(n=1):
    return [pl.BlockSpec(memory_space=pltpu.VMEM)] * n


def params(mib):
    return pltpu.CompilerParams(vmem_limit_bytes=mib * 1024 * 1024)


def shaped(*shape):
    return jax.ShapeDtypeStruct(shape, F32)


def iota(shape, dim):
    return lax.broadcasted_iota(jnp.int32, shape, dim)


def right(v):
    return pltpu.roll(v, v.shape[1] - 1, 1)


def left(v):
    return pltpu.roll(v, 1, 1)


def deeper(v):
    return pltpu.roll(v, v.shape[0] - 1, 0)


def higher(v):
    return pltpu.roll(v, 1, 0)


def lanes(v, shift):
    return v if shift % 128 == 0 else pltpu.roll(v, shift % 128, v.ndim - 1)


def pieces(v):
    high = v.astype(BF16)
    rest = v - high.astype(F32)
    mid = rest.astype(BF16)
    low = (rest - mid.astype(F32)).astype(BF16)
    return high, mid, low


def in_hbm(v):
    return pltpu.with_memory_space_constraint(v, pltpu.HBM)


def smem():
    return pl.BlockSpec(memory_space=pltpu.SMEM)


def looked_up(kinds, table):
    found = [jnp.zeros(kinds.shape, F32) for _ in range(table.shape[0])]
    for kind in range(table.shape[1]):
        hit = kinds == kind
        for m in range(table.shape[0]):
            found[m] = jnp.where(hit, table[m, kind], found[m])
    return found


def hits(index):
    row = lax.shift_right_logical(index, 8)
    col = jnp.bitwise_and(index, COLS - 1)
    row_hit = iota((ROWS, COLS), 0) == row
    col_hit = iota((COLS, COLS), 0) == col
    return row_hit, jnp.where(col_hit, 1.0, 0.0).astype(BF16)


def canopy_send_kernel(
    forcing, cover, canopy_table, counts, cols, state, payload, conductance, split
):
    weights = looked_up(cover[...], canopy_table)
    total = weights[0] * forcing[0]
    for m in range(1, FORC):
        total = total + weights[m] * forcing[m]
    g = 2.0 * jax.nn.sigmoid(total)
    conductance[...] = g
    channels = [forcing[0], forcing[1], forcing[2], jnp.tanh(forcing[4]), g]
    used = len(channels)
    for c, channel in enumerate(channels):
        for p, piece in enumerate(pieces(channel)):
            split[pl.ds((p * used + c) * ROWS, ROWS), :] = piece

    def owner(o, carry):
        row_hit, onehot = hits(cols[o])
        picked = jnp.dot(split[...], onehot, preferred_element_type=F32)
        span = used * ROWS
        picked = picked[:span] + picked[span : 2 * span] + picked[2 * span :]
        sub = iota((8, COLS), 0)
        out = pltpu.roll(state[o, 0:8, :], 6, 0)
        for c in range(used):
            chosen = jnp.where(row_hit, picked[c * ROWS : (c + 1) * ROWS], 0.0)
            chosen = jnp.sum(chosen, axis=0, keepdims=True)
            out = jnp.where(sub == c, chosen, out)
        live = jnp.where(iota((8, COLS), 1) < counts[o], 1.0, 0.0)
        payload[o] = jnp.where(sub == used, live, out)
        return carry

    lax.fori_loop(0, cols.shape[0], owner, 0, unroll=8)


def canopy_send(forcing, cover, canopy_table, counts, cols, state):
    owners = cols.shape[0]
    return pl.pallas_call(
        canopy_send_kernel,
        out_shape=(shaped(owners, 8, COLS), shaped(ROWS, COLS)),
        in_specs=vmem(2) + [smem(), smem()] + vmem(2),
        out_specs=tuple(vmem(2)),
        scratch_shapes=[pltpu.VMEM((15 * ROWS, COLS), BF16)],
        compiler_params=params(16),
        name="canopy_send",
    )(forcing, cover, canopy_table, counts, cols, state)


def softplus(v):
    return jnp.maximum(v, 0.0) + jnp.log1p(jnp.exp(-jnp.abs(v)))


def leaf(start, f0, f1, f2, g):
    temp = start
    for _ in range(3):
        temp = 0.5 * (start + f0) + 0.5 * jnp.tanh(f1 - g * (temp - f2))
    return temp


def source_kernel(
    arrived, cols, counts, forcing, conductance, uptake, surface, edge_left, edge_right,
    source, to_right, to_left, total, turned,
):
    total[...] = jnp.zeros_like(total)

    def owner(o, carry):
        row_hit, onehot = hits(cols[o])
        wanted = jnp.logical_and(row_hit, iota((ROWS, COLS), 1) < counts[o])
        block = arrived[o]
        parts = []
        for c in (6, 7):
            value = jnp.where(wanted, block[c : c + 1, :], 0.0)
            parts.extend(pieces(value))
        stacked = jnp.concatenate(parts, axis=0)
        total[...] += lax.dot_general(
            stacked, onehot, (((1,), (1,)), ((), ())), preferred_element_type=F32
        )
        return carry

    lax.fori_loop(0, cols.shape[0], owner, 0, unroll=8)

    def piece(k):
        return total[k * ROWS : (k + 1) * ROWS, :]

    water = piece(0) + piece(1) + piece(2)
    start = piece(3) + piece(4) + piece(5)
    g = conductance[...]
    temp = leaf(start, forcing[0], forcing[1], forcing[2], g)
    demand = g * softplus(temp - forcing[3]) / (1.0 + water * water)
    for m in range(ROOT):
        value = -(demand * uptake[m])
        if m == 0:
            value = value + surface[...]
        for t in range(2):
            turned[pl.ds(t * 128 + m * ROWS, ROWS), :] = value[:, t * 128 : t * 128 + 128]
    lane = iota((L, 128), 1)
    first = jnp.zeros((L, 128), F32)
    last = jnp.zeros((L, 128), F32)
    for x in range(ROWS):
        low = turned[pl.ds(x, L, stride=ROWS), :]
        high = turned[pl.ds(128 + x, L, stride=ROWS), :]
        source[x, :, :128] = low
        source[x, :, 128:] = high
        here = jnp.logical_and(lane >= 8 * x, lane < 8 * x + 8)
        first = jnp.where(here, lanes(low, 8 * x), first)
        last = jnp.where(here, lanes(high, 8 * x - 120), last)
    for target, edge, own_edge in ((to_left, edge_left, first), (to_right, edge_right, last)):
        target[0 : 2 * L] = edge[...]
        target[2 * L] = own_edge


def canopy_source(*arrays):
    v = vmem()[0]
    return pl.pallas_call(
        source_kernel,
        out_shape=(shaped(ROWS, ROOT, COLS), shaped(SIDE, L, 128), shaped(SIDE, L, 128)),
        in_specs=[v, v, smem(), v, v, v, v, v, v],
        out_specs=(v, v, v),
        scratch_shapes=[pltpu.VMEM((6 * ROWS, COLS), F32), pltpu.VMEM((2 * 128, 128), F32)],
        compiler_params=params(16),
        name="canopy_source",
    )(*arrays)


def owner_kernel(arrived, state, updated):
    def slot(i, carry):
        block = arrived[i]
        old = state[i]
        temp = leaf(old[1:2], block[0:1], block[1:2], block[2:3], block[4:5])
        sub = iota(old.shape, 0)
        base = jnp.where(sub == 1, temp, old)
        upper = pltpu.roll(base, 1, 0)
        lower = pltpu.roll(base, base.shape[0] - 1, 0)
        lower = jnp.where(sub == base.shape[0] - 1, base, lower)
        fresh = 0.6 * base + 0.2 * upper + 0.2 * lower
        fresh = jnp.where(sub == 1, temp, fresh)
        fresh = jnp.where(sub == 0, 0.8 * old + 0.2 * block[3:4], fresh)
        updated[i] = jnp.where(block[5:6] > 0.5, fresh, old)
        return carry

    lax.fori_loop(0, arrived.shape[0], slot, 0, unroll=8)


def owner_update(arrived, state):
    return pl.pallas_call(
        owner_kernel,
        out_shape=shaped(*state.shape),
        in_specs=vmem(2),
        out_specs=vmem()[0],
        compiler_params=params(8),
        name="owner_update",
    )(arrived, state)


def flat(v):
    return v.reshape(LEV, 2, 8, 2, 128).transpose(0, 1, 3, 2, 4).reshape(32 * LEV, 128)


def unflat(v):
    return v.reshape(LEV, 2, 2, 8, 128).transpose(0, 1, 3, 2, 4).reshape(LEV, ROWS, COLS)


def chunk(x, l, t):
    return pl.ds(32 * l + 16 * (x // 8) + 8 * t + x % 8, 8, stride=32 * L)


RIM = 2 * HALO * 2


def turn_kernel(
    pressure, conductivity, forcing, cover, vegetated, root_table, after,
    q, k, to_next, to_prev, edge_left, edge_right, uptake, surface,
    next_rim, prev_rim, sems,
):
    lane = iota((8, 128), 1)

    def layer(l, carry):
        for f, (field, target) in enumerate(((pressure, q), (conductivity, k))):
            first = jnp.zeros((8, 128), F32)
            last = jnp.zeros((8, 128), F32)
            for x in range(ROWS):
                for t in range(2):
                    part = field[chunk(x, l, t), :]
                    target[x, l, :, 128 * t : 128 * t + 128] = part
                    if x < HALO:
                        prev_rim[2 * (f * HALO + x) + t, l] = part
                    if x >= ROWS - HALO:
                        next_rim[2 * (f * HALO + x - ROWS + HALO) + t, l] = part
                    here = jnp.logical_and(lane >= 8 * x, lane < 8 * x + 8)
                    if t == 0:
                        first = jnp.where(here, lanes(part, 8 * x), first)
                    else:
                        last = jnp.where(here, lanes(part, 8 * x - 120), last)
            edge_left[f * L + l] = first
            edge_right[f * L + l] = last
        return carry

    lax.fori_loop(0, L, layer, 0)
    sends = [
        pltpu.make_async_copy(next_rim, to_next, sems.at[0]),
        pltpu.make_async_copy(prev_rim, to_prev, sems.at[1]),
    ]
    for send in sends:
        send.start()
    roots = looked_up(cover[...], root_table)
    planted = vegetated[...] == 1
    for m in range(ROOT):
        top = jnp.concatenate(
            [
                jnp.concatenate([pressure[pl.ds(32 * m + 16 * xt + 8 * t, 8), :] for t in range(2)], axis=1)
                for xt in range(2)
            ],
            axis=0,
        )
        moist = jax.nn.sigmoid(2.0 * (top + 1.5))
        uptake[m] = jnp.where(planted, roots[m] * moist, 0.0)
        if m == 0:
            evaporation = jnp.where(planted, 0.0, 0.5) * softplus(forcing[3] - forcing[2]) * moist
            surface[...] = 0.3 * softplus(forcing[4]) - evaporation
    for send in sends:
        send.wait()


def turn(*arrays):
    own_shape = shaped(ROWS, L, 8, COLS)
    rim = pltpu.HBM((RIM, L, 8, 128), F32)
    edge = shaped(2 * L, 8, 128)
    outs = (own_shape, own_shape, rim, rim, edge, edge, shaped(ROOT, ROWS, COLS), shaped(ROWS, COLS))
    return pl.pallas_call(
        turn_kernel,
        out_shape=outs,
        in_specs=vmem(5) + [smem(), pl.BlockSpec(memory_space=pl.ANY)],
        out_specs=(*vmem(2), *[pl.BlockSpec(memory_space=pltpu.HBM)] * 2, *vmem(4)),
        scratch_shapes=[
            pltpu.VMEM((RIM, L, 8, 128), F32),
            pltpu.VMEM((RIM, L, 8, 128), F32),
            pltpu.SemaphoreType.DMA((2,)),
        ],
        compiler_params=params(24),
        name="turn",
    )(*arrays)


def corner_kernel(source, from_left, from_right, after, to_next, to_prev):
    low = iota((8, 128), 1) < 64
    for i in range(BHALO):
        for t in range(2):
            part = pl.ds(128 * t, 128)
            to_next[2 * i + t] = source[ROWS - BHALO + i, :, part]
            to_prev[2 * i + t] = source[i, :, part]
    for j in range(SIDE):
        a, b = from_left[j], from_right[j]
        to_next[2 * BHALO + j] = jnp.where(low, lanes(a, 64), b)
        to_prev[2 * BHALO + j] = jnp.where(low, a, lanes(b, 64))


def corners(*arrays):
    outs = (shaped(CORNER, 8, 128), shaped(CORNER, 8, 128))
    return pl.pallas_call(
        corner_kernel,
        out_shape=outs,
        in_specs=vmem(3) + [pl.BlockSpec(memory_space=pl.ANY)],
        out_specs=tuple(vmem(2)),
        compiler_params=params(16),
        name="corners",
    )(*arrays)


def inside(axis):
    at, count = lax.axis_index(axis), lax.axis_size(axis)
    return jnp.where(at > 0, 1.0, 0.0), jnp.where(at < count - 1, 1.0, 0.0)


def side_mask(lane):
    has_left, has_right = inside("gy")
    return jnp.where(lane < 8, has_right, jnp.where(lane >= 120, has_left, 0.0))


def halo_tile(from_left, from_right, lane, at_left, at_right):
    tile = jnp.where(lane < 8, lanes(from_right, -at_right), 0.0)
    return jnp.where(lane >= 120, lanes(from_left, 120 - at_left), tile)


def own(v):
    return v[:, :COLS]


def local_terms(q, k):
    bend = jnp.tanh(q)
    s = 0.5 + 0.5 * bend
    m = k * (0.1 + 0.9 * s)
    return bend, jnp.where(m > 0.0, 0.5 / m, OUTSIDE), 1.4 * s * (1.0 - s) + STORE


def blocks(rows, block, row, carry=None):
    def step(i, held):
        for j in range(block):
            held = row(rows[0] + i * block + j, held)
        return held

    return lax.fori_loop(0, (rows[1] - rows[0]) // block, step, carry)


def couplings(q, resist, cx, cy, cyl, cz, diag, rows, block, emit):
    last = iota((8, XC), 0) == 7

    def row(r, carry):
        q_0, m_0, q_7, m_7 = q[r, 0], resist[r, 0], q[r, 7], resist[r, 7]
        c_7 = jnp.where(last, 0.0, 1.0 / (m_7 + deeper(m_0)))
        f_7 = c_7 * (q_7 - deeper(q_0) + GRAV)
        cz[r, 7] = c_7
        c_up, f_up = higher(c_7), higher(f_7)
        v, m = q_0, m_0
        for l in range(L):
            if l < L - 1:
                m_n, v_n = resist[r, l + 1], q[r, l + 1]
                c = 1.0 / (m + m_n)
                f = c * (v - v_n + GRAV)
                cz[r, l] = c
            else:
                c, f = c_7, f_7
            y = 1.0 / (m + right(m))
            yl = 1.0 / (m + left(m))
            x = 1.0 / (m + resist[r + 1, l])
            xp = cx[r - 1, l]
            cy[r, l] = y
            cyl[r, l] = yl
            cx[r, l] = x
            out = y * (v - right(v)) + yl * (v - left(v))
            out = out + (x * (v - q[r + 1, l]) + xp * (v - q[r - 1, l])) + (f - f_up)
            diag[r, l] = diag[r, l] + ((y + yl) + (x + xp) + (c + c_up))
            emit(r, l, out)
            c_up, f_up = c, f
            if l < L - 1:
                v, m = v_n, m_n
        return carry

    for l in range(L):
        cx[rows[0] - 1, l] = 1.0 / (resist[rows[0] - 1, l] + resist[rows[0], l])
    blocks(rows, block, row, 0)


def apply(v_in, v_out, coefs, shift, rows, block, held, counted):
    cx, cy, cyl, cz, diag = coefs

    def row(r, held):
        at = r - shift
        c_up, v_up = higher(cz[at, 7]), higher(v_in[r, 7])
        v_0 = v_in[r, 0]
        v = v_0
        square, cross = held
        for l in range(L):
            v_n = v_in[r, l + 1] if l < L - 1 else deeper(v_0)
            c = cz[at, l]
            image = diag[at, l] * v - cy[at, l] * right(v) - cyl[at, l] * left(v)
            image = image - cx[at, l] * v_in[r + 1, l] - cx[at - 1, l] * v_in[r - 1, l]
            image = image - c * v_n - c_up * v_up
            if v_out is not None:
                v_out[r, l] = image
            if counted:
                a, b = own(v), own(image)
                square = square + a * a
                cross = cross + a * b
            v_up, c_up, v = v, c, v_n
        return square, cross

    return blocks(rows, block, row, held)


def write_moments(sums, moments):
    row = jnp.zeros((1, 128), F32)
    lane = iota((1, 128), 1)
    for k, held in enumerate(sums):
        value = jnp.sum(jnp.sum(held, axis=0, keepdims=True), axis=1, keepdims=True)
        row = jnp.where(lane == k, value, row)
    moments[...] = jnp.broadcast_to(row, moments.shape)


def no_sums():
    zero = jnp.zeros((8, COLS), F32)
    return zero, zero


def coefficients(gathered):
    row = jnp.sum(gathered[...], axis=0, keepdims=True)
    lane = iota((1, 128), 1)
    m = [jnp.sum(jnp.where(lane == k, row, 0.0), axis=1, keepdims=True) for k in range(6)]

    def dot(a, b, shift):
        total = jnp.zeros((1, 1), F32)
        for i, p in enumerate(a):
            for j, q in enumerate(b):
                total = total + p * q * m[i + j + shift]
        return total

    one = jnp.ones((1, 1), F32)
    a0 = m[0] / m[1]
    r1 = [one, -a0]
    n1 = dot(r1, r1, 0)
    b0 = n1 / m[0]
    p1 = [one + b0, -a0]
    a1 = n1 / dot(p1, p1, 1)
    r2 = [one, -a0 - a1 * p1[0], -a1 * p1[1]]
    n2 = dot(r2, r2, 0)
    b1 = n2 / n1
    p2 = [r2[0] + b1 * p1[0], r2[1] + b1 * p1[1], r2[2]]
    a2 = n2 / dot(p2, p2, 1)
    return (
        a0 + a1 * p1[0] + a2 * p2[0],
        a1 * p1[1] + a2 * p2[1],
        a2 * p2[2],
    )


def source_at(b, r, l, sub):
    return jnp.where(sub == 0, pltpu.roll(b[r], (8 - l) % 8, 0), 0.0)


def prepare_kernel(
    q_own, k_own, from_left, from_right, source,
    q, k, resist, cx, cy, cyl, cz, diag, v0, v1, v2, sums,
    b,
):
    lane = iota((8, 128), 1)
    keep = side_mask(lane)

    def fill(l, carry):
        for f, (field, target) in enumerate(((q_own, q), (k_own, k))):
            a, c = from_left[f * L + l], from_right[f * L + l]
            for x in range(ROWS):
                target[x, l, :, :COLS] = field[x, l]
                tile = halo_tile(a, c, lane, 8 * x, 8 * x)
                target[x, l, :, COLS:] = tile * keep if f == 1 else tile
        for x in range(ROWS):
            _, resist[x, l], diag[x, l] = local_terms(q[x, l], k[x, l])
        return carry

    lax.fori_loop(0, L, fill, 0)

    a, c = from_left[2 * L], from_right[2 * L]
    for x in range(ROWS):
        b[x, :, :COLS] = source[x]
        b[x, :, COLS:] = halo_tile(a, c, lane, 8 * x, 8 * x)
    sub = iota((8, XC), 0)

    def emit(r, l, out):
        v0[r, l] = source_at(b, r, l, sub) - out

    coefs = (cx, cy, cyl, cz, diag)
    couplings(q, resist, *coefs, (1, ROWS - 1), 2, emit)
    for step, (v_in, v_out, rows, block) in enumerate(
        ((v0, v1, (2, 14), 6), (v1, v2, (3, 13), 5), (v2, None, (4, 12), 8))
    ):
        held = apply(v_in, v_out, coefs, 0, rows, block, no_sums(), True)
        sums[2 * step], sums[2 * step + 1] = held


def prepare(*arrays):
    outs = (shaped(ROWS, L, 8, XC),) * 11 + (shaped(6, 8, COLS),)
    return pl.pallas_call(
        prepare_kernel,
        out_shape=outs,
        in_specs=vmem(len(arrays)),
        out_specs=tuple(vmem(len(outs))),
        scratch_shapes=[pltpu.VMEM((ROWS, L, XC), F32)],
        compiler_params=params(4),
        name="prepare",
    )(*arrays)


RSHIFT = 12
RROWS = 18


def first_kernel(
    q_mid, k_mid, resist_mid, cx_mid, cy_mid, cyl_mid, cz_mid, diag_mid, v0_mid, v1_mid, v2_mid, sums_mid,
    from_prev, from_next, source, corner_prev, corner_next, from_left, from_right,
    q, k, b, v0, v1, v2, moments,
    resist, cx, cy, cyl, cz, diag,
):
    lane = iota((8, 128), 1)
    keep = side_mask(lane)
    has_prev, has_next = inside("gx")

    def fill(l, carry):
        for f, target in enumerate((q, k)):
            at = 2 * BHALO + f * L + l
            for side, corner, r, spot, here in (
                (from_prev, corner_prev, 0, 8 * (8 - HALO), has_prev),
                (from_next, corner_next, HALO + ROWS - RSHIFT, 0, has_next),
            ):
                tile = corner[at]
                for i in range(HALO):
                    left_at = spot + 8 * i
                    row = [side[2 * (f * HALO + i) + t, l] for t in range(2)]
                    row.append(halo_tile(tile, tile, lane, left_at, 64 + left_at))
                    for t in range(3):
                        part = row[t]
                        if f == 1:
                            part = part * (here * keep if t == 2 else here)
                        target[r + i, l, :, 128 * t : 128 * t + 128] = part
        for r in (*range(HALO), *range(RROWS - HALO, RROWS)):
            _, resist[r, l], diag[r, l] = local_terms(q[r, l], k[r, l])
        for r, x in ((7, 0), (8, 1), (9, ROWS - 2), (10, ROWS - 1)):
            q[r, l] = q_mid[x, l]
            resist[r, l] = resist_mid[x, l]
            diag[r, l] = diag_mid[x, l]
        return carry

    lax.fori_loop(0, L, fill, 0)

    a, c = from_left[2 * L], from_right[2 * L]
    for x in range(ROWS):
        b[HALO + x, :, :COLS] = source[x]
        b[HALO + x, :, COLS:] = halo_tile(a, c, lane, 8 * x, 8 * x)
    for side, r, spot in (
        (corner_prev, HALO - BHALO, 8 * (8 - BHALO)),
        (corner_next, HALO + ROWS, 0),
    ):
        tile = side[CORNER - 1]
        for i in range(BHALO):
            for t in range(2):
                b[r + i, :, 128 * t : 128 * t + 128] = side[2 * i + t]
            left_at = spot + 8 * i
            b[r + i, :, COLS:] = halo_tile(tile, tile, lane, left_at, 64 + left_at)

    sub = iota((8, XC), 0)
    coefs = (cx, cy, cyl, cz, diag)
    mids = (cx_mid, cy_mid, cyl_mid, cz_mid, diag_mid)

    for shift, rows in ((0, (1, HALO + 1)), (RSHIFT, (RROWS - HALO - 1, RROWS - 1))):

        def emit(r, l, out, shift=shift):
            v0[r + shift, l] = source_at(b, r + shift, l, sub) - out

        couplings(q, resist, *coefs, rows, 1, emit)

    for mid, full, first in ((v0_mid, v0, 1), (v1_mid, v1, 2), (v2_mid, v2, 3)):
        for x in (first, first + 1, ROWS - 2 - first, ROWS - 1 - first):
            full[HALO + x] = mid[x]

    low, high = HALO, HALO + ROWS - 1
    sums = []
    for step, (v_in, v_out, deep) in enumerate(((v0, v1, 5), (v1, v2, 4), (v2, None, 0))):
        held = sums_mid[2 * step], sums_mid[2 * step + 1]
        more = step + 1
        for rows in ((low + 1, low + 1 + more), (high - more, high)):
            held = apply(v_in, v_out, mids, HALO, rows, more, held, True)
        held = apply(v_in, v_out, coefs, 0, (low, low + 1), 1, held, True)
        held = apply(v_in, v_out, coefs, RSHIFT, (high, high + 1), 1, held, True)
        if deep:
            apply(v_in, v_out, coefs, 0, (low - deep, low), deep, no_sums(), False)
            apply(v_in, v_out, coefs, RSHIFT, (high + 1, high + 1 + deep), deep, no_sums(), False)
        sums += held
    write_moments(sums, moments)


def first_newton(*arrays):
    w = shaped(XR, L, 8, XC)
    rim = shaped(RROWS, L, 8, XC)
    outs = (rim, rim, shaped(XR, L, XC), w, w, w, shaped(128, 128))
    return pl.pallas_call(
        first_kernel,
        out_shape=outs,
        in_specs=vmem(len(arrays)),
        out_specs=tuple(vmem(len(outs))),
        scratch_shapes=[pltpu.VMEM((RROWS, L, 8, XC), F32)] * 6,
        compiler_params=params(14),
        name="first_newton",
    )(*arrays)


def second_kernel(
    q_mid, k_mid, v0_mid, v1_mid, v2_mid, q_rim, k_rim, b, u0, u1, u2, gathered,
    q_own, p0, p1, p2, moments,
    q1, resist, cx, cy, cyl, cz, diag, v0, v2,
):
    v1 = resist
    c0, c1, c2 = coefficients(gathered)
    sub = iota((8, XC), 0)

    full, mid = (u0, u1, u2), (v0_mid, v1_mid, v2_mid)
    low, high = HALO, HALO + ROWS
    for q, k, shift, held, back, rows, block in (
        (q_rim, k_rim, 0, full, 0, (3, low), 2),
        (q_mid, k_mid, low, full, 0, (low, low + 3), 3),
        (q_mid, k_mid, low, mid, low, (low + 3, high - 3), 2),
        (q_mid, k_mid, low, full, 0, (high - 3, high), 3),
        (q_rim, k_rim, RSHIFT, full, 0, (high, XR - 3), 2),
    ):

        def update(r, carry, q=q, k=k, shift=shift, held=held, back=back):
            for l in range(L):
                old = q[r - shift, l]
                w0, w1, w2 = (w[r - back, l] for w in held)
                step = c0 * w0 + c1 * w1 + c2 * w2
                new = old + step
                q1[r, l] = new
                bend, resist[r, l], diag[r, l] = local_terms(new, k[r - shift, l])
                stored = 0.35 * (bend - jnp.tanh(old)) + STORE * step
                v0[r, l] = source_at(b, r, l, sub) - stored
            return carry

        blocks(rows, block, update, 0)

    def emit(r, l, out):
        v0[r, l] = v0[r, l] - out

    coefs = (cx, cy, cyl, cz, diag)
    couplings(q1, resist, *coefs, (4, XR - 4), 2, emit)
    sums = []
    for v_in, v_out, deep in ((v0, v1, 2), (v1, v2, 1), (v2, None, 0)):
        sums += apply(v_in, v_out, coefs, 0, (low, high), 8, no_sums(), True)
        if deep:
            apply(v_in, v_out, coefs, 0, (low - deep, low), deep, no_sums(), False)
            apply(v_in, v_out, coefs, 0, (high, high + deep), deep, no_sums(), False)
    write_moments(sums, moments)

    def keep(x, carry):
        for l in range(L):
            for source, target in ((q1, q_own), (v0, p0), (v1, p1), (v2, p2)):
                target[x, l] = source[HALO + x, l, :, :COLS]
        return carry

    lax.fori_loop(0, ROWS, keep, 0)


def second_newton(*arrays):
    o = shaped(ROWS, L, 8, COLS)
    outs = (o, o, o, o, shaped(128, 128))
    return pl.pallas_call(
        second_kernel,
        out_shape=outs,
        in_specs=vmem(len(arrays)),
        out_specs=tuple(vmem(len(outs))),
        scratch_shapes=[pltpu.VMEM((XR, L, 8, XC), F32)] * 9,
        compiler_params=params(28),
        name="second_newton",
    )(*arrays)


def final_kernel(q, v0, v1, v2, gathered, out):
    c0, c1, c2 = coefficients(gathered)

    def row(x, carry):
        for l in range(L):
            value = q[x, l] + c0 * v0[x, l] + c1 * v1[x, l] + c2 * v2[x, l]
            out[chunk(x, l, 0), :] = value[:, :128]
            out[chunk(x, l, 1), :] = value[:, 128:]
        return carry

    lax.fori_loop(0, ROWS, row, 0, unroll=2)


def final_update(*arrays):
    return pl.pallas_call(
        final_kernel,
        out_shape=shaped(32 * LEV, 128),
        in_specs=vmem(len(arrays)),
        out_specs=vmem()[0],
        compiler_params=params(4),
        name="final_update",
    )(*arrays)


def exchange(to_high, to_low, axis):
    count = lax.axis_size(axis)
    up = [(i, (i + 1) % count) for i in range(count)]
    down = [((i + 1) % count, i) for i in range(count)]
    return lax.ppermute(to_high, axis, up), lax.ppermute(to_low, axis, down)


def share(moments):
    return lax.all_to_all(moments, ("gx", "gy"), split_axis=0, concat_axis=0, tiled=True)


def body(
    pressure_old,
    conductivity,
    forcing,
    vegetated,
    cover_type,
    canopy_table,
    root_table,
    pair_counts,
    send_cols,
    canopy_state,
):
    owners = send_cols.shape[1]
    cols = in_hbm(send_cols.reshape(owners, 1, COLS))
    counts = in_hbm(pair_counts.reshape(owners))
    state = in_hbm(canopy_state.reshape(owners, 16, COLS))
    forcing, cover_type, vegetated = in_hbm(forcing), in_hbm(cover_type), in_hbm(vegetated)
    old, conductivity = in_hbm(flat(pressure_old)), in_hbm(flat(conductivity))
    canopy_table, root_table = in_hbm(canopy_table.T), in_hbm(root_table.T)

    payload, conductance = canopy_send(forcing, cover_type, canopy_table, counts, cols, state)
    arrived = lax.all_to_all(payload, "gx", split_axis=0, concat_axis=0, tiled=True)
    q_own, k_own, to_next, to_prev, edge_left, edge_right, uptake, surface = turn(
        old, conductivity, forcing, cover_type, vegetated, root_table, payload
    )
    to_next, to_prev, arrived = lax.optimization_barrier((to_next, to_prev, arrived))
    from_prev, from_next = exchange(to_next, to_prev, "gx")
    source, to_right, to_left = canopy_source(
        arrived, cols, counts, forcing, conductance, uptake, surface, edge_left, edge_right
    )
    from_left, from_right = exchange(to_right, to_left, "gy")
    new_state = owner_update(arrived, state)
    to_next, to_prev = corners(source, from_left, from_right, in_hbm(new_state))
    corner_prev, corner_next = exchange(to_next, to_prev, "gx")

    mids = prepare(q_own, k_own, from_left, from_right, source)
    q, k, b, v0, v1, v2, moments = first_newton(
        *mids, from_prev, from_next, source, corner_prev, corner_next, from_left, from_right
    )
    q1, w0, w1, w2, moments = second_newton(
        mids[0], mids[1], *mids[8:11], q, k, b, v0, v1, v2, share(moments)
    )
    pressure = unflat(final_update(q1, w0, w1, w2, share(moments)))
    return pressure, new_state.reshape(canopy_state.shape)


def solution(mesh):
    placed = (
        P(None, "gx", "gy"),
        P(None, "gx", "gy"),
        P(None, "gx", "gy"),
        P("gx", "gy"),
        P("gx", "gy"),
        P(),
        P(),
        P("gx", None, "gy"),
        P("gx", None, "gy", None),
        P("gx", None, "gy", None, None),
    )
    return jax.shard_map(
        body,
        mesh=mesh,
        in_specs=placed,
        out_specs=(P(None, "gx", "gy"), P("gx", None, "gy", None, None)),
        check_vma=False,
    )
```

```python
import jax
import jax.numpy as jnp
from jax import lax
from jax.experimental import pallas as pl
from jax.experimental.pallas import tpu as pltpu
from jax.sharding import PartitionSpec as P

FORC = 8
ROOT = 8
LEV = 64
ROWS = 16
COLS = 256
L = 8
HALO = 7
NEAR = 4
FAR = HALO - NEAR
XR = ROWS + 2 * HALO
XC = 384
OUTSIDE = 1e37
BHALO = 6
SIDE = 2 * L + 1
CORNER = 2 * BHALO + SIDE
STORE = 0.05
GRAV = 0.5
F32 = jnp.float32
BF16 = jnp.bfloat16


def vmem(n=1):
    return [pl.BlockSpec(memory_space=pltpu.VMEM)] * n


def params(mib):
    return pltpu.CompilerParams(vmem_limit_bytes=mib * 1024 * 1024)


def shaped(*shape):
    return jax.ShapeDtypeStruct(shape, F32)


def iota(shape, dim):
    return lax.broadcasted_iota(jnp.int32, shape, dim)


def right(v):
    return pltpu.roll(v, v.shape[1] - 1, 1)


def left(v):
    return pltpu.roll(v, 1, 1)


def deeper(v):
    return pltpu.roll(v, v.shape[0] - 1, 0)


def higher(v):
    return pltpu.roll(v, 1, 0)


def lanes(v, shift):
    return v if shift % 128 == 0 else pltpu.roll(v, shift % 128, v.ndim - 1)


def pieces(v):
    high = v.astype(BF16)
    rest = v - high.astype(F32)
    mid = rest.astype(BF16)
    low = (rest - mid.astype(F32)).astype(BF16)
    return high, mid, low


def in_hbm(v):
    return pltpu.with_memory_space_constraint(v, pltpu.HBM)


def smem():
    return pl.BlockSpec(memory_space=pltpu.SMEM)


def looked_up(kinds, table):
    found = [jnp.zeros(kinds.shape, F32) for _ in range(table.shape[0])]
    for kind in range(table.shape[1]):
        hit = kinds == kind
        for m in range(table.shape[0]):
            found[m] = jnp.where(hit, table[m, kind], found[m])
    return found


def hits(index):
    row = lax.shift_right_logical(index, 8)
    col = jnp.bitwise_and(index, COLS - 1)
    row_hit = iota((ROWS, COLS), 0) == row
    col_hit = iota((COLS, COLS), 0) == col
    return row_hit, jnp.where(col_hit, 1.0, 0.0).astype(BF16)


def canopy_send_kernel(
    forcing, cover, canopy_table, counts, cols, state, after, payload, conductance, split
):
    weights = looked_up(cover[...], canopy_table)
    total = weights[0] * forcing[0]
    for m in range(1, FORC):
        total = total + weights[m] * forcing[m]
    g = 2.0 * jax.nn.sigmoid(total)
    conductance[...] = g
    channels = [forcing[0], forcing[1], forcing[2], jnp.tanh(forcing[4]), g]
    used = len(channels)
    for c, channel in enumerate(channels):
        for p, piece in enumerate(pieces(channel)):
            split[pl.ds((p * used + c) * ROWS, ROWS), :] = piece

    def owner(o, carry):
        row_hit, onehot = hits(cols[o])
        picked = jnp.dot(split[...], onehot, preferred_element_type=F32)
        span = used * ROWS
        picked = picked[:span] + picked[span : 2 * span] + picked[2 * span :]
        sub = iota((8, COLS), 0)
        out = pltpu.roll(state[o, 0:8, :], 6, 0)
        for c in range(used):
            chosen = jnp.where(row_hit, picked[c * ROWS : (c + 1) * ROWS], 0.0)
            chosen = jnp.sum(chosen, axis=0, keepdims=True)
            out = jnp.where(sub == c, chosen, out)
        live = jnp.where(iota((8, COLS), 1) < counts[o], 1.0, 0.0)
        payload[o] = jnp.where(sub == used, live, out)
        return carry

    lax.fori_loop(0, cols.shape[0], owner, 0, unroll=8)


def canopy_send(forcing, cover, canopy_table, counts, cols, state, after):
    owners = cols.shape[0]
    return pl.pallas_call(
        canopy_send_kernel,
        out_shape=(shaped(owners, 8, COLS), shaped(ROWS, COLS)),
        in_specs=vmem(2) + [smem(), smem()] + vmem(2) + [pl.BlockSpec(memory_space=pl.ANY)],
        out_specs=tuple(vmem(2)),
        scratch_shapes=[pltpu.VMEM((15 * ROWS, COLS), BF16)],
        compiler_params=params(16),
        name="canopy_send",
    )(forcing, cover, canopy_table, counts, cols, state, after)


def softplus(v):
    return jnp.maximum(v, 0.0) + jnp.log1p(jnp.exp(-jnp.abs(v)))


def leaf(start, f0, f1, f2, g):
    temp = start
    for _ in range(3):
        temp = 0.5 * (start + f0) + 0.5 * jnp.tanh(f1 - g * (temp - f2))
    return temp


def source_kernel(
    arrived, cols, counts, forcing, conductance, uptake, surface, edge_left, edge_right,
    source, to_right, to_left, total, turned,
):
    total[...] = jnp.zeros_like(total)

    def owner(o, carry):
        row_hit, onehot = hits(cols[o])
        wanted = jnp.logical_and(row_hit, iota((ROWS, COLS), 1) < counts[o])
        block = arrived[o]
        parts = []
        for c in (6, 7):
            value = jnp.where(wanted, block[c : c + 1, :], 0.0)
            parts.extend(pieces(value))
        stacked = jnp.concatenate(parts, axis=0)
        total[...] += lax.dot_general(
            stacked, onehot, (((1,), (1,)), ((), ())), preferred_element_type=F32
        )
        return carry

    lax.fori_loop(0, cols.shape[0], owner, 0, unroll=8)

    def piece(k):
        return total[k * ROWS : (k + 1) * ROWS, :]

    water = piece(0) + piece(1) + piece(2)
    start = piece(3) + piece(4) + piece(5)
    g = conductance[...]
    temp = leaf(start, forcing[0], forcing[1], forcing[2], g)
    demand = g * softplus(temp - forcing[3]) / (1.0 + water * water)
    for m in range(ROOT):
        value = -(demand * uptake[m])
        if m == 0:
            value = value + surface[...]
        for t in range(2):
            turned[pl.ds(t * 128 + m * ROWS, ROWS), :] = value[:, t * 128 : t * 128 + 128]
    lane = iota((L, 128), 1)
    first = jnp.zeros((L, 128), F32)
    last = jnp.zeros((L, 128), F32)
    for x in range(ROWS):
        low = turned[pl.ds(x, L, stride=ROWS), :]
        high = turned[pl.ds(128 + x, L, stride=ROWS), :]
        source[x, :, :128] = low
        source[x, :, 128:] = high
        here = jnp.logical_and(lane >= 8 * x, lane < 8 * x + 8)
        first = jnp.where(here, lanes(low, 8 * x), first)
        last = jnp.where(here, lanes(high, 8 * x - 120), last)
    for target, edge, own_edge in ((to_left, edge_left, first), (to_right, edge_right, last)):
        target[0 : 2 * L] = edge[...]
        target[2 * L] = own_edge


def canopy_source(*arrays):
    v = vmem()[0]
    return pl.pallas_call(
        source_kernel,
        out_shape=(shaped(ROWS, ROOT, COLS), shaped(SIDE, L, 128), shaped(SIDE, L, 128)),
        in_specs=[v, v, smem(), v, v, v, v, v, v],
        out_specs=(v, v, v),
        scratch_shapes=[pltpu.VMEM((6 * ROWS, COLS), F32), pltpu.VMEM((2 * 128, 128), F32)],
        compiler_params=params(16),
        name="canopy_source",
    )(*arrays)


def owner_kernel(arrived, state, updated):
    def slot(i, carry):
        block = arrived[i]
        old = state[i]
        temp = leaf(old[1:2], block[0:1], block[1:2], block[2:3], block[4:5])
        sub = iota(old.shape, 0)
        base = jnp.where(sub == 1, temp, old)
        upper = pltpu.roll(base, 1, 0)
        lower = pltpu.roll(base, base.shape[0] - 1, 0)
        lower = jnp.where(sub == base.shape[0] - 1, base, lower)
        fresh = 0.6 * base + 0.2 * upper + 0.2 * lower
        fresh = jnp.where(sub == 1, temp, fresh)
        fresh = jnp.where(sub == 0, 0.8 * old + 0.2 * block[3:4], fresh)
        updated[i] = jnp.where(block[5:6] > 0.5, fresh, old)
        return carry

    lax.fori_loop(0, arrived.shape[0], slot, 0, unroll=8)


def owner_update(arrived, state):
    return pl.pallas_call(
        owner_kernel,
        out_shape=shaped(*state.shape),
        in_specs=vmem(2),
        out_specs=vmem()[0],
        compiler_params=params(8),
        name="owner_update",
    )(arrived, state)


def flat(v):
    return v.reshape(LEV, 2, 8, 2, 128).transpose(0, 1, 3, 2, 4).reshape(32 * LEV, 128)


def unflat(v):
    return v.reshape(LEV, 2, 2, 8, 128).transpose(0, 1, 3, 2, 4).reshape(LEV, ROWS, COLS)


def chunk(x, l, t):
    return pl.ds(32 * l + 16 * (x // 8) + 8 * t + x % 8, 8, stride=32 * L)


def rim_shape(rows):
    return 2 * rows * 2, L, 8, 128


def turn_kernel(
    pressure, conductivity,
    q, k, top, near_next, near_prev, far_next, far_prev,
    held_q, held_k, near_next_rim, near_prev_rim, far_next_rim, far_prev_rim, sems,
):
    fetches = []
    for l in range(L):
        part = pl.ds(32 * l, 32)
        for f, (field, held) in enumerate(((pressure, held_q), (conductivity, held_k))):
            fetches.append(pltpu.make_async_copy(field.at[:, part], held.at[:, part], sems.at[f, l]))
    for fetch in fetches:
        fetch.start()
    sends = []
    for l in range(L):
        fetches[2 * l].wait()
        fetches[2 * l + 1].wait()
        for f, (held, target) in enumerate(((held_q, q), (held_k, k))):
            for x in range(ROWS):
                for t in range(2):
                    part = held[:, 32 * l + 16 * (x // 8) + 8 * t + x % 8, :]
                    target[x, l, :, 128 * t : 128 * t + 128] = part
                    if x < NEAR:
                        near_prev_rim[2 * (f * NEAR + x) + t, l] = part
                    elif x < HALO:
                        far_prev_rim[2 * (f * FAR + x - NEAR) + t, l] = part
                    if x >= ROWS - NEAR:
                        near_next_rim[2 * (f * NEAR + x - ROWS + NEAR) + t, l] = part
                    elif x >= ROWS - HALO:
                        far_next_rim[2 * (f * FAR + x - ROWS + HALO) + t, l] = part
        if l % 4 == 3:
            part = pl.ds(l - 3, 4)
            for i, (rim, out) in enumerate(
                (
                    (far_next_rim, far_next),
                    (far_prev_rim, far_prev),
                    (near_next_rim, near_next),
                    (near_prev_rim, near_prev),
                )
            ):
                sends.append(pltpu.make_async_copy(rim.at[:, part], out.at[:, part], sems.at[2 + i, l]))
                sends[-1].start()
    for m in range(ROOT):
        for xt in range(2):
            for t in range(2):
                top[m, 8 * xt : 8 * xt + 8, 128 * t : 128 * t + 128] = held_q[
                    0, pl.ds(32 * m + 16 * xt + 8 * t, 8), :
                ]
    for send in sends:
        send.wait()


def turn(*arrays):
    own_shape = shaped(ROWS, L, 8, COLS)
    near, far = rim_shape(NEAR), rim_shape(FAR)
    rims = [pltpu.HBM(shape, F32) for shape in (near, near, far, far)]
    hbm = pl.BlockSpec(memory_space=pltpu.HBM)
    return pl.pallas_call(
        turn_kernel,
        out_shape=(own_shape, own_shape, shaped(ROOT, ROWS, COLS), *rims),
        in_specs=[hbm, hbm],
        out_specs=(*vmem(3), hbm, hbm, hbm, hbm),
        scratch_shapes=[
            pltpu.VMEM((8, 32 * L, 128), F32),
            pltpu.VMEM((8, 32 * L, 128), F32),
            *[pltpu.VMEM(shape, F32) for shape in (near, near, far, far)],
            pltpu.SemaphoreType.DMA((6, L)),
        ],
        compiler_params=params(8),
        name="turn",
    )(*arrays)


def sides_kernel(
    q, k, top, forcing, cover, vegetated, root_table, edge_left, edge_right, uptake, surface
):
    lane = iota((8, 128), 1)

    def layer(l, carry):
        for f, field in enumerate((q, k)):
            first = jnp.zeros((8, 128), F32)
            last = jnp.zeros((8, 128), F32)
            for x in range(ROWS):
                here = jnp.logical_and(lane >= 8 * x, lane < 8 * x + 8)
                first = jnp.where(here, lanes(field[x, l, :, :128], 8 * x), first)
                last = jnp.where(here, lanes(field[x, l, :, 128:], 8 * x - 120), last)
            edge_left[f * L + l] = first
            edge_right[f * L + l] = last
        return carry

    lax.fori_loop(0, L, layer, 0, unroll=4)
    roots = looked_up(cover[...], root_table)
    planted = vegetated[...] == 1
    for m in range(ROOT):
        moist = jax.nn.sigmoid(2.0 * (top[m] + 1.5))
        uptake[m] = jnp.where(planted, roots[m] * moist, 0.0)
        if m == 0:
            evaporation = jnp.where(planted, 0.0, 0.5) * softplus(forcing[3] - forcing[2]) * moist
            surface[...] = 0.3 * softplus(forcing[4]) - evaporation


def sides(*arrays):
    edge = shaped(2 * L, 8, 128)
    outs = (edge, edge, shaped(ROOT, ROWS, COLS), shaped(ROWS, COLS))
    return pl.pallas_call(
        sides_kernel,
        out_shape=outs,
        in_specs=vmem(6) + [smem()],
        out_specs=tuple(vmem(len(outs))),
        compiler_params=params(8),
        name="sides",
    )(*arrays)


def corner_kernel(source, from_left, from_right, after, to_next, to_prev):
    low = iota((8, 128), 1) < 64
    for i in range(BHALO):
        for t in range(2):
            part = pl.ds(128 * t, 128)
            to_next[2 * i + t] = source[ROWS - BHALO + i, :, part]
            to_prev[2 * i + t] = source[i, :, part]
    for j in range(SIDE):
        a, b = from_left[j], from_right[j]
        to_next[2 * BHALO + j] = jnp.where(low, lanes(a, 64), b)
        to_prev[2 * BHALO + j] = jnp.where(low, a, lanes(b, 64))


def corners(*arrays):
    outs = (shaped(CORNER, 8, 128), shaped(CORNER, 8, 128))
    return pl.pallas_call(
        corner_kernel,
        out_shape=outs,
        in_specs=vmem(3) + [pl.BlockSpec(memory_space=pl.ANY)],
        out_specs=tuple(vmem(2)),
        compiler_params=params(16),
        name="corners",
    )(*arrays)


def inside(axis):
    at, count = lax.axis_index(axis), lax.axis_size(axis)
    return jnp.where(at > 0, 1.0, 0.0), jnp.where(at < count - 1, 1.0, 0.0)


def side_mask(lane):
    has_left, has_right = inside("gy")
    return jnp.where(lane < 8, has_right, jnp.where(lane >= 120, has_left, 0.0))


def halo_tile(from_left, from_right, lane, at_left, at_right):
    tile = jnp.where(lane < 8, lanes(from_right, -at_right), 0.0)
    return jnp.where(lane >= 120, lanes(from_left, 120 - at_left), tile)


def own(v):
    return v[:, :COLS]


def local_terms(q, k):
    bend = jnp.tanh(q)
    s = 0.5 + 0.5 * bend
    m = k * (0.1 + 0.9 * s)
    return bend, jnp.where(m > 0.0, 0.5 / m, OUTSIDE), 1.4 * s * (1.0 - s) + STORE


def blocks(rows, block, row, carry=None):
    def step(i, held):
        for j in range(block):
            held = row(rows[0] + i * block + j, held)
        return held

    steps = (rows[1] - rows[0]) // block
    return step(0, carry) if steps == 1 else lax.fori_loop(0, steps, step, carry)


def couplings(q, resist, cx, cy, cyl, cz, diag, rows, block, emit):
    last = iota((8, XC), 0) == 7

    def row(r, carry):
        q_0, m_0, q_7, m_7 = q[r, 0], resist[r, 0], q[r, 7], resist[r, 7]
        c_7 = jnp.where(last, 0.0, 1.0 / (m_7 + deeper(m_0)))
        f_7 = c_7 * (q_7 - deeper(q_0) + GRAV)
        cz[r, 7] = c_7
        c_up, f_up = higher(c_7), higher(f_7)
        v, m = q_0, m_0
        for l in range(L):
            if l < L - 1:
                m_n, v_n = resist[r, l + 1], q[r, l + 1]
                c = 1.0 / (m + m_n)
                f = c * (v - v_n + GRAV)
                cz[r, l] = c
            else:
                c, f = c_7, f_7
            y = 1.0 / (m + right(m))
            yl = 1.0 / (m + left(m))
            x = 1.0 / (m + resist[r + 1, l])
            xp = cx[r - 1, l]
            cy[r, l] = y
            cyl[r, l] = yl
            cx[r, l] = x
            out = y * (v - right(v)) + yl * (v - left(v))
            out = out + (x * (v - q[r + 1, l]) + xp * (v - q[r - 1, l])) + (f - f_up)
            diag[r, l] = diag[r, l] + ((y + yl) + (x + xp) + (c + c_up))
            emit(r, l, out)
            c_up, f_up = c, f
            if l < L - 1:
                v, m = v_n, m_n
        return carry

    for l in range(L):
        cx[rows[0] - 1, l] = 1.0 / (resist[rows[0] - 1, l] + resist[rows[0], l])
    blocks(rows, block, row, 0)


def apply(v_in, v_out, coefs, shift, rows, block, held, counted):
    cx, cy, cyl, cz, diag = coefs

    def row(r, held):
        at = r - shift
        c_up, v_up = higher(cz[at, 7]), higher(v_in[r, 7])
        v_0 = v_in[r, 0]
        v = v_0
        square, cross = held
        for l in range(L):
            v_n = v_in[r, l + 1] if l < L - 1 else deeper(v_0)
            c = cz[at, l]
            image = diag[at, l] * v - cy[at, l] * right(v) - cyl[at, l] * left(v)
            image = image - cx[at, l] * v_in[r + 1, l] - cx[at - 1, l] * v_in[r - 1, l]
            image = image - c * v_n - c_up * v_up
            if v_out is not None:
                v_out[r, l] = image
            if counted:
                a, b = own(v), own(image)
                square = square + a * a
                cross = cross + a * b
            v_up, c_up, v = v, c, v_n
        return square, cross

    return blocks(rows, block, row, held)


def write_moments(sums, moments):
    row = jnp.zeros((1, 128), F32)
    lane = iota((1, 128), 1)
    for k, held in enumerate(sums):
        value = jnp.sum(jnp.sum(held, axis=0, keepdims=True), axis=1, keepdims=True)
        row = jnp.where(lane == k, value, row)
    moments[...] = jnp.broadcast_to(row, moments.shape)


def no_sums():
    zero = jnp.zeros((8, COLS), F32)
    return zero, zero


def coefficients(gathered):
    row = jnp.sum(gathered[...], axis=0, keepdims=True)
    lane = iota((1, 128), 1)
    m = [jnp.sum(jnp.where(lane == k, row, 0.0), axis=1, keepdims=True) for k in range(6)]

    def dot(a, b, shift):
        total = jnp.zeros((1, 1), F32)
        for i, p in enumerate(a):
            for j, q in enumerate(b):
                total = total + p * q * m[i + j + shift]
        return total

    one = jnp.ones((1, 1), F32)
    a0 = m[0] / m[1]
    r1 = [one, -a0]
    n1 = dot(r1, r1, 0)
    b0 = n1 / m[0]
    p1 = [one + b0, -a0]
    a1 = n1 / dot(p1, p1, 1)
    r2 = [one, -a0 - a1 * p1[0], -a1 * p1[1]]
    n2 = dot(r2, r2, 0)
    b1 = n2 / n1
    p2 = [r2[0] + b1 * p1[0], r2[1] + b1 * p1[1], r2[2]]
    a2 = n2 / dot(p2, p2, 1)
    return (
        a0 + a1 * p1[0] + a2 * p2[0],
        a1 * p1[1] + a2 * p2[1],
        a2 * p2[2],
    )


def source_at(b, r, l, sub):
    return jnp.where(sub == 0, pltpu.roll(b[r], (8 - l) % 8, 0), 0.0)


def prepare_kernel(
    q_own, k_own, from_left, from_right, source,
    q, k, resist, cx, cy, cyl, cz, diag, v0, v1, v2, sums,
    b,
):
    lane = iota((8, 128), 1)
    keep = side_mask(lane)

    def fill(l, carry):
        for f, (field, target) in enumerate(((q_own, q), (k_own, k))):
            a, c = from_left[f * L + l], from_right[f * L + l]
            for x in range(ROWS):
                target[x, l, :, :COLS] = field[x, l]
                tile = halo_tile(a, c, lane, 8 * x, 8 * x)
                target[x, l, :, COLS:] = tile * keep if f == 1 else tile
        for x in range(ROWS):
            _, resist[x, l], diag[x, l] = local_terms(q[x, l], k[x, l])
        return carry

    lax.fori_loop(0, L, fill, 0)

    a, c = from_left[2 * L], from_right[2 * L]
    for x in range(ROWS):
        b[x, :, :COLS] = source[x]
        b[x, :, COLS:] = halo_tile(a, c, lane, 8 * x, 8 * x)
    sub = iota((8, XC), 0)

    def emit(r, l, out):
        v0[r, l] = source_at(b, r, l, sub) - out

    coefs = (cx, cy, cyl, cz, diag)
    couplings(q, resist, *coefs, (1, ROWS - 1), 7, emit)
    for step, (v_in, v_out, rows, block) in enumerate(
        ((v0, v1, (2, 14), 6), (v1, v2, (3, 13), 5), (v2, None, (4, 12), 8))
    ):
        held = apply(v_in, v_out, coefs, 0, rows, block, no_sums(), True)
        sums[2 * step], sums[2 * step + 1] = held


def prepare(*arrays):
    outs = (shaped(ROWS, L, 8, XC),) * 11 + (shaped(6, 8, COLS),)
    return pl.pallas_call(
        prepare_kernel,
        out_shape=outs,
        in_specs=vmem(len(arrays)),
        out_specs=tuple(vmem(len(outs))),
        scratch_shapes=[pltpu.VMEM((ROWS, L, XC), F32)],
        compiler_params=params(4),
        name="prepare",
    )(*arrays)


RSHIFT = 12
RROWS = 18


def first_kernel(
    q_mid, k_mid, resist_mid, cx_mid, cy_mid, cyl_mid, cz_mid, diag_mid, v0_mid, v1_mid, v2_mid, sums_mid,
    near_prev, near_next, far_prev, far_next, source, corner_prev, corner_next, from_left, from_right,
    q, k, b, v0, v1, v2, moments,
    resist, cx, cy, cyl, cz, diag,
):
    lane = iota((8, 128), 1)
    keep = side_mask(lane)
    has_prev, has_next = inside("gx")

    def fill(l, carry):
        for f, target in enumerate((q, k)):
            at = 2 * BHALO + f * L + l
            for side, rows, corner, r, spot, here in (
                (far_prev, FAR, corner_prev, 0, 8 * (8 - HALO), has_prev),
                (near_prev, NEAR, corner_prev, FAR, 8 * (8 - NEAR), has_prev),
                (near_next, NEAR, corner_next, RROWS - HALO, 0, has_next),
                (far_next, FAR, corner_next, RROWS - FAR, 8 * NEAR, has_next),
            ):
                tile = corner[at]
                for i in range(rows):
                    left_at = spot + 8 * i
                    row = [side[2 * (f * rows + i) + t, l] for t in range(2)]
                    row.append(halo_tile(tile, tile, lane, left_at, 64 + left_at))
                    for t in range(3):
                        part = row[t]
                        if f == 1:
                            part = part * (here * keep if t == 2 else here)
                        target[r + i, l, :, 128 * t : 128 * t + 128] = part
        for r in (*range(HALO), *range(RROWS - HALO, RROWS)):
            _, resist[r, l], diag[r, l] = local_terms(q[r, l], k[r, l])
        for r, x in ((7, 0), (8, 1), (9, ROWS - 2), (10, ROWS - 1)):
            q[r, l] = q_mid[x, l]
            resist[r, l] = resist_mid[x, l]
            diag[r, l] = diag_mid[x, l]
        return carry

    lax.fori_loop(0, L, fill, 0)

    a, c = from_left[2 * L], from_right[2 * L]
    for x in range(ROWS):
        b[HALO + x, :, :COLS] = source[x]
        b[HALO + x, :, COLS:] = halo_tile(a, c, lane, 8 * x, 8 * x)
    for side, r, spot in (
        (corner_prev, HALO - BHALO, 8 * (8 - BHALO)),
        (corner_next, HALO + ROWS, 0),
    ):
        tile = side[CORNER - 1]
        for i in range(BHALO):
            for t in range(2):
                b[r + i, :, 128 * t : 128 * t + 128] = side[2 * i + t]
            left_at = spot + 8 * i
            b[r + i, :, COLS:] = halo_tile(tile, tile, lane, left_at, 64 + left_at)

    sub = iota((8, XC), 0)
    coefs = (cx, cy, cyl, cz, diag)
    mids = (cx_mid, cy_mid, cyl_mid, cz_mid, diag_mid)

    for shift, rows in ((0, (1, HALO + 1)), (RSHIFT, (RROWS - HALO - 1, RROWS - 1))):

        def emit(r, l, out, shift=shift):
            v0[r + shift, l] = source_at(b, r + shift, l, sub) - out

        couplings(q, resist, *coefs, rows, HALO, emit)

    for mid, full, first in ((v0_mid, v0, 1), (v1_mid, v1, 2), (v2_mid, v2, 3)):
        for x in (first, first + 1, ROWS - 2 - first, ROWS - 1 - first):
            full[HALO + x] = mid[x]

    low, high = HALO, HALO + ROWS - 1
    sums = []
    for step, (v_in, v_out, deep) in enumerate(((v0, v1, 5), (v1, v2, 4), (v2, None, 0))):
        held = sums_mid[2 * step], sums_mid[2 * step + 1]
        more = step + 1
        for rows in ((low + 1, low + 1 + more), (high - more, high)):
            held = apply(v_in, v_out, mids, HALO, rows, more, held, True)
        held = apply(v_in, v_out, coefs, 0, (low, low + 1), 1, held, True)
        held = apply(v_in, v_out, coefs, RSHIFT, (high, high + 1), 1, held, True)
        if deep:
            apply(v_in, v_out, coefs, 0, (low - deep, low), deep, no_sums(), False)
            apply(v_in, v_out, coefs, RSHIFT, (high + 1, high + 1 + deep), deep, no_sums(), False)
        sums += held
    write_moments(sums, moments)


def first_newton(*arrays):
    w = shaped(XR, L, 8, XC)
    rim = shaped(RROWS, L, 8, XC)
    outs = (rim, rim, shaped(XR, L, XC), w, w, w, shaped(128, 128))
    return pl.pallas_call(
        first_kernel,
        out_shape=outs,
        in_specs=vmem(len(arrays)),
        out_specs=tuple(vmem(len(outs))),
        scratch_shapes=[pltpu.VMEM((RROWS, L, 8, XC), F32)] * 6,
        compiler_params=params(14),
        name="first_newton",
    )(*arrays)


def second_kernel(
    q_mid, k_mid, v0_mid, v1_mid, v2_mid, q_rim, k_rim, b, u0, u1, u2, gathered,
    q_own, p0, p1, p2, moments,
    q1, resist, cx, cy, cyl, cz, diag, v0, v2,
):
    v1 = resist
    c0, c1, c2 = coefficients(gathered)
    sub = iota((8, XC), 0)

    full, mid = (u0, u1, u2), (v0_mid, v1_mid, v2_mid)
    low, high = HALO, HALO + ROWS
    for q, k, shift, held, back, rows, block in (
        (q_rim, k_rim, 0, full, 0, (3, low), 2),
        (q_mid, k_mid, low, full, 0, (low, low + 3), 3),
        (q_mid, k_mid, low, mid, low, (low + 3, high - 3), 2),
        (q_mid, k_mid, low, full, 0, (high - 3, high), 3),
        (q_rim, k_rim, RSHIFT, full, 0, (high, XR - 3), 2),
    ):

        def update(r, carry, q=q, k=k, shift=shift, held=held, back=back):
            for l in range(L):
                old = q[r - shift, l]
                w0, w1, w2 = (w[r - back, l] for w in held)
                step = c0 * w0 + c1 * w1 + c2 * w2
                new = old + step
                q1[r, l] = new
                bend, resist[r, l], diag[r, l] = local_terms(new, k[r - shift, l])
                stored = 0.35 * (bend - jnp.tanh(old)) + STORE * step
                v0[r, l] = source_at(b, r, l, sub) - stored
            return carry

        blocks(rows, block, update, 0)

    def emit(r, l, out):
        v0[r, l] = v0[r, l] - out

    coefs = (cx, cy, cyl, cz, diag)
    couplings(q1, resist, *coefs, (4, XR - 4), 11, emit)
    sums = []
    for v_in, v_out, deep in ((v0, v1, 2), (v1, v2, 1), (v2, None, 0)):
        sums += apply(v_in, v_out, coefs, 0, (low, high), 8, no_sums(), True)
        if deep:
            apply(v_in, v_out, coefs, 0, (low - deep, low), deep, no_sums(), False)
            apply(v_in, v_out, coefs, 0, (high, high + deep), deep, no_sums(), False)
    write_moments(sums, moments)

    def keep(x, carry):
        for l in range(L):
            for source, target in ((q1, q_own), (v0, p0), (v1, p1), (v2, p2)):
                target[x, l] = source[HALO + x, l, :, :COLS]
        return carry

    lax.fori_loop(0, ROWS, keep, 0)


def second_newton(*arrays):
    o = shaped(ROWS, L, 8, COLS)
    outs = (o, o, o, o, shaped(128, 128))
    return pl.pallas_call(
        second_kernel,
        out_shape=outs,
        in_specs=vmem(len(arrays)),
        out_specs=tuple(vmem(len(outs))),
        scratch_shapes=[pltpu.VMEM((XR, L, 8, XC), F32)] * 9,
        compiler_params=params(28),
        name="second_newton",
    )(*arrays)


def final_kernel(q, v0, v1, v2, gathered, out):
    c0, c1, c2 = coefficients(gathered)

    def row(x, carry):
        for l in range(L):
            value = q[x, l] + c0 * v0[x, l] + c1 * v1[x, l] + c2 * v2[x, l]
            out[chunk(x, l, 0), :] = value[:, :128]
            out[chunk(x, l, 1), :] = value[:, 128:]
        return carry

    lax.fori_loop(0, ROWS, row, 0, unroll=2)


def final_update(*arrays):
    return pl.pallas_call(
        final_kernel,
        out_shape=shaped(32 * LEV, 128),
        in_specs=vmem(len(arrays)),
        out_specs=vmem()[0],
        compiler_params=params(4),
        name="final_update",
    )(*arrays)


def exchange(to_high, to_low, axis):
    count = lax.axis_size(axis)
    up = [(i, (i + 1) % count) for i in range(count)]
    down = [((i + 1) % count, i) for i in range(count)]
    return lax.ppermute(to_high, axis, up), lax.ppermute(to_low, axis, down)


def share(moments):
    return lax.all_to_all(moments, ("gx", "gy"), split_axis=0, concat_axis=0, tiled=True)


def body(
    pressure_old,
    conductivity,
    forcing,
    vegetated,
    cover_type,
    canopy_table,
    root_table,
    pair_counts,
    send_cols,
    canopy_state,
):
    owners = send_cols.shape[1]
    cols = in_hbm(send_cols.reshape(owners, 1, COLS))
    counts = in_hbm(pair_counts.reshape(owners))
    state = in_hbm(canopy_state.reshape(owners, 16, COLS))
    forcing, cover_type, vegetated = in_hbm(forcing), in_hbm(cover_type), in_hbm(vegetated)
    old, conductivity = (in_hbm(flat(v).reshape(8, 32 * L, 128)) for v in (pressure_old, conductivity))
    canopy_table, root_table = in_hbm(canopy_table.T), in_hbm(root_table.T)

    q_own, k_own, top, near_next, near_prev, far_next, far_prev = turn(old, conductivity)
    far_prev, far_next = exchange(far_next, far_prev, "gx")
    payload, conductance = canopy_send(forcing, cover_type, canopy_table, counts, cols, state, top)
    arrived = lax.all_to_all(payload, "gx", split_axis=0, concat_axis=0, tiled=True)
    top, payload = lax.optimization_barrier((top, payload))
    edge_left, edge_right, uptake, surface = sides(
        q_own, k_own, top, forcing, cover_type, vegetated, root_table
    )
    near_next, near_prev, arrived, far_prev, far_next, surface = lax.optimization_barrier(
        (near_next, near_prev, arrived, far_prev, far_next, surface)
    )
    near_prev, near_next = exchange(near_next, near_prev, "gx")
    source, to_right, to_left = canopy_source(
        arrived, cols, counts, forcing, conductance, uptake, surface, edge_left, edge_right
    )
    from_left, from_right = exchange(to_right, to_left, "gy")
    new_state = owner_update(arrived, state)
    to_next, to_prev = corners(source, from_left, from_right, in_hbm(new_state))
    corner_prev, corner_next = exchange(to_next, to_prev, "gx")

    mids = prepare(q_own, k_own, from_left, from_right, source)
    q, k, b, v0, v1, v2, moments = first_newton(
        *mids, near_prev, near_next, far_prev, far_next, source, corner_prev, corner_next, from_left, from_right
    )
    q1, w0, w1, w2, moments = second_newton(
        mids[0], mids[1], *mids[8:11], q, k, b, v0, v1, v2, share(moments)
    )
    pressure = unflat(final_update(q1, w0, w1, w2, share(moments)))
    return pressure, new_state.reshape(canopy_state.shape)


def solution(mesh):
    placed = (
        P(None, "gx", "gy"),
        P(None, "gx", "gy"),
        P(None, "gx", "gy"),
        P("gx", "gy"),
        P("gx", "gy"),
        P(),
        P(),
        P("gx", None, "gy"),
        P("gx", None, "gy", None),
        P("gx", None, "gy", None, None),
    )
    return jax.shard_map(
        body,
        mesh=mesh,
        in_specs=placed,
        out_specs=(P(None, "gx", "gy"), P("gx", None, "gy", None, None)),
        check_vma=False,
    )
```

```python
import jax
import jax.numpy as jnp
from jax import lax
from jax.experimental import pallas as pl
from jax.experimental.pallas import tpu as pltpu
from jax.sharding import PartitionSpec as P

FORC = 8
ROOT = 8
LEV = 64
ROWS = 16
COLS = 256
L = 8
HALO = 7
NEAR = 4
FAR = HALO - NEAR
XR = ROWS + 2 * HALO
XC = 384
OUTSIDE = 1e37
BHALO = 6
SIDE = 2 * L + 1
CORNER = 2 * BHALO + SIDE
STORE = 0.05
GRAV = 0.5
F32 = jnp.float32
BF16 = jnp.bfloat16


def vmem(n=1):
    return [pl.BlockSpec(memory_space=pltpu.VMEM)] * n


def params(mib):
    return pltpu.CompilerParams(vmem_limit_bytes=mib * 1024 * 1024)


def shaped(*shape):
    return jax.ShapeDtypeStruct(shape, F32)


def iota(shape, dim):
    return lax.broadcasted_iota(jnp.int32, shape, dim)


def right(v):
    return pltpu.roll(v, v.shape[1] - 1, 1)


def left(v):
    return pltpu.roll(v, 1, 1)


def deeper(v):
    return pltpu.roll(v, v.shape[0] - 1, 0)


def higher(v):
    return pltpu.roll(v, 1, 0)


def lanes(v, shift):
    return v if shift % 128 == 0 else pltpu.roll(v, shift % 128, v.ndim - 1)


def pieces(v):
    high = v.astype(BF16)
    rest = v - high.astype(F32)
    mid = rest.astype(BF16)
    low = (rest - mid.astype(F32)).astype(BF16)
    return high, mid, low


def in_hbm(v):
    return pltpu.with_memory_space_constraint(v, pltpu.HBM)


def smem():
    return pl.BlockSpec(memory_space=pltpu.SMEM)


def looked_up(kinds, table):
    found = [jnp.zeros(kinds.shape, F32) for _ in range(table.shape[0])]
    for kind in range(table.shape[1]):
        hit = kinds == kind
        for m in range(table.shape[0]):
            found[m] = jnp.where(hit, table[m, kind], found[m])
    return found


def hits(index):
    row = lax.shift_right_logical(index, 8)
    col = jnp.bitwise_and(index, COLS - 1)
    row_hit = iota((ROWS, COLS), 0) == row
    col_hit = iota((COLS, COLS), 0) == col
    return row_hit, jnp.where(col_hit, 1.0, 0.0).astype(BF16)


def canopy_send_kernel(
    forcing, cover, canopy_table, counts, cols, state, after, payload, conductance, split
):
    weights = looked_up(cover[...], canopy_table)
    total = weights[0] * forcing[0]
    for m in range(1, FORC):
        total = total + weights[m] * forcing[m]
    g = 2.0 * jax.nn.sigmoid(total)
    conductance[...] = g
    channels = [forcing[0], forcing[1], forcing[2], jnp.tanh(forcing[4]), g]
    used = len(channels)
    for c, channel in enumerate(channels):
        for p, piece in enumerate(pieces(channel)):
            split[pl.ds((p * used + c) * ROWS, ROWS), :] = piece

    def owner(o, carry):
        row_hit, onehot = hits(cols[o])
        picked = jnp.dot(split[...], onehot, preferred_element_type=F32)
        span = used * ROWS
        picked = picked[:span] + picked[span : 2 * span] + picked[2 * span :]
        sub = iota((8, COLS), 0)
        out = pltpu.roll(state[o, 0:8, :], 6, 0)
        for c in range(used):
            chosen = jnp.where(row_hit, picked[c * ROWS : (c + 1) * ROWS], 0.0)
            chosen = jnp.sum(chosen, axis=0, keepdims=True)
            out = jnp.where(sub == c, chosen, out)
        live = jnp.where(iota((8, COLS), 1) < counts[o], 1.0, 0.0)
        payload[o] = jnp.where(sub == used, live, out)
        return carry

    lax.fori_loop(0, cols.shape[0], owner, 0, unroll=16)


def canopy_send(forcing, cover, canopy_table, counts, cols, state, after):
    owners = cols.shape[0]
    return pl.pallas_call(
        canopy_send_kernel,
        out_shape=(shaped(owners, 8, COLS), shaped(ROWS, COLS)),
        in_specs=vmem(2) + [smem(), smem()] + vmem(2) + [pl.BlockSpec(memory_space=pl.ANY)],
        out_specs=tuple(vmem(2)),
        scratch_shapes=[pltpu.VMEM((15 * ROWS, COLS), BF16)],
        compiler_params=params(16),
        name="canopy_send",
    )(forcing, cover, canopy_table, counts, cols, state, after)


def softplus(v):
    return jnp.maximum(v, 0.0) + jnp.log1p(jnp.exp(-jnp.abs(v)))


def leaf(start, f0, f1, f2, g):
    temp = start
    for _ in range(3):
        temp = 0.5 * (start + f0) + 0.5 * jnp.tanh(f1 - g * (temp - f2))
    return temp


def source_kernel(
    arrived, cols, counts, forcing, conductance, uptake, surface, edge_left, edge_right,
    source, to_right, to_left, total, turned,
):
    total[...] = jnp.zeros_like(total)

    def owner(o, carry):
        row_hit, onehot = hits(cols[o])
        wanted = jnp.logical_and(row_hit, iota((ROWS, COLS), 1) < counts[o])
        block = arrived[o]
        parts = []
        for c in (6, 7):
            value = jnp.where(wanted, block[c : c + 1, :], 0.0)
            parts.extend(pieces(value))
        stacked = jnp.concatenate(parts, axis=0)
        total[...] += lax.dot_general(
            stacked, onehot, (((1,), (1,)), ((), ())), preferred_element_type=F32
        )
        return carry

    lax.fori_loop(0, cols.shape[0], owner, 0, unroll=16)

    def piece(k):
        return total[k * ROWS : (k + 1) * ROWS, :]

    water = piece(0) + piece(1) + piece(2)
    start = piece(3) + piece(4) + piece(5)
    g = conductance[...]
    temp = leaf(start, forcing[0], forcing[1], forcing[2], g)
    demand = g * softplus(temp - forcing[3]) / (1.0 + water * water)
    for m in range(ROOT):
        value = -(demand * uptake[m])
        if m == 0:
            value = value + surface[...]
        for t in range(2):
            turned[pl.ds(t * 128 + m * ROWS, ROWS), :] = value[:, t * 128 : t * 128 + 128]
    lane = iota((L, 128), 1)
    first = jnp.zeros((L, 128), F32)
    last = jnp.zeros((L, 128), F32)
    for x in range(ROWS):
        low = turned[pl.ds(x, L, stride=ROWS), :]
        high = turned[pl.ds(128 + x, L, stride=ROWS), :]
        source[x, :, :128] = low
        source[x, :, 128:] = high
        here = jnp.logical_and(lane >= 8 * x, lane < 8 * x + 8)
        first = jnp.where(here, lanes(low, 8 * x), first)
        last = jnp.where(here, lanes(high, 8 * x - 120), last)
    for target, edge, own_edge in ((to_left, edge_left, first), (to_right, edge_right, last)):
        target[0 : 2 * L] = edge[...]
        target[2 * L] = own_edge


def canopy_source(*arrays):
    v = vmem()[0]
    return pl.pallas_call(
        source_kernel,
        out_shape=(shaped(ROWS, ROOT, COLS), shaped(SIDE, L, 128), shaped(SIDE, L, 128)),
        in_specs=[v, v, smem(), v, v, v, v, v, v],
        out_specs=(v, v, v),
        scratch_shapes=[pltpu.VMEM((6 * ROWS, COLS), F32), pltpu.VMEM((2 * 128, 128), F32)],
        compiler_params=params(16),
        name="canopy_source",
    )(*arrays)


def owner_kernel(arrived, state, updated):
    def slot(i, carry):
        block = arrived[i]
        old = state[i]
        temp = leaf(old[1:2], block[0:1], block[1:2], block[2:3], block[4:5])
        sub = iota(old.shape, 0)
        base = jnp.where(sub == 1, temp, old)
        upper = pltpu.roll(base, 1, 0)
        lower = pltpu.roll(base, base.shape[0] - 1, 0)
        lower = jnp.where(sub == base.shape[0] - 1, base, lower)
        fresh = 0.6 * base + 0.2 * upper + 0.2 * lower
        fresh = jnp.where(sub == 1, temp, fresh)
        fresh = jnp.where(sub == 0, 0.8 * old + 0.2 * block[3:4], fresh)
        updated[i] = jnp.where(block[5:6] > 0.5, fresh, old)
        return carry

    lax.fori_loop(0, arrived.shape[0], slot, 0, unroll=16)


def owner_update(arrived, state):
    return pl.pallas_call(
        owner_kernel,
        out_shape=shaped(*state.shape),
        in_specs=vmem(2),
        out_specs=vmem()[0],
        compiler_params=params(8),
        name="owner_update",
    )(arrived, state)


def flat(v):
    return v.reshape(LEV, 2, 8, 2, 128).transpose(0, 1, 3, 2, 4).reshape(32 * LEV, 128)


def unflat(v):
    return v.reshape(LEV, 2, 2, 8, 128).transpose(0, 1, 3, 2, 4).reshape(LEV, ROWS, COLS)


def chunk(x, l, t):
    return pl.ds(32 * l + 16 * (x // 8) + 8 * t + x % 8, 8, stride=32 * L)


def rim_shape(rows):
    return 2 * rows * 2, L, 8, 128


def turn_kernel(
    pressure, conductivity,
    q, k, top, near_next, near_prev, far_next, far_prev,
    held_q, held_k, near_next_rim, near_prev_rim, far_next_rim, far_prev_rim, sems,
):
    fetches = []
    for l in range(L):
        part = pl.ds(32 * l, 32)
        for f, (field, held) in enumerate(((pressure, held_q), (conductivity, held_k))):
            fetches.append(pltpu.make_async_copy(field.at[:, part], held.at[:, part], sems.at[f, l]))
    for fetch in fetches:
        fetch.start()
    sends = []
    for l in range(L):
        fetches[2 * l].wait()
        fetches[2 * l + 1].wait()
        for f, (held, target) in enumerate(((held_q, q), (held_k, k))):
            for x in range(ROWS):
                for t in range(2):
                    part = held[:, 32 * l + 16 * (x // 8) + 8 * t + x % 8, :]
                    target[x, l, :, 128 * t : 128 * t + 128] = part
                    if x < NEAR:
                        near_prev_rim[2 * (f * NEAR + x) + t, l] = part
                    elif x < HALO:
                        far_prev_rim[2 * (f * FAR + x - NEAR) + t, l] = part
                    if x >= ROWS - NEAR:
                        near_next_rim[2 * (f * NEAR + x - ROWS + NEAR) + t, l] = part
                    elif x >= ROWS - HALO:
                        far_next_rim[2 * (f * FAR + x - ROWS + HALO) + t, l] = part
        if l % 4 == 3:
            part = pl.ds(l - 3, 4)
            for i, (rim, out) in enumerate(
                (
                    (far_next_rim, far_next),
                    (far_prev_rim, far_prev),
                    (near_next_rim, near_next),
                    (near_prev_rim, near_prev),
                )
            ):
                sends.append(pltpu.make_async_copy(rim.at[:, part], out.at[:, part], sems.at[2 + i, l]))
                sends[-1].start()
    for m in range(ROOT):
        for xt in range(2):
            for t in range(2):
                top[m, 8 * xt : 8 * xt + 8, 128 * t : 128 * t + 128] = held_q[
                    0, pl.ds(32 * m + 16 * xt + 8 * t, 8), :
                ]
    for send in sends:
        send.wait()


def turn(*arrays):
    own_shape = shaped(ROWS, L, 8, COLS)
    near, far = rim_shape(NEAR), rim_shape(FAR)
    rims = [pltpu.HBM(shape, F32) for shape in (near, near, far, far)]
    hbm = pl.BlockSpec(memory_space=pltpu.HBM)
    return pl.pallas_call(
        turn_kernel,
        out_shape=(own_shape, own_shape, shaped(ROOT, ROWS, COLS), *rims),
        in_specs=[hbm, hbm],
        out_specs=(*vmem(3), hbm, hbm, hbm, hbm),
        scratch_shapes=[
            pltpu.VMEM((8, 32 * L, 128), F32),
            pltpu.VMEM((8, 32 * L, 128), F32),
            *[pltpu.VMEM(shape, F32) for shape in (near, near, far, far)],
            pltpu.SemaphoreType.DMA((6, L)),
        ],
        compiler_params=params(8),
        name="turn",
    )(*arrays)


def sides_kernel(
    q, k, top, forcing, cover, vegetated, root_table, edge_left, edge_right, uptake, surface
):
    lane = iota((8, 128), 1)

    def layer(l, carry):
        for f, field in enumerate((q, k)):
            first = jnp.zeros((8, 128), F32)
            last = jnp.zeros((8, 128), F32)
            for x in range(ROWS):
                here = jnp.logical_and(lane >= 8 * x, lane < 8 * x + 8)
                first = jnp.where(here, lanes(field[x, l, :, :128], 8 * x), first)
                last = jnp.where(here, lanes(field[x, l, :, 128:], 8 * x - 120), last)
            edge_left[f * L + l] = first
            edge_right[f * L + l] = last
        return carry

    lax.fori_loop(0, L, layer, 0, unroll=4)
    roots = looked_up(cover[...], root_table)
    planted = vegetated[...] == 1
    for m in range(ROOT):
        moist = jax.nn.sigmoid(2.0 * (top[m] + 1.5))
        uptake[m] = jnp.where(planted, roots[m] * moist, 0.0)
        if m == 0:
            evaporation = jnp.where(planted, 0.0, 0.5) * softplus(forcing[3] - forcing[2]) * moist
            surface[...] = 0.3 * softplus(forcing[4]) - evaporation


def sides(*arrays):
    edge = shaped(2 * L, 8, 128)
    outs = (edge, edge, shaped(ROOT, ROWS, COLS), shaped(ROWS, COLS))
    return pl.pallas_call(
        sides_kernel,
        out_shape=outs,
        in_specs=vmem(6) + [smem()],
        out_specs=tuple(vmem(len(outs))),
        compiler_params=params(8),
        name="sides",
    )(*arrays)


def corner_kernel(source, from_left, from_right, after, to_next, to_prev):
    low = iota((8, 128), 1) < 64
    for i in range(BHALO):
        for t in range(2):
            part = pl.ds(128 * t, 128)
            to_next[2 * i + t] = source[ROWS - BHALO + i, :, part]
            to_prev[2 * i + t] = source[i, :, part]
    for j in range(SIDE):
        a, b = from_left[j], from_right[j]
        to_next[2 * BHALO + j] = jnp.where(low, lanes(a, 64), b)
        to_prev[2 * BHALO + j] = jnp.where(low, a, lanes(b, 64))


def corners(*arrays):
    outs = (shaped(CORNER, 8, 128), shaped(CORNER, 8, 128))
    return pl.pallas_call(
        corner_kernel,
        out_shape=outs,
        in_specs=vmem(3) + [pl.BlockSpec(memory_space=pl.ANY)],
        out_specs=tuple(vmem(2)),
        compiler_params=params(16),
        name="corners",
    )(*arrays)


def inside(axis):
    at, count = lax.axis_index(axis), lax.axis_size(axis)
    return jnp.where(at > 0, 1.0, 0.0), jnp.where(at < count - 1, 1.0, 0.0)


def side_mask(lane):
    has_left, has_right = inside("gy")
    return jnp.where(lane < 8, has_right, jnp.where(lane >= 120, has_left, 0.0))


def halo_tile(from_left, from_right, lane, at_left, at_right):
    tile = jnp.where(lane < 8, lanes(from_right, -at_right), 0.0)
    return jnp.where(lane >= 120, lanes(from_left, 120 - at_left), tile)


def own(v):
    return v[:, :COLS]


def local_terms(q, k):
    bend = jnp.tanh(q)
    s = 0.5 + 0.5 * bend
    m = k * (0.1 + 0.9 * s)
    return bend, jnp.where(m > 0.0, 0.5 / m, OUTSIDE), 1.4 * s * (1.0 - s) + STORE


def blocks(rows, block, row, carry=None):
    def step(i, held):
        for j in range(block):
            held = row(rows[0] + i * block + j, held)
        return held

    steps = (rows[1] - rows[0]) // block
    return step(0, carry) if steps == 1 else lax.fori_loop(0, steps, step, carry)


def couplings(q, resist, cx, cy, cyl, cz, diag, rows, block, emit):
    last = iota((8, XC), 0) == 7

    def row(r, carry):
        q_0, m_0, q_7, m_7 = q[r, 0], resist[r, 0], q[r, 7], resist[r, 7]
        c_7 = jnp.where(last, 0.0, 1.0 / (m_7 + deeper(m_0)))
        f_7 = c_7 * (q_7 - deeper(q_0) + GRAV)
        cz[r, 7] = c_7
        c_up, f_up = higher(c_7), higher(f_7)
        v, m = q_0, m_0
        for l in range(L):
            if l < L - 1:
                m_n, v_n = resist[r, l + 1], q[r, l + 1]
                c = 1.0 / (m + m_n)
                f = c * (v - v_n + GRAV)
                cz[r, l] = c
            else:
                c, f = c_7, f_7
            y = 1.0 / (m + right(m))
            yl = 1.0 / (m + left(m))
            x = 1.0 / (m + resist[r + 1, l])
            xp = cx[r - 1, l]
            cy[r, l] = y
            cyl[r, l] = yl
            cx[r, l] = x
            out = y * (v - right(v)) + yl * (v - left(v))
            out = out + (x * (v - q[r + 1, l]) + xp * (v - q[r - 1, l])) + (f - f_up)
            diag[r, l] = diag[r, l] + ((y + yl) + (x + xp) + (c + c_up))
            emit(r, l, out)
            c_up, f_up = c, f
            if l < L - 1:
                v, m = v_n, m_n
        return carry

    for l in range(L):
        cx[rows[0] - 1, l] = 1.0 / (resist[rows[0] - 1, l] + resist[rows[0], l])
    blocks(rows, block, row, 0)


def apply(v_in, v_out, coefs, shift, rows, block, held, counted):
    cx, cy, cyl, cz, diag = coefs

    def row(r, held):
        at = r - shift
        c_up, v_up = higher(cz[at, 7]), higher(v_in[r, 7])
        v_0 = v_in[r, 0]
        v = v_0
        square, cross = held
        for l in range(L):
            v_n = v_in[r, l + 1] if l < L - 1 else deeper(v_0)
            c = cz[at, l]
            image = diag[at, l] * v - cy[at, l] * right(v) - cyl[at, l] * left(v)
            image = image - cx[at, l] * v_in[r + 1, l] - cx[at - 1, l] * v_in[r - 1, l]
            image = image - c * v_n - c_up * v_up
            if v_out is not None:
                v_out[r, l] = image
            if counted:
                a, b = own(v), own(image)
                square = square + a * a
                cross = cross + a * b
            v_up, c_up, v = v, c, v_n
        return square, cross

    return blocks(rows, block, row, held)


def write_moments(sums, moments):
    row = jnp.zeros((1, 128), F32)
    lane = iota((1, 128), 1)
    for k, held in enumerate(sums):
        value = jnp.sum(jnp.sum(held, axis=0, keepdims=True), axis=1, keepdims=True)
        row = jnp.where(lane == k, value, row)
    moments[...] = jnp.broadcast_to(row, moments.shape)


def no_sums():
    zero = jnp.zeros((8, COLS), F32)
    return zero, zero


def coefficients(gathered):
    row = jnp.sum(gathered[...], axis=0, keepdims=True)
    lane = iota((1, 128), 1)
    m = [jnp.sum(jnp.where(lane == k, row, 0.0), axis=1, keepdims=True) for k in range(6)]

    def dot(a, b, shift):
        total = jnp.zeros((1, 1), F32)
        for i, p in enumerate(a):
            for j, q in enumerate(b):
                total = total + p * q * m[i + j + shift]
        return total

    one = jnp.ones((1, 1), F32)
    a0 = m[0] / m[1]
    r1 = [one, -a0]
    n1 = dot(r1, r1, 0)
    b0 = n1 / m[0]
    p1 = [one + b0, -a0]
    a1 = n1 / dot(p1, p1, 1)
    r2 = [one, -a0 - a1 * p1[0], -a1 * p1[1]]
    n2 = dot(r2, r2, 0)
    b1 = n2 / n1
    p2 = [r2[0] + b1 * p1[0], r2[1] + b1 * p1[1], r2[2]]
    a2 = n2 / dot(p2, p2, 1)
    return (
        a0 + a1 * p1[0] + a2 * p2[0],
        a1 * p1[1] + a2 * p2[1],
        a2 * p2[2],
    )


def source_at(b, r, l, sub):
    return jnp.where(sub == 0, pltpu.roll(b[r], (8 - l) % 8, 0), 0.0)


def prepare_kernel(
    q_own, k_own, from_left, from_right, source,
    q, k, resist, cx, cy, cyl, cz, diag, v0, v1, v2, sums,
    b,
):
    lane = iota((8, 128), 1)
    keep = side_mask(lane)

    def fill(l, carry):
        for f, (field, target) in enumerate(((q_own, q), (k_own, k))):
            a, c = from_left[f * L + l], from_right[f * L + l]
            for x in range(ROWS):
                target[x, l, :, :COLS] = field[x, l]
                tile = halo_tile(a, c, lane, 8 * x, 8 * x)
                target[x, l, :, COLS:] = tile * keep if f == 1 else tile
        for x in range(ROWS):
            _, resist[x, l], diag[x, l] = local_terms(q[x, l], k[x, l])
        return carry

    lax.fori_loop(0, L, fill, 0)

    a, c = from_left[2 * L], from_right[2 * L]
    for x in range(ROWS):
        b[x, :, :COLS] = source[x]
        b[x, :, COLS:] = halo_tile(a, c, lane, 8 * x, 8 * x)
    sub = iota((8, XC), 0)

    def emit(r, l, out):
        v0[r, l] = source_at(b, r, l, sub) - out

    coefs = (cx, cy, cyl, cz, diag)
    couplings(q, resist, *coefs, (1, ROWS - 1), 14, emit)
    for step, (v_in, v_out, rows, block) in enumerate(
        ((v0, v1, (2, 14), 12), (v1, v2, (3, 13), 10), (v2, None, (4, 12), 8))
    ):
        held = apply(v_in, v_out, coefs, 0, rows, block, no_sums(), True)
        sums[2 * step], sums[2 * step + 1] = held


def prepare(*arrays):
    outs = (shaped(ROWS, L, 8, XC),) * 11 + (shaped(6, 8, COLS),)
    return pl.pallas_call(
        prepare_kernel,
        out_shape=outs,
        in_specs=vmem(len(arrays)),
        out_specs=tuple(vmem(len(outs))),
        scratch_shapes=[pltpu.VMEM((ROWS, L, XC), F32)],
        compiler_params=params(4),
        name="prepare",
    )(*arrays)


RSHIFT = 12
RROWS = 18


def first_kernel(
    q_mid, k_mid, resist_mid, cx_mid, cy_mid, cyl_mid, cz_mid, diag_mid, v0_mid, v1_mid, v2_mid, sums_mid,
    near_prev, near_next, far_prev, far_next, source, corner_prev, corner_next, from_left, from_right,
    q, k, b, v0, v1, v2, moments,
    resist, cx, cy, cyl, cz, diag,
):
    lane = iota((8, 128), 1)
    keep = side_mask(lane)
    has_prev, has_next = inside("gx")

    def fill(l, carry):
        for f, target in enumerate((q, k)):
            at = 2 * BHALO + f * L + l
            for side, rows, corner, r, spot, here in (
                (far_prev, FAR, corner_prev, 0, 8 * (8 - HALO), has_prev),
                (near_prev, NEAR, corner_prev, FAR, 8 * (8 - NEAR), has_prev),
                (near_next, NEAR, corner_next, RROWS - HALO, 0, has_next),
                (far_next, FAR, corner_next, RROWS - FAR, 8 * NEAR, has_next),
            ):
                tile = corner[at]
                for i in range(rows):
                    left_at = spot + 8 * i
                    row = [side[2 * (f * rows + i) + t, l] for t in range(2)]
                    row.append(halo_tile(tile, tile, lane, left_at, 64 + left_at))
                    for t in range(3):
                        part = row[t]
                        if f == 1:
                            part = part * (here * keep if t == 2 else here)
                        target[r + i, l, :, 128 * t : 128 * t + 128] = part
        for r in (*range(HALO), *range(RROWS - HALO, RROWS)):
            _, resist[r, l], diag[r, l] = local_terms(q[r, l], k[r, l])
        for r, x in ((7, 0), (8, 1), (9, ROWS - 2), (10, ROWS - 1)):
            q[r, l] = q_mid[x, l]
            resist[r, l] = resist_mid[x, l]
            diag[r, l] = diag_mid[x, l]
        return carry

    lax.fori_loop(0, L, fill, 0)

    a, c = from_left[2 * L], from_right[2 * L]
    for x in range(ROWS):
        b[HALO + x, :, :COLS] = source[x]
        b[HALO + x, :, COLS:] = halo_tile(a, c, lane, 8 * x, 8 * x)
    for side, r, spot in (
        (corner_prev, HALO - BHALO, 8 * (8 - BHALO)),
        (corner_next, HALO + ROWS, 0),
    ):
        tile = side[CORNER - 1]
        for i in range(BHALO):
            for t in range(2):
                b[r + i, :, 128 * t : 128 * t + 128] = side[2 * i + t]
            left_at = spot + 8 * i
            b[r + i, :, COLS:] = halo_tile(tile, tile, lane, left_at, 64 + left_at)

    sub = iota((8, XC), 0)
    coefs = (cx, cy, cyl, cz, diag)
    mids = (cx_mid, cy_mid, cyl_mid, cz_mid, diag_mid)

    for shift, rows in ((0, (1, HALO + 1)), (RSHIFT, (RROWS - HALO - 1, RROWS - 1))):

        def emit(r, l, out, shift=shift):
            v0[r + shift, l] = source_at(b, r + shift, l, sub) - out

        couplings(q, resist, *coefs, rows, HALO, emit)

    for mid, full, first in ((v0_mid, v0, 1), (v1_mid, v1, 2), (v2_mid, v2, 3)):
        for x in (first, first + 1, ROWS - 2 - first, ROWS - 1 - first):
            full[HALO + x] = mid[x]

    low, high = HALO, HALO + ROWS - 1
    sums = []
    for step, (v_in, v_out, deep) in enumerate(((v0, v1, 5), (v1, v2, 4), (v2, None, 0))):
        held = sums_mid[2 * step], sums_mid[2 * step + 1]
        more = step + 1
        for rows in ((low + 1, low + 1 + more), (high - more, high)):
            held = apply(v_in, v_out, mids, HALO, rows, more, held, True)
        held = apply(v_in, v_out, coefs, 0, (low, low + 1), 1, held, True)
        held = apply(v_in, v_out, coefs, RSHIFT, (high, high + 1), 1, held, True)
        if deep:
            apply(v_in, v_out, coefs, 0, (low - deep, low), deep, no_sums(), False)
            apply(v_in, v_out, coefs, RSHIFT, (high + 1, high + 1 + deep), deep, no_sums(), False)
        sums += held
    write_moments(sums, moments)


def first_newton(*arrays):
    w = shaped(XR, L, 8, XC)
    rim = shaped(RROWS, L, 8, XC)
    outs = (rim, rim, shaped(XR, L, XC), w, w, w, shaped(128, 128))
    return pl.pallas_call(
        first_kernel,
        out_shape=outs,
        in_specs=vmem(len(arrays)),
        out_specs=tuple(vmem(len(outs))),
        scratch_shapes=[pltpu.VMEM((RROWS, L, 8, XC), F32)] * 6,
        compiler_params=params(14),
        name="first_newton",
    )(*arrays)


def second_kernel(
    q_mid, k_mid, v0_mid, v1_mid, v2_mid, q_rim, k_rim, b, u0, u1, u2, gathered,
    q_own, p0, p1, p2, moments,
    q1, resist, cx, cy, cyl, cz, diag, v0, v2,
):
    v1 = resist
    c0, c1, c2 = coefficients(gathered)
    sub = iota((8, XC), 0)

    full, mid = (u0, u1, u2), (v0_mid, v1_mid, v2_mid)
    low, high = HALO, HALO + ROWS
    for q, k, shift, held, back, rows, block in (
        (q_rim, k_rim, 0, full, 0, (3, low), 4),
        (q_mid, k_mid, low, full, 0, (low, low + 3), 3),
        (q_mid, k_mid, low, mid, low, (low + 3, high - 3), 5),
        (q_mid, k_mid, low, full, 0, (high - 3, high), 3),
        (q_rim, k_rim, RSHIFT, full, 0, (high, XR - 3), 4),
    ):

        def update(r, carry, q=q, k=k, shift=shift, held=held, back=back):
            for l in range(L):
                old = q[r - shift, l]
                w0, w1, w2 = (w[r - back, l] for w in held)
                step = c0 * w0 + c1 * w1 + c2 * w2
                new = old + step
                q1[r, l] = new
                bend, resist[r, l], diag[r, l] = local_terms(new, k[r - shift, l])
                stored = 0.35 * (bend - jnp.tanh(old)) + STORE * step
                v0[r, l] = source_at(b, r, l, sub) - stored
            return carry

        blocks(rows, block, update, 0)

    def emit(r, l, out):
        v0[r, l] = v0[r, l] - out

    coefs = (cx, cy, cyl, cz, diag)
    couplings(q1, resist, *coefs, (4, XR - 4), 22, emit)
    sums = []
    for v_in, v_out, deep in ((v0, v1, 2), (v1, v2, 1), (v2, None, 0)):
        sums += apply(v_in, v_out, coefs, 0, (low, high), 16, no_sums(), True)
        if deep:
            apply(v_in, v_out, coefs, 0, (low - deep, low), deep, no_sums(), False)
            apply(v_in, v_out, coefs, 0, (high, high + deep), deep, no_sums(), False)
    write_moments(sums, moments)

    def keep(x, carry):
        for l in range(L):
            for source, target in ((q1, q_own), (v0, p0), (v1, p1), (v2, p2)):
                target[x, l] = source[HALO + x, l, :, :COLS]
        return carry

    lax.fori_loop(0, ROWS, keep, 0, unroll=4)


def second_newton(*arrays):
    o = shaped(ROWS, L, 8, COLS)
    outs = (o, o, o, o, shaped(128, 128))
    return pl.pallas_call(
        second_kernel,
        out_shape=outs,
        in_specs=vmem(len(arrays)),
        out_specs=tuple(vmem(len(outs))),
        scratch_shapes=[pltpu.VMEM((XR, L, 8, XC), F32)] * 9,
        compiler_params=params(28),
        name="second_newton",
    )(*arrays)


def final_kernel(q, v0, v1, v2, gathered, out):
    c0, c1, c2 = coefficients(gathered)

    def row(x, carry):
        for l in range(L):
            value = q[x, l] + c0 * v0[x, l] + c1 * v1[x, l] + c2 * v2[x, l]
            out[chunk(x, l, 0), :] = value[:, :128]
            out[chunk(x, l, 1), :] = value[:, 128:]
        return carry

    lax.fori_loop(0, ROWS, row, 0, unroll=4)


def final_update(*arrays):
    return pl.pallas_call(
        final_kernel,
        out_shape=shaped(32 * LEV, 128),
        in_specs=vmem(len(arrays)),
        out_specs=vmem()[0],
        compiler_params=params(4),
        name="final_update",
    )(*arrays)


def exchange(to_high, to_low, axis):
    count = lax.axis_size(axis)
    up = [(i, (i + 1) % count) for i in range(count)]
    down = [((i + 1) % count, i) for i in range(count)]
    return lax.ppermute(to_high, axis, up), lax.ppermute(to_low, axis, down)


def share(moments):
    return lax.all_to_all(moments, ("gx", "gy"), split_axis=0, concat_axis=0, tiled=True)


def body(
    pressure_old,
    conductivity,
    forcing,
    vegetated,
    cover_type,
    canopy_table,
    root_table,
    pair_counts,
    send_cols,
    canopy_state,
):
    owners = send_cols.shape[1]
    cols = in_hbm(send_cols.reshape(owners, 1, COLS))
    counts = in_hbm(pair_counts.reshape(owners))
    state = in_hbm(canopy_state.reshape(owners, 16, COLS))
    forcing, cover_type, vegetated = in_hbm(forcing), in_hbm(cover_type), in_hbm(vegetated)
    old, conductivity = (in_hbm(flat(v).reshape(8, 32 * L, 128)) for v in (pressure_old, conductivity))
    canopy_table, root_table = in_hbm(canopy_table.T), in_hbm(root_table.T)

    q_own, k_own, top, near_next, near_prev, far_next, far_prev = turn(old, conductivity)
    far_prev, far_next = exchange(far_next, far_prev, "gx")
    payload, conductance = canopy_send(forcing, cover_type, canopy_table, counts, cols, state, top)
    arrived = lax.all_to_all(payload, "gx", split_axis=0, concat_axis=0, tiled=True)
    top, payload = lax.optimization_barrier((top, payload))
    edge_left, edge_right, uptake, surface = sides(
        q_own, k_own, top, forcing, cover_type, vegetated, root_table
    )
    near_next, near_prev, arrived, far_prev, far_next, surface = lax.optimization_barrier(
        (near_next, near_prev, arrived, far_prev, far_next, surface)
    )
    near_prev, near_next = exchange(near_next, near_prev, "gx")
    source, to_right, to_left = canopy_source(
        arrived, cols, counts, forcing, conductance, uptake, surface, edge_left, edge_right
    )
    from_left, from_right = exchange(to_right, to_left, "gy")
    new_state = owner_update(arrived, state)
    to_next, to_prev = corners(source, from_left, from_right, in_hbm(new_state))
    corner_prev, corner_next = exchange(to_next, to_prev, "gx")

    mids = prepare(q_own, k_own, from_left, from_right, source)
    q, k, b, v0, v1, v2, moments = first_newton(
        *mids, near_prev, near_next, far_prev, far_next, source, corner_prev, corner_next, from_left, from_right
    )
    q1, w0, w1, w2, moments = second_newton(
        mids[0], mids[1], *mids[8:11], q, k, b, v0, v1, v2, share(moments)
    )
    pressure = unflat(final_update(q1, w0, w1, w2, share(moments)))
    return pressure, new_state.reshape(canopy_state.shape)


def solution(mesh):
    placed = (
        P(None, "gx", "gy"),
        P(None, "gx", "gy"),
        P(None, "gx", "gy"),
        P("gx", "gy"),
        P("gx", "gy"),
        P(),
        P(),
        P("gx", None, "gy"),
        P("gx", None, "gy", None),
        P("gx", None, "gy", None, None),
    )
    return jax.shard_map(
        body,
        mesh=mesh,
        in_specs=placed,
        out_specs=(P(None, "gx", "gy"), P("gx", None, "gy", None, None)),
        check_vma=False,
    )
```

```python
import jax
import jax.numpy as jnp
from jax import lax
from jax.experimental import pallas as pl
from jax.experimental.pallas import tpu as pltpu
from jax.sharding import PartitionSpec as P

FORC = 8
ROOT = 8
LEV = 64
ROWS = 16
COLS = 256
L = 8
HALO = 7
NEAR = 4
FAR = HALO - NEAR
XR = ROWS + 2 * HALO
XC = 384
OUTSIDE = 1e37
BHALO = 6
SIDE = 2 * L + 1
CORNER = 2 * BHALO + SIDE
STORE = 0.05
GRAV = 0.5
F32 = jnp.float32
BF16 = jnp.bfloat16


def vmem(n=1):
    return [pl.BlockSpec(memory_space=pltpu.VMEM)] * n


def params(mib):
    return pltpu.CompilerParams(vmem_limit_bytes=mib * 1024 * 1024)


def shaped(*shape):
    return jax.ShapeDtypeStruct(shape, F32)


def iota(shape, dim):
    return lax.broadcasted_iota(jnp.int32, shape, dim)


def right(v):
    return pltpu.roll(v, v.shape[1] - 1, 1)


def left(v):
    return pltpu.roll(v, 1, 1)


def deeper(v):
    return pltpu.roll(v, v.shape[0] - 1, 0)


def higher(v):
    return pltpu.roll(v, 1, 0)


def lanes(v, shift):
    return v if shift % 128 == 0 else pltpu.roll(v, shift % 128, v.ndim - 1)


def pieces(v):
    high = v.astype(BF16)
    rest = v - high.astype(F32)
    mid = rest.astype(BF16)
    low = (rest - mid.astype(F32)).astype(BF16)
    return high, mid, low


def in_hbm(v):
    return pltpu.with_memory_space_constraint(v, pltpu.HBM)


def smem():
    return pl.BlockSpec(memory_space=pltpu.SMEM)


def looked_up(kinds, table):
    found = [jnp.zeros(kinds.shape, F32) for _ in range(table.shape[0])]
    for kind in range(table.shape[1]):
        hit = kinds == kind
        for m in range(table.shape[0]):
            found[m] = jnp.where(hit, table[m, kind], found[m])
    return found


def hits(index):
    row = lax.shift_right_logical(index, 8)
    col = jnp.bitwise_and(index, COLS - 1)
    row_hit = iota((ROWS, COLS), 0) == row
    col_hit = iota((COLS, COLS), 0) == col
    return row_hit, jnp.where(col_hit, 1.0, 0.0).astype(BF16)


def canopy_send_kernel(
    forcing, cover, canopy_table, counts, cols, state, after, payload, conductance, split
):
    weights = looked_up(cover[...], canopy_table)
    total = weights[0] * forcing[0]
    for m in range(1, FORC):
        total = total + weights[m] * forcing[m]
    g = 2.0 * jax.nn.sigmoid(total)
    conductance[...] = g
    channels = [forcing[0], forcing[1], forcing[2], jnp.tanh(forcing[4]), g]
    used = len(channels)
    for c, channel in enumerate(channels):
        for p, piece in enumerate(pieces(channel)):
            split[pl.ds((p * used + c) * ROWS, ROWS), :] = piece

    def owner(o, carry):
        row_hit, onehot = hits(cols[o])
        picked = jnp.dot(split[...], onehot, preferred_element_type=F32)
        span = used * ROWS
        picked = picked[:span] + picked[span : 2 * span] + picked[2 * span :]
        sub = iota((8, COLS), 0)
        out = pltpu.roll(state[o, 0:8, :], 6, 0)
        for c in range(used):
            chosen = jnp.where(row_hit, picked[c * ROWS : (c + 1) * ROWS], 0.0)
            chosen = jnp.sum(chosen, axis=0, keepdims=True)
            out = jnp.where(sub == c, chosen, out)
        live = jnp.where(iota((8, COLS), 1) < counts[o], 1.0, 0.0)
        payload[o] = jnp.where(sub == used, live, out)
        return carry

    lax.fori_loop(0, cols.shape[0], owner, 0, unroll=16)


def canopy_send(forcing, cover, canopy_table, counts, cols, state, after):
    owners = cols.shape[0]
    return pl.pallas_call(
        canopy_send_kernel,
        out_shape=(shaped(owners, 8, COLS), shaped(ROWS, COLS)),
        in_specs=vmem(2) + [smem(), smem()] + vmem(2) + [pl.BlockSpec(memory_space=pl.ANY)],
        out_specs=tuple(vmem(2)),
        scratch_shapes=[pltpu.VMEM((15 * ROWS, COLS), BF16)],
        compiler_params=params(16),
        name="canopy_send",
    )(forcing, cover, canopy_table, counts, cols, state, after)


def softplus(v):
    return jnp.maximum(v, 0.0) + jnp.log1p(jnp.exp(-jnp.abs(v)))


def leaf(start, f0, f1, f2, g):
    temp = start
    for _ in range(3):
        temp = 0.5 * (start + f0) + 0.5 * jnp.tanh(f1 - g * (temp - f2))
    return temp


def source_kernel(
    arrived, cols, counts, forcing, conductance, uptake, surface, edge_left, edge_right,
    source, to_right, to_left, total, turned,
):
    total[...] = jnp.zeros_like(total)

    def owner(o, carry):
        row_hit, onehot = hits(cols[o])
        wanted = jnp.logical_and(row_hit, iota((ROWS, COLS), 1) < counts[o])
        block = arrived[o]
        parts = []
        for c in (6, 7):
            value = jnp.where(wanted, block[c : c + 1, :], 0.0)
            parts.extend(pieces(value))
        stacked = jnp.concatenate(parts, axis=0)
        total[...] += lax.dot_general(
            stacked, onehot, (((1,), (1,)), ((), ())), preferred_element_type=F32
        )
        return carry

    lax.fori_loop(0, cols.shape[0], owner, 0, unroll=16)

    def piece(k):
        return total[k * ROWS : (k + 1) * ROWS, :]

    water = piece(0) + piece(1) + piece(2)
    start = piece(3) + piece(4) + piece(5)
    g = conductance[...]
    temp = leaf(start, forcing[0], forcing[1], forcing[2], g)
    demand = g * softplus(temp - forcing[3]) / (1.0 + water * water)
    for m in range(ROOT):
        value = -(demand * uptake[m])
        if m == 0:
            value = value + surface[...]
        for t in range(2):
            turned[pl.ds(t * 128 + m * ROWS, ROWS), :] = value[:, t * 128 : t * 128 + 128]
    lane = iota((L, 128), 1)
    first = jnp.zeros((L, 128), F32)
    last = jnp.zeros((L, 128), F32)
    for x in range(ROWS):
        low = turned[pl.ds(x, L, stride=ROWS), :]
        high = turned[pl.ds(128 + x, L, stride=ROWS), :]
        source[x, :, :128] = low
        source[x, :, 128:] = high
        here = jnp.logical_and(lane >= 8 * x, lane < 8 * x + 8)
        first = jnp.where(here, lanes(low, 8 * x), first)
        last = jnp.where(here, lanes(high, 8 * x - 120), last)
    for target, edge, own_edge in ((to_left, edge_left, first), (to_right, edge_right, last)):
        target[0 : 2 * L] = edge[...]
        target[2 * L] = own_edge


def canopy_source(*arrays):
    v = vmem()[0]
    return pl.pallas_call(
        source_kernel,
        out_shape=(shaped(ROWS, ROOT, COLS), shaped(SIDE, L, 128), shaped(SIDE, L, 128)),
        in_specs=[v, v, smem(), v, v, v, v, v, v],
        out_specs=(v, v, v),
        scratch_shapes=[pltpu.VMEM((6 * ROWS, COLS), F32), pltpu.VMEM((2 * 128, 128), F32)],
        compiler_params=params(16),
        name="canopy_source",
    )(*arrays)


def owner_kernel(arrived, state, updated):
    def slot(i, carry):
        block = arrived[i]
        old = state[i]
        temp = leaf(old[1:2], block[0:1], block[1:2], block[2:3], block[4:5])
        sub = iota(old.shape, 0)
        base = jnp.where(sub == 1, temp, old)
        upper = pltpu.roll(base, 1, 0)
        lower = pltpu.roll(base, base.shape[0] - 1, 0)
        lower = jnp.where(sub == base.shape[0] - 1, base, lower)
        fresh = 0.6 * base + 0.2 * upper + 0.2 * lower
        fresh = jnp.where(sub == 1, temp, fresh)
        fresh = jnp.where(sub == 0, 0.8 * old + 0.2 * block[3:4], fresh)
        updated[i] = jnp.where(block[5:6] > 0.5, fresh, old)
        return carry

    lax.fori_loop(0, arrived.shape[0], slot, 0, unroll=16)


def owner_update(arrived, state):
    return pl.pallas_call(
        owner_kernel,
        out_shape=shaped(*state.shape),
        in_specs=vmem(2),
        out_specs=vmem()[0],
        compiler_params=params(8),
        name="owner_update",
    )(arrived, state)


def flat(v):
    return v.reshape(LEV, 2, 8, 2, 128).transpose(0, 1, 3, 2, 4).reshape(32 * LEV, 128)


def unflat(v):
    return v.reshape(LEV, 2, 2, 8, 128).transpose(0, 1, 3, 2, 4).reshape(LEV, ROWS, COLS)


def chunk(x, l, t):
    return pl.ds(32 * l + 16 * (x // 8) + 8 * t + x % 8, 8, stride=32 * L)


def rim_shape(rows):
    return 2 * rows * 2, L, 8, 128


def turn_kernel(
    pressure, conductivity,
    q, k, top, near_next, near_prev, far_next, far_prev,
    held_q, held_k, near_next_rim, near_prev_rim, far_next_rim, far_prev_rim, sems,
):
    fetches = []
    for l in range(L):
        part = pl.ds(32 * l, 32)
        for f, (field, held) in enumerate(((pressure, held_q), (conductivity, held_k))):
            fetches.append(pltpu.make_async_copy(field.at[:, part], held.at[:, part], sems.at[f, l]))
    for fetch in fetches:
        fetch.start()
    sends = []
    for l in range(L):
        fetches[2 * l].wait()
        fetches[2 * l + 1].wait()
        for f, (held, target) in enumerate(((held_q, q), (held_k, k))):
            for x in range(ROWS):
                for t in range(2):
                    part = held[:, 32 * l + 16 * (x // 8) + 8 * t + x % 8, :]
                    target[x, l, :, 128 * t : 128 * t + 128] = part
                    if x < NEAR:
                        near_prev_rim[2 * (f * NEAR + x) + t, l] = part
                    elif x < HALO:
                        far_prev_rim[2 * (f * FAR + x - NEAR) + t, l] = part
                    if x >= ROWS - NEAR:
                        near_next_rim[2 * (f * NEAR + x - ROWS + NEAR) + t, l] = part
                    elif x >= ROWS - HALO:
                        far_next_rim[2 * (f * FAR + x - ROWS + HALO) + t, l] = part
        if l % 4 == 3:
            part = pl.ds(l - 3, 4)
            for i, (rim, out) in enumerate(
                (
                    (far_next_rim, far_next),
                    (far_prev_rim, far_prev),
                    (near_next_rim, near_next),
                    (near_prev_rim, near_prev),
                )
            ):
                sends.append(pltpu.make_async_copy(rim.at[:, part], out.at[:, part], sems.at[2 + i, l]))
                sends[-1].start()
    for m in range(ROOT):
        for xt in range(2):
            for t in range(2):
                top[m, 8 * xt : 8 * xt + 8, 128 * t : 128 * t + 128] = held_q[
                    0, pl.ds(32 * m + 16 * xt + 8 * t, 8), :
                ]
    for send in sends:
        send.wait()


def turn(*arrays):
    own_shape = shaped(ROWS, L, 8, COLS)
    near, far = rim_shape(NEAR), rim_shape(FAR)
    rims = [pltpu.HBM(shape, F32) for shape in (near, near, far, far)]
    hbm = pl.BlockSpec(memory_space=pltpu.HBM)
    return pl.pallas_call(
        turn_kernel,
        out_shape=(own_shape, own_shape, shaped(ROOT, ROWS, COLS), *rims),
        in_specs=[hbm, hbm],
        out_specs=(*vmem(3), hbm, hbm, hbm, hbm),
        scratch_shapes=[
            pltpu.VMEM((8, 32 * L, 128), F32),
            pltpu.VMEM((8, 32 * L, 128), F32),
            *[pltpu.VMEM(shape, F32) for shape in (near, near, far, far)],
            pltpu.SemaphoreType.DMA((6, L)),
        ],
        compiler_params=params(8),
        name="turn",
    )(*arrays)


def sides_kernel(
    q, k, top, forcing, cover, vegetated, root_table, edge_left, edge_right, uptake, surface
):
    lane = iota((8, 128), 1)

    def layer(l, carry):
        for f, field in enumerate((q, k)):
            first = jnp.zeros((8, 128), F32)
            last = jnp.zeros((8, 128), F32)
            for x in range(ROWS):
                here = jnp.logical_and(lane >= 8 * x, lane < 8 * x + 8)
                first = jnp.where(here, lanes(field[x, l, :, :128], 8 * x), first)
                last = jnp.where(here, lanes(field[x, l, :, 128:], 8 * x - 120), last)
            edge_left[f * L + l] = first
            edge_right[f * L + l] = last
        return carry

    lax.fori_loop(0, L, layer, 0, unroll=8)
    roots = looked_up(cover[...], root_table)
    planted = vegetated[...] == 1
    for m in range(ROOT):
        moist = jax.nn.sigmoid(2.0 * (top[m] + 1.5))
        uptake[m] = jnp.where(planted, roots[m] * moist, 0.0)
        if m == 0:
            evaporation = jnp.where(planted, 0.0, 0.5) * softplus(forcing[3] - forcing[2]) * moist
            surface[...] = 0.3 * softplus(forcing[4]) - evaporation


def sides(*arrays):
    edge = shaped(2 * L, 8, 128)
    outs = (edge, edge, shaped(ROOT, ROWS, COLS), shaped(ROWS, COLS))
    return pl.pallas_call(
        sides_kernel,
        out_shape=outs,
        in_specs=vmem(6) + [smem()],
        out_specs=tuple(vmem(len(outs))),
        compiler_params=params(8),
        name="sides",
    )(*arrays)


def corner_kernel(source, from_left, from_right, after, to_next, to_prev):
    low = iota((8, 128), 1) < 64
    for i in range(BHALO):
        for t in range(2):
            part = pl.ds(128 * t, 128)
            to_next[2 * i + t] = source[ROWS - BHALO + i, :, part]
            to_prev[2 * i + t] = source[i, :, part]
    for j in range(SIDE):
        a, b = from_left[j], from_right[j]
        to_next[2 * BHALO + j] = jnp.where(low, lanes(a, 64), b)
        to_prev[2 * BHALO + j] = jnp.where(low, a, lanes(b, 64))


def corners(*arrays):
    outs = (shaped(CORNER, 8, 128), shaped(CORNER, 8, 128))
    return pl.pallas_call(
        corner_kernel,
        out_shape=outs,
        in_specs=vmem(3) + [pl.BlockSpec(memory_space=pl.ANY)],
        out_specs=tuple(vmem(2)),
        compiler_params=params(16),
        name="corners",
    )(*arrays)


def inside(axis):
    at, count = lax.axis_index(axis), lax.axis_size(axis)
    return jnp.where(at > 0, 1.0, 0.0), jnp.where(at < count - 1, 1.0, 0.0)


def side_mask(lane):
    has_left, has_right = inside("gy")
    return jnp.where(lane < 8, has_right, jnp.where(lane >= 120, has_left, 0.0))


def halo_tile(from_left, from_right, lane, at_left, at_right):
    tile = jnp.where(lane < 8, lanes(from_right, -at_right), 0.0)
    return jnp.where(lane >= 120, lanes(from_left, 120 - at_left), tile)


def own(v):
    return v[:, :COLS]


def local_terms(q, k):
    bend = jnp.tanh(q)
    s = 0.5 + 0.5 * bend
    m = k * (0.1 + 0.9 * s)
    return bend, jnp.where(m > 0.0, 0.5 / m, OUTSIDE), 1.4 * s * (1.0 - s) + STORE


def blocks(rows, block, row, carry=None):
    def step(i, held):
        for j in range(block):
            held = row(rows[0] + i * block + j, held)
        return held

    steps = (rows[1] - rows[0]) // block
    return step(0, carry) if steps == 1 else lax.fori_loop(0, steps, step, carry)


def couplings(q, resist, cx, cy, cyl, cz, diag, rows, block, emit):
    last = iota((8, XC), 0) == 7

    def row(r, carry):
        q_0, m_0, q_7, m_7 = q[r, 0], resist[r, 0], q[r, 7], resist[r, 7]
        c_7 = jnp.where(last, 0.0, 1.0 / (m_7 + deeper(m_0)))
        f_7 = c_7 * (q_7 - deeper(q_0) + GRAV)
        cz[r, 7] = c_7
        c_up, f_up = higher(c_7), higher(f_7)
        v, m = q_0, m_0
        for l in range(L):
            if l < L - 1:
                m_n, v_n = resist[r, l + 1], q[r, l + 1]
                c = 1.0 / (m + m_n)
                f = c * (v - v_n + GRAV)
                cz[r, l] = c
            else:
                c, f = c_7, f_7
            y = 1.0 / (m + right(m))
            yl = 1.0 / (m + left(m))
            x = 1.0 / (m + resist[r + 1, l])
            xp = cx[r - 1, l]
            cy[r, l] = y
            cyl[r, l] = yl
            cx[r, l] = x
            out = y * (v - right(v)) + yl * (v - left(v))
            out = out + (x * (v - q[r + 1, l]) + xp * (v - q[r - 1, l])) + (f - f_up)
            diag[r, l] = diag[r, l] + ((y + yl) + (x + xp) + (c + c_up))
            emit(r, l, out)
            c_up, f_up = c, f
            if l < L - 1:
                v, m = v_n, m_n
        return carry

    for l in range(L):
        cx[rows[0] - 1, l] = 1.0 / (resist[rows[0] - 1, l] + resist[rows[0], l])
    blocks(rows, block, row, 0)


def apply(v_in, v_out, coefs, shift, rows, block, held, counted):
    cx, cy, cyl, cz, diag = coefs

    def row(r, held):
        at = r - shift
        c_up, v_up = higher(cz[at, 7]), higher(v_in[r, 7])
        v_0 = v_in[r, 0]
        v = v_0
        square, cross = held
        for l in range(L):
            v_n = v_in[r, l + 1] if l < L - 1 else deeper(v_0)
            c = cz[at, l]
            image = diag[at, l] * v - cy[at, l] * right(v) - cyl[at, l] * left(v)
            image = image - cx[at, l] * v_in[r + 1, l] - cx[at - 1, l] * v_in[r - 1, l]
            image = image - c * v_n - c_up * v_up
            if v_out is not None:
                v_out[r, l] = image
            if counted:
                a, b = own(v), own(image)
                square = square + a * a
                cross = cross + a * b
            v_up, c_up, v = v, c, v_n
        return square, cross

    return blocks(rows, block, row, held)


def write_moments(sums, moments):
    row = jnp.zeros((1, 128), F32)
    lane = iota((1, 128), 1)
    for k, held in enumerate(sums):
        value = jnp.sum(jnp.sum(held, axis=0, keepdims=True), axis=1, keepdims=True)
        row = jnp.where(lane == k, value, row)
    moments[...] = jnp.broadcast_to(row, moments.shape)


def no_sums():
    zero = jnp.zeros((8, COLS), F32)
    return zero, zero


def coefficients(gathered):
    row = jnp.sum(gathered[...], axis=0, keepdims=True)
    lane = iota((1, 128), 1)
    m = [jnp.sum(jnp.where(lane == k, row, 0.0), axis=1, keepdims=True) for k in range(6)]

    def dot(a, b, shift):
        total = jnp.zeros((1, 1), F32)
        for i, p in enumerate(a):
            for j, q in enumerate(b):
                total = total + p * q * m[i + j + shift]
        return total

    one = jnp.ones((1, 1), F32)
    a0 = m[0] / m[1]
    r1 = [one, -a0]
    n1 = dot(r1, r1, 0)
    b0 = n1 / m[0]
    p1 = [one + b0, -a0]
    a1 = n1 / dot(p1, p1, 1)
    r2 = [one, -a0 - a1 * p1[0], -a1 * p1[1]]
    n2 = dot(r2, r2, 0)
    b1 = n2 / n1
    p2 = [r2[0] + b1 * p1[0], r2[1] + b1 * p1[1], r2[2]]
    a2 = n2 / dot(p2, p2, 1)
    return (
        a0 + a1 * p1[0] + a2 * p2[0],
        a1 * p1[1] + a2 * p2[1],
        a2 * p2[2],
    )


def source_at(b, r, l, sub):
    return jnp.where(sub == 0, pltpu.roll(b[r], (8 - l) % 8, 0), 0.0)


def prepare_kernel(
    q_own, k_own, from_left, from_right, source,
    q, k, resist, cx, cy, cyl, cz, diag, v0, v1, v2, sums,
    b,
):
    lane = iota((8, 128), 1)
    keep = side_mask(lane)

    def fill(l, carry):
        for f, (field, target) in enumerate(((q_own, q), (k_own, k))):
            a, c = from_left[f * L + l], from_right[f * L + l]
            for x in range(ROWS):
                target[x, l, :, :COLS] = field[x, l]
                tile = halo_tile(a, c, lane, 8 * x, 8 * x)
                target[x, l, :, COLS:] = tile * keep if f == 1 else tile
        for x in range(ROWS):
            _, resist[x, l], diag[x, l] = local_terms(q[x, l], k[x, l])
        return carry

    lax.fori_loop(0, L, fill, 0)

    a, c = from_left[2 * L], from_right[2 * L]
    for x in range(ROWS):
        b[x, :, :COLS] = source[x]
        b[x, :, COLS:] = halo_tile(a, c, lane, 8 * x, 8 * x)
    sub = iota((8, XC), 0)

    def emit(r, l, out):
        v0[r, l] = source_at(b, r, l, sub) - out

    coefs = (cx, cy, cyl, cz, diag)
    couplings(q, resist, *coefs, (1, ROWS - 1), 14, emit)
    for step, (v_in, v_out, rows, block) in enumerate(
        ((v0, v1, (2, 14), 12), (v1, v2, (3, 13), 10), (v2, None, (4, 12), 8))
    ):
        held = apply(v_in, v_out, coefs, 0, rows, block, no_sums(), True)
        sums[2 * step], sums[2 * step + 1] = held


def prepare(*arrays):
    outs = (shaped(ROWS, L, 8, XC),) * 11 + (shaped(6, 8, COLS),)
    return pl.pallas_call(
        prepare_kernel,
        out_shape=outs,
        in_specs=vmem(len(arrays)),
        out_specs=tuple(vmem(len(outs))),
        scratch_shapes=[pltpu.VMEM((ROWS, L, XC), F32)],
        compiler_params=params(4),
        name="prepare",
    )(*arrays)


RSHIFT = 12
RROWS = 18


def first_kernel(
    q_mid, k_mid, resist_mid, cx_mid, cy_mid, cyl_mid, cz_mid, diag_mid, v0_mid, v1_mid, v2_mid, sums_mid,
    near_prev, near_next, far_prev, far_next, source, corner_prev, corner_next, from_left, from_right,
    q, k, b, v0, v1, v2, moments,
    resist, cx, cy, cyl, cz, diag,
):
    lane = iota((8, 128), 1)
    keep = side_mask(lane)
    has_prev, has_next = inside("gx")

    def fill(l, carry):
        for f, target in enumerate((q, k)):
            at = 2 * BHALO + f * L + l
            for side, rows, corner, r, spot, here in (
                (far_prev, FAR, corner_prev, 0, 8 * (8 - HALO), has_prev),
                (near_prev, NEAR, corner_prev, FAR, 8 * (8 - NEAR), has_prev),
                (near_next, NEAR, corner_next, RROWS - HALO, 0, has_next),
                (far_next, FAR, corner_next, RROWS - FAR, 8 * NEAR, has_next),
            ):
                tile = corner[at]
                for i in range(rows):
                    left_at = spot + 8 * i
                    row = [side[2 * (f * rows + i) + t, l] for t in range(2)]
                    row.append(halo_tile(tile, tile, lane, left_at, 64 + left_at))
                    for t in range(3):
                        part = row[t]
                        if f == 1:
                            part = part * (here * keep if t == 2 else here)
                        target[r + i, l, :, 128 * t : 128 * t + 128] = part
        for r in (*range(HALO), *range(RROWS - HALO, RROWS)):
            _, resist[r, l], diag[r, l] = local_terms(q[r, l], k[r, l])
        for r, x in ((7, 0), (8, 1), (9, ROWS - 2), (10, ROWS - 1)):
            q[r, l] = q_mid[x, l]
            resist[r, l] = resist_mid[x, l]
            diag[r, l] = diag_mid[x, l]
        return carry

    lax.fori_loop(0, L, fill, 0)

    a, c = from_left[2 * L], from_right[2 * L]
    for x in range(ROWS):
        b[HALO + x, :, :COLS] = source[x]
        b[HALO + x, :, COLS:] = halo_tile(a, c, lane, 8 * x, 8 * x)
    for side, r, spot in (
        (corner_prev, HALO - BHALO, 8 * (8 - BHALO)),
        (corner_next, HALO + ROWS, 0),
    ):
        tile = side[CORNER - 1]
        for i in range(BHALO):
            for t in range(2):
                b[r + i, :, 128 * t : 128 * t + 128] = side[2 * i + t]
            left_at = spot + 8 * i
            b[r + i, :, COLS:] = halo_tile(tile, tile, lane, left_at, 64 + left_at)

    sub = iota((8, XC), 0)
    coefs = (cx, cy, cyl, cz, diag)
    mids = (cx_mid, cy_mid, cyl_mid, cz_mid, diag_mid)

    for shift, rows in ((0, (1, HALO + 1)), (RSHIFT, (RROWS - HALO - 1, RROWS - 1))):

        def emit(r, l, out, shift=shift):
            v0[r + shift, l] = source_at(b, r + shift, l, sub) - out

        couplings(q, resist, *coefs, rows, HALO, emit)

    for mid, full, first in ((v0_mid, v0, 1), (v1_mid, v1, 2), (v2_mid, v2, 3)):
        for x in (first, first + 1, ROWS - 2 - first, ROWS - 1 - first):
            full[HALO + x] = mid[x]

    low, high = HALO, HALO + ROWS - 1
    sums = []
    for step, (v_in, v_out, deep) in enumerate(((v0, v1, 5), (v1, v2, 4), (v2, None, 0))):
        held = sums_mid[2 * step], sums_mid[2 * step + 1]
        more = step + 1
        for rows in ((low + 1, low + 1 + more), (high - more, high)):
            held = apply(v_in, v_out, mids, HALO, rows, more, held, True)
        held = apply(v_in, v_out, coefs, 0, (low, low + 1), 1, held, True)
        held = apply(v_in, v_out, coefs, RSHIFT, (high, high + 1), 1, held, True)
        if deep:
            apply(v_in, v_out, coefs, 0, (low - deep, low), deep, no_sums(), False)
            apply(v_in, v_out, coefs, RSHIFT, (high + 1, high + 1 + deep), deep, no_sums(), False)
        sums += held
    write_moments(sums, moments)


def first_newton(*arrays):
    w = shaped(XR, L, 8, XC)
    rim = shaped(RROWS, L, 8, XC)
    outs = (rim, rim, shaped(XR, L, XC), w, w, w, shaped(128, 128))
    return pl.pallas_call(
        first_kernel,
        out_shape=outs,
        in_specs=vmem(len(arrays)),
        out_specs=tuple(vmem(len(outs))),
        scratch_shapes=[pltpu.VMEM((RROWS, L, 8, XC), F32)] * 6,
        compiler_params=params(14),
        name="first_newton",
    )(*arrays)


def second_kernel(
    q_mid, k_mid, v0_mid, v1_mid, v2_mid, q_rim, k_rim, b, u0, u1, u2, gathered,
    q_own, p0, p1, p2, moments,
    q1, resist, cx, cy, cyl, cz, diag, v0, v2,
):
    v1 = resist
    c0, c1, c2 = coefficients(gathered)
    sub = iota((8, XC), 0)

    full, mid = (u0, u1, u2), (v0_mid, v1_mid, v2_mid)
    low, high = HALO, HALO + ROWS
    for q, k, shift, held, back, rows, block in (
        (q_rim, k_rim, 0, full, 0, (3, low), 4),
        (q_mid, k_mid, low, full, 0, (low, low + 3), 3),
        (q_mid, k_mid, low, mid, low, (low + 3, high - 3), 10),
        (q_mid, k_mid, low, full, 0, (high - 3, high), 3),
        (q_rim, k_rim, RSHIFT, full, 0, (high, XR - 3), 4),
    ):

        def update(r, carry, q=q, k=k, shift=shift, held=held, back=back):
            for l in range(L):
                old = q[r - shift, l]
                w0, w1, w2 = (w[r - back, l] for w in held)
                step = c0 * w0 + c1 * w1 + c2 * w2
                new = old + step
                q1[r, l] = new
                bend, resist[r, l], diag[r, l] = local_terms(new, k[r - shift, l])
                stored = 0.35 * (bend - jnp.tanh(old)) + STORE * step
                v0[r, l] = source_at(b, r, l, sub) - stored
            return carry

        blocks(rows, block, update, 0)

    def emit(r, l, out):
        v0[r, l] = v0[r, l] - out

    coefs = (cx, cy, cyl, cz, diag)
    couplings(q1, resist, *coefs, (4, XR - 4), 22, emit)
    sums = []
    for v_in, v_out, deep in ((v0, v1, 2), (v1, v2, 1), (v2, None, 0)):
        sums += apply(v_in, v_out, coefs, 0, (low, high), 16, no_sums(), True)
        if deep:
            apply(v_in, v_out, coefs, 0, (low - deep, low), deep, no_sums(), False)
            apply(v_in, v_out, coefs, 0, (high, high + deep), deep, no_sums(), False)
    write_moments(sums, moments)

    def keep(x, carry):
        for l in range(L):
            for source, target in ((q1, q_own), (v0, p0), (v1, p1), (v2, p2)):
                target[x, l] = source[HALO + x, l, :, :COLS]
        return carry

    lax.fori_loop(0, ROWS, keep, 0, unroll=8)


def second_newton(*arrays):
    o = shaped(ROWS, L, 8, COLS)
    outs = (o, o, o, o, shaped(128, 128))
    return pl.pallas_call(
        second_kernel,
        out_shape=outs,
        in_specs=vmem(len(arrays)),
        out_specs=tuple(vmem(len(outs))),
        scratch_shapes=[pltpu.VMEM((XR, L, 8, XC), F32)] * 9,
        compiler_params=params(28),
        name="second_newton",
    )(*arrays)


def final_kernel(q, v0, v1, v2, gathered, out, held, sems):
    c0, c1, c2 = coefficients(gathered)
    sends = []
    for half in range(2):

        def row(i, carry, half=half):
            x = 8 * half + i
            for l in range(L):
                value = q[x, l] + c0 * v0[x, l] + c1 * v1[x, l] + c2 * v2[x, l]
                held[:, l, half, i, :] = value[:, :128]
                held[:, l, half, 8 + i, :] = value[:, 128:]
            return carry

        lax.fori_loop(0, 8, row, 0, unroll=4)
        sends.append(pltpu.make_async_copy(held.at[:, :, half], out.at[:, :, half], sems.at[half]))
        sends[-1].start()
    for send in sends:
        send.wait()


def final_update(*arrays):
    shape = (8, L, 2, 16, 128)
    return pl.pallas_call(
        final_kernel,
        out_shape=shaped(*shape),
        in_specs=vmem(len(arrays)),
        out_specs=pl.BlockSpec(memory_space=pltpu.HBM),
        scratch_shapes=[pltpu.VMEM(shape, F32), pltpu.SemaphoreType.DMA((2,))],
        compiler_params=params(4),
        name="final_update",
    )(*arrays)


def exchange(to_high, to_low, axis):
    count = lax.axis_size(axis)
    up = [(i, (i + 1) % count) for i in range(count)]
    down = [((i + 1) % count, i) for i in range(count)]
    return lax.ppermute(to_high, axis, up), lax.ppermute(to_low, axis, down)


def share(moments):
    return lax.all_to_all(moments, ("gx", "gy"), split_axis=0, concat_axis=0, tiled=True)


def body(
    pressure_old,
    conductivity,
    forcing,
    vegetated,
    cover_type,
    canopy_table,
    root_table,
    pair_counts,
    send_cols,
    canopy_state,
):
    owners = send_cols.shape[1]
    cols = in_hbm(send_cols.reshape(owners, 1, COLS))
    counts = in_hbm(pair_counts.reshape(owners))
    state = in_hbm(canopy_state.reshape(owners, 16, COLS))
    forcing, cover_type, vegetated = in_hbm(forcing), in_hbm(cover_type), in_hbm(vegetated)
    old, conductivity = (in_hbm(flat(v).reshape(8, 32 * L, 128)) for v in (pressure_old, conductivity))
    canopy_table, root_table = in_hbm(canopy_table.T), in_hbm(root_table.T)

    q_own, k_own, top, near_next, near_prev, far_next, far_prev = turn(old, conductivity)
    far_prev, far_next = exchange(far_next, far_prev, "gx")
    payload, conductance = canopy_send(forcing, cover_type, canopy_table, counts, cols, state, top)
    arrived = lax.all_to_all(payload, "gx", split_axis=0, concat_axis=0, tiled=True)
    top, payload = lax.optimization_barrier((top, payload))
    edge_left, edge_right, uptake, surface = sides(
        q_own, k_own, top, forcing, cover_type, vegetated, root_table
    )
    near_next, near_prev, arrived, far_prev, far_next, surface = lax.optimization_barrier(
        (near_next, near_prev, arrived, far_prev, far_next, surface)
    )
    near_prev, near_next = exchange(near_next, near_prev, "gx")
    source, to_right, to_left = canopy_source(
        arrived, cols, counts, forcing, conductance, uptake, surface, edge_left, edge_right
    )
    from_left, from_right = exchange(to_right, to_left, "gy")
    new_state = owner_update(arrived, state)
    to_next, to_prev = corners(source, from_left, from_right, in_hbm(new_state))
    corner_prev, corner_next = exchange(to_next, to_prev, "gx")

    mids = prepare(q_own, k_own, from_left, from_right, source)
    q, k, b, v0, v1, v2, moments = first_newton(
        *mids, near_prev, near_next, far_prev, far_next, source, corner_prev, corner_next, from_left, from_right
    )
    q1, w0, w1, w2, moments = second_newton(
        mids[0], mids[1], *mids[8:11], q, k, b, v0, v1, v2, share(moments)
    )
    pressure = unflat(final_update(q1, w0, w1, w2, share(moments)))
    return pressure, new_state.reshape(canopy_state.shape)


def solution(mesh):
    placed = (
        P(None, "gx", "gy"),
        P(None, "gx", "gy"),
        P(None, "gx", "gy"),
        P("gx", "gy"),
        P("gx", "gy"),
        P(),
        P(),
        P("gx", None, "gy"),
        P("gx", None, "gy", None),
        P("gx", None, "gy", None, None),
    )
    return jax.shard_map(
        body,
        mesh=mesh,
        in_specs=placed,
        out_specs=(P(None, "gx", "gy"), P("gx", None, "gy", None, None)),
        check_vma=False,
    )
```
